32 devices in a mesh: row: 4 (over z), col: 8 (over y, x, core).
Axes of the slice: x: 2, y: 2, z: 4, core: 2. Of those that a mesh axis runs over, the one named last changes fastest.
Arguments:
- tokens: bfloat16 [8192, 2048], P('row', 'col'), may hold values from -6 to 6
- cotangent: bfloat16 [8192, 2048], P('row', 'col'), may hold values from -6 to 6
- dealing: int32 [8192], replicated, may hold values from 0 to 8191, each once
- doc_lengths: int32 [4, 4], P('row'), may hold values from 1 to 1024, 2048 in all within a row
- routes: int32 [8192, 6], P('row'), may hold values from 0 to 15, all different within a row; in each aligned block of 2048 rows (0 to 2047, 2048 to 4095, ...) at most 1024 rows name the same one
- gate_weights: float32 [8192, 6], P('row'), may hold values from 0.3 to 1
- attn_gain: bfloat16 [2048], P('row'), may hold values from 0.5 to 1.5
- w_query: bfloat16 [2048, 3072], P('row', 'col'), may hold values from -0.1875 to 0.1875
- w_latent: bfloat16 [2048, 576], P('row'), may hold values from -0.125 to 0.125
- latent_gain: bfloat16 [512], P('row'), may hold values from 0.5 to 1.5
- w_expand: bfloat16 [512, 4096], P('row', 'col'), may hold values from -0.25 to 0.25
- w_output: bfloat16 [2048, 2048], P('col', 'row'), may hold values from -1 to 1
- ffn_gain: bfloat16 [2048], P('row'), may hold values from 0.5 to 1.5
- shared_gate: bfloat16 [2048, 2816], P('row', 'col'), may hold values from -0.125 to 0.125
- shared_up: bfloat16 [2048, 2816], P('row', 'col'), may hold values from -0.125 to 0.125
- shared_down: bfloat16 [2816, 2048], P('col', 'row'), may hold values from -0.109375 to 0.109375
- expert_gate: bfloat16 [16, 2048, 1408], P('col', 'row'), may hold values from -0.125 to 0.125
- expert_up: bfloat16 [16, 2048, 1408], P('col', 'row'), may hold values from -0.125 to 0.125
- expert_down: bfloat16 [16, 1408, 2048], P('col', None, 'row'), may hold values from -0.15625 to 0.15625
Outputs:
- result: bfloat16 [8192, 2048], P('row', 'col')
- tokens_grad: bfloat16 [8192, 2048], P('row', 'col')
- attn_gain_grad: float32 [2048], P('row')
- w_query_grad: float32 [2048, 3072], P('row', 'col')
- w_latent_grad: float32 [2048, 576], P('row')
- latent_gain_grad: float32 [512], P('row')
- w_expand_grad: float32 [512, 4096], P('row', 'col')
- w_output_grad: float32 [2048, 2048], P('col', 'row')
- ffn_gain_grad: float32 [2048], P('row')
- shared_gate_grad: float32 [2048, 2816], P('row', 'col')
- shared_up_grad: float32 [2048, 2816], P('row', 'col')
- shared_down_grad: float32 [2816, 2048], P('col', 'row')
- expert_gate_grad: float32 [16, 2048, 1408], P('col', 'row')
- expert_up_grad: float32 [16, 2048, 1408], P('col', 'row')
- expert_down_grad: float32 [16, 1408, 2048], P('col', None, 'row')
The draws below stay inside these ranges and needn't reach their ends.
Inputs may be any that keep to these rules, and one draw needn't show every extreme that they name: `dealing`: each number appears once. `doc_lengths`: each row holds 4 lengths that sum to 2048; its largest is exactly 1024. `routes`: a token's 6 experts differ; within the 2048 rows of one group no expert is named by more than 1024 rows, and some expert reaches 1024 in some groups.
All inputs are finite; a program needn't handle non-finite values.
Results may differ from the reference program's by a relative error of at most 0.023.
Values may be sent and summed in bfloat16 or wider, within the bound.
No kernel may reach another device: no remote copies, remote signals or barrier semaphores. Data moves between devices by JAX's collectives and lax.ppermute only.
A program may use at most 448 MiB of HBM per device.

```python
import math
import jax
import jax.numpy as jnp
import numpy as np
from jax import lax

D = 2048
HEADS = 16
NOPE = 128
ROPE = 64
VDIM = 128
LAT = 512
MOE_FF = 1408
SH_FF = 2816
TOPK = 6
TOK_GRP = 2048
MAXLEN = 1024
DOCS = 4
EXPERTS = 16
CAP = 1024
GROUPS = 4
TOKENS = 8192


def levels(rng, shape, cuts, low, largest):
    gain, own = 1.0, jax.random.fold_in(rng, 6)
    for axis_at, blocks in cuts:
        heights = jnp.exp(jax.random.uniform(jax.random.fold_in(own, axis_at), (blocks,), jnp.float32, low / len(cuts), largest / len(cuts)))
        gain = gain * jnp.repeat(heights, shape[axis_at] // blocks).reshape([-1 if axis == axis_at else 1 for axis in range(len(shape))])
    return gain


def profile(number_of, total, limit, lean):
    portions = [(1 << 20) // math.isqrt(grade ** lean) + 1 for grade in range(2, number_of + 1)]
    rest, holding = total - limit - (number_of - 1), [1] * (number_of - 1)
    while rest > 0:
        candidates = [i for i in range(number_of - 1) if holding[i] < limit]
        whole, remaining = sum([portions[i] for i in candidates]), rest
        for i in candidates:
            more = min(limit - holding[i], max(1, remaining * portions[i] // whole), rest)
            holding[i] = holding[i] + more
            rest = rest - more
    return np.array([limit] + holding)


def uneven(key, count, total, most, slope):
    if count == 2:
        one = jax.random.randint(key, (), max(1, total - most), min(most, total - 1) + 1)
        return jnp.stack([one, total - one])
    lengths = jnp.asarray(profile(count, total, most, slope), jnp.int32)
    couples = (count - 1) // 2
    donor, receiver = lengths[1:1 + 2 * couples:2], lengths[2:2 + 2 * couples:2]
    room = jnp.minimum(donor - 1, most - receiver)
    shifted = jax.random.randint(jax.random.fold_in(key, 1), (couples,), 0, 1 << 20) % (room + 1)
    lengths = lengths.at[1:1 + 2 * couples:2].set(donor - shifted).at[2:2 + 2 * couples:2].set(receiver + shifted)
    return lengths[jax.random.permutation(jax.random.fold_in(key, 2), count)]


def assign_block(rng, own, number, rows, amount, top, limit, skew):
    sequence = jax.random.permutation(rng, amount)
    crowded, usual = portions_of(amount, rows * top, limit, skew, True), portions_of(amount, rows * top, limit, skew, False)
    places = jnp.arange(amount)

    def named(sizes, offset_by):
        used = int((sizes > 0).sum())
        fixed = max(1, used // 4)
        shifted = fixed + (places - fixed + offset_by * (used - fixed)) % max(1, amount - fixed)
        return jnp.zeros((amount,), jnp.int32).at[sequence[jnp.where(places < fixed, places, shifted)]].set(jnp.asarray(sizes, jnp.int32))

    sizes = jnp.where(number % 4 == 0, named(crowded, number // 4), named(usual, number - number // 4 - 1))
    mixed = jax.random.permutation(jax.random.fold_in(own, 3), amount)
    source_of, taker = mixed[0:amount // 2 * 2:2], mixed[1:amount // 2 * 2:2]
    slack = jnp.minimum(sizes[source_of] - 1, limit - sizes[taker]) // 2
    slack = jnp.where((source_of == sequence[0]) | (taker == sequence[0]) | (sizes[taker] == 0), 0, jnp.maximum(slack, 0))
    shifted = jax.random.randint(jax.random.fold_in(own, 4), (amount // 2,), 0, 1 << 20) % (slack + 1)
    sizes = sizes.at[source_of].add(-shifted).at[taker].add(shifted)
    items = jnp.searchsorted(jnp.cumsum(sizes), jnp.arange(rows * top), side="right").astype(jnp.int32)
    listing = items.reshape(top, rows).T
    listing = listing[jax.random.permutation(jax.random.fold_in(own, 1), rows)]
    offset_by = jax.random.randint(jax.random.fold_in(own, 2), (rows, 1), 0, top)
    return jnp.take_along_axis(listing, (jnp.arange(top)[None, :] + offset_by) % top, axis=1)


def portions_of(amount, total, reach, lean, full):
    loads = [(1 << 20) // math.isqrt(rank ** lean) + 1 for rank in range(1, amount + 1)]
    largest = reach if full else min(reach, max(-(-total // amount), total * loads[0] // sum(loads)))
    least = 1 if total - largest >= amount - 1 else 0
    given, surplus = [largest] + [least] * (amount - 1), total - largest - least * (amount - 1)
    while surplus > 0:
        movable = [i for i in range(1, amount) if given[i] < largest] or [i for i in range(1, amount) if given[i] < reach]
        pool, left = sum([loads[i] for i in movable]), surplus
        for i in movable:
            extra = min(reach - given[i], max(1, left * loads[i] // pool), surplus)
            given[i] = given[i] + extra
            surplus = surplus - extra
    return np.array(given)


def normal_values(stream_key, shape, deviation, bound, cuts=(), held_as=jnp.bfloat16):
    entries = jax.random.normal(stream_key, shape, jnp.float32) * deviation
    if len(cuts) > 0:
        entries = levels(stream_key, shape, cuts, -0.22, 0.18) * entries
    return jnp.clip(entries, min=-bound, max=bound).astype(held_as)


def setup_inputs(seed: int = 0) -> dict:
    key_list = jax.random.split(jax.random.key(seed), 20)
    tokens = normal_values(key_list[0], (TOKENS, D), 1.0, 6.0, ((0, 4), (1, 8)))
    cotangent = normal_values(key_list[1], (TOKENS, D), 1.0, 6.0, ((0, 4), (1, 8)))
    dealing = jax.random.permutation(key_list[2], TOKENS).astype(jnp.int32)
    doc_lengths = jax.vmap(lambda own: uneven(own, DOCS, TOK_GRP, MAXLEN, 2))(jax.random.split(key_list[3], GROUPS)).reshape((GROUPS, DOCS)).astype(jnp.int32)
    routes_keys = jax.random.split(jax.random.fold_in(key_list[4], 1), TOKENS // TOK_GRP)
    routes_turns = jax.random.permutation(jax.random.fold_in(key_list[4], 3), TOKENS // TOK_GRP)
    routes = jax.vmap(lambda own, number: assign_block(jax.random.fold_in(key_list[4], 2), own, number, TOK_GRP, EXPERTS, TOPK, CAP, 1))(routes_keys, routes_turns).reshape((TOKENS, TOPK))
    gate_weights = jnp.clip(jnp.exp(math.log(1.0) - 1.2039728 * jax.random.uniform(key_list[5], (TOKENS, TOPK), jnp.float32) ** levels(key_list[5], (TOKENS, TOPK), ((0, 4),), -0.2, 0.2)), 0.3, 1.0)
    attn_gain = jnp.clip(1.0 + 0.1 * jax.random.normal(key_list[6], (D,), jnp.float32), 0.5, 1.5).astype(jnp.bfloat16)
    w_query = normal_values(key_list[7], (D, HEADS * (NOPE + ROPE)), (D // 2) ** -0.5, 0.1875, ((0, 4), (1, 8)))
    w_latent = normal_values(key_list[8], (D, LAT + ROPE), D ** -0.5, 0.125, ((0, 4),))
    latent_gain = jnp.clip(1.0 + 0.1 * jax.random.normal(key_list[9], (LAT,), jnp.float32), 0.5, 1.5).astype(jnp.bfloat16)
    w_expand = normal_values(key_list[10], (LAT, HEADS * (NOPE + VDIM)), LAT ** -0.5, 0.25, ((0, 4), (1, 8)))
    w_output = normal_values(key_list[11], (HEADS * VDIM, D), (HEADS * VDIM // 64) ** -0.5, 1.0, ((0, 8), (1, 4)))
    ffn_gain = jnp.clip(1.0 + 0.1 * jax.random.normal(key_list[12], (D,), jnp.float32), 0.5, 1.5).astype(jnp.bfloat16)
    shared_gate = normal_values(key_list[13], (D, SH_FF), D ** -0.5, 0.125, ((0, 4), (1, 8)))
    shared_up = normal_values(key_list[14], (D, SH_FF), D ** -0.5, 0.125, ((0, 4), (1, 8)))
    shared_down = normal_values(key_list[15], (SH_FF, D), SH_FF ** -0.5, 0.109375, ((0, 8), (1, 4)))
    expert_gate = normal_values(key_list[16], (EXPERTS, D, MOE_FF), D ** -0.5, 0.125, ((0, 8), (1, 4)))
    expert_up = normal_values(key_list[17], (EXPERTS, D, MOE_FF), D ** -0.5, 0.125, ((0, 8), (1, 4)))
    expert_down = normal_values(key_list[18], (EXPERTS, MOE_FF, D), MOE_FF ** -0.5, 0.15625, ((0, 8), (2, 4)))
    return dict(tokens=tokens, cotangent=cotangent, dealing=dealing, doc_lengths=doc_lengths, routes=routes, gate_weights=gate_weights, attn_gain=attn_gain, w_query=w_query, w_latent=w_latent, latent_gain=latent_gain, w_expand=w_expand, w_output=w_output, ffn_gain=ffn_gain, shared_gate=shared_gate, shared_up=shared_up, shared_down=shared_down, expert_gate=expert_gate, expert_up=expert_up, expert_down=expert_down)


EPSILON = 1e-06
HIGHEST = lax.Precision.HIGHEST

@jax.custom_vjp
def low(v):
    return lax.optimization_barrier(v.astype(jnp.bfloat16)).astype(jnp.float32)

@jax.custom_vjp
def low_back(v):
    return v

def low_keep(v):
    return (low(v), None)

def low_pass(kept, grad):
    return (grad,)

def back_keep(v):
    return (v, None)

def back_low(kept, grad):
    return (low(grad),)
low.defvjp(low_keep, low_pass)
low_back.defvjp(back_keep, back_low)

def rotate(value, position, orient):
    half_width = value.shape[-1] // 2
    frequency = 10000.0 ** (-jnp.arange(half_width, dtype=jnp.float32) / half_width)
    angles = position.astype(jnp.float32)[:, None] * frequency[None, :]
    shape_out = (value.shape[0],) + (1,) * (value.ndim - 2) + (half_width,)
    cosine = jnp.cos(angles).reshape(shape_out)
    sine_part = jnp.sin(angles).reshape(shape_out)
    first_half = value[..., :half_width]
    second = value[..., half_width:]
    return jnp.concatenate([first_half * cosine - orient * second * sine_part, second * cosine + orient * first_half * sine_part], axis=-1)

def normalize(value, gain_vector):
    return value * lax.rsqrt(lax.optimization_barrier(jnp.mean(value * value, axis=-1, keepdims=True)) + EPSILON) * gain_vector

def silu(value):
    return value * jax.nn.sigmoid(value)

def documents(lengths_row, row_count):
    doc_ends = jnp.cumsum(lengths_row).astype(jnp.int32)
    starts = (doc_ends - lengths_row).astype(jnp.int32)
    row_number = jnp.arange(row_count, dtype=jnp.int32)
    document = lax.optimization_barrier(jnp.sum((row_number[:, None] >= doc_ends[None, :]).astype(jnp.int32), axis=1)).astype(jnp.int32)
    onehot = document[:, None] == jnp.arange(lengths_row.shape[0], dtype=jnp.int32)[None, :]
    position = (row_number - lax.optimization_barrier(jnp.sum(jnp.where(onehot, starts[None, :], 0), axis=1))).astype(jnp.int32)
    return (document, position)

def expert_slots(flat_routes, expert, capacity):
    sentinel = flat_routes.shape[0]
    return jnp.nonzero(flat_routes == expert, size=capacity, fill_value=sentinel)[0].astype(jnp.int32)

def one_layer(group_x, lengths_row, group_routes, group_gates, params):
    gain_one, query_w, latent_w, latent_g, expand_w, output_w, gain_two, shared_g_w, shared_u_w, shared_d_w, expert_g_w, expert_u_w, expert_d_w = params
    group_rows = group_x.shape[0]
    document, position = documents(lengths_row, group_rows)
    normed_one = low(normalize(group_x, gain_one))
    query_raw = low_back(jnp.dot(normed_one, query_w, precision=HIGHEST)).reshape(group_rows, HEADS, NOPE + ROPE)
    query_heads = low(jnp.concatenate([query_raw[..., :NOPE], rotate(query_raw[..., NOPE:], position, 1.0)], axis=-1))
    latent = low_back(jnp.dot(normed_one, latent_w, precision=HIGHEST))
    compressed = low(normalize(latent[:, :LAT], latent_g))
    rope_key = low(rotate(latent[:, LAT:], position, 1.0))
    expanded = low(low_back(jnp.dot(compressed, expand_w, precision=HIGHEST))).reshape(group_rows, HEADS, NOPE + VDIM)
    key_heads = jnp.concatenate([expanded[..., :NOPE], jnp.broadcast_to(rope_key[:, None, :], (group_rows, HEADS, ROPE))], axis=-1)
    value_heads = expanded[..., NOPE:]
    row_number = jnp.arange(group_rows, dtype=jnp.int32)
    allowed = (document[:, None] == document[None, :]) & (row_number[:, None] >= row_number[None, :])
    softmax_scale = (NOPE + ROPE) ** (-0.5)
    scores = low_back(softmax_scale * jnp.einsum('qhd,khd->hqk', query_heads, key_heads, precision=HIGHEST))
    scores = jnp.where(allowed[None], scores, -1e+30)
    row_top = lax.optimization_barrier(jnp.max(scores, axis=-1, keepdims=True))
    exp_scores = jnp.exp(scores - row_top)
    probs = exp_scores / lax.optimization_barrier(jnp.sum(exp_scores, axis=-1, keepdims=True))
    mixed = low(low_back(jnp.einsum('hqk,khd->qhd', low(probs), value_heads, precision=HIGHEST)))
    mixed = mixed.reshape(group_rows, HEADS * VDIM)
    hidden_one = group_x + low_back(jnp.dot(mixed, output_w, precision=HIGHEST))
    normed_two = low(normalize(hidden_one, gain_two))
    shared_gate_out = low_back(jnp.dot(normed_two, shared_g_w, precision=HIGHEST))
    shared_up_out = low_back(jnp.dot(normed_two, shared_u_w, precision=HIGHEST))
    shared_out = jnp.dot(low(silu(shared_gate_out) * shared_up_out), shared_d_w, precision=HIGHEST)
    flat_routes = group_routes.reshape(-1)
    flat_gates = group_gates.reshape(-1)
    sentinel = flat_routes.shape[0]

    def expert_step(running, expert_item):
        number, gate_w, up_w, down_w = expert_item
        picked = expert_slots(flat_routes, number, CAP)
        is_used = picked < sentinel
        token_of = (picked // TOPK).astype(jnp.int32)
        weight = jnp.where(is_used, flat_gates[jnp.minimum(picked, sentinel - 1)], 0.0)
        expert_rows = normed_two[jnp.minimum(token_of, group_rows - 1)]
        gate_out = low_back(jnp.dot(expert_rows, gate_w, precision=HIGHEST))
        up_out = low_back(jnp.dot(expert_rows, up_w, precision=HIGHEST))
        expert_result = low_back(jnp.dot(low(silu(gate_out) * up_out), down_w, precision=HIGHEST))
        running = running.at[token_of].add(weight[:, None] * expert_result, mode='drop')
        return (running, None)
    routed, unused = lax.scan(expert_step, jnp.zeros((group_rows, D), jnp.float32), (jnp.arange(EXPERTS, dtype=jnp.int32), expert_g_w, expert_u_w, expert_d_w))
    return hidden_one + shared_out + routed

def forward(whole_x, params, dealing, doc_lengths, routes, gate_weights):
    dealt = whole_x[dealing].reshape(GROUPS, TOK_GRP, D)

    def group_step(carry_in, group_item):
        group_x, lengths_row, group_routes, group_gates = group_item
        return (carry_in, jax.checkpoint(one_layer)(group_x, lengths_row, group_routes, group_gates, params))
    unused, group_outs = lax.scan(group_step, jnp.zeros((), jnp.int32), (dealt, doc_lengths, routes.reshape(GROUPS, TOK_GRP, TOPK), gate_weights.reshape(GROUPS, TOK_GRP, TOPK)))
    return jnp.zeros_like(whole_x).at[dealing].set(group_outs.reshape(TOKENS, D))

def reference(tokens, cotangent, dealing, doc_lengths, routes, gate_weights, attn_gain, w_query, w_latent, latent_gain, w_expand, w_output, ffn_gain, shared_gate, shared_up, shared_down, expert_gate, expert_up, expert_down):
    weights = (attn_gain, w_query, w_latent, latent_gain, w_expand, w_output, ffn_gain, shared_gate, shared_up, shared_down, expert_gate, expert_up, expert_down)
    weights = tuple((item.astype(jnp.float32) for item in weights))

    def apply_layer(whole_x, *params):
        return forward(whole_x, params, dealing, doc_lengths, routes, gate_weights)
    layer_out, pullback = jax.vjp(apply_layer, tokens.astype(jnp.float32), *weights)
    gradients = pullback(cotangent.astype(jnp.float32))
    return (layer_out.astype(jnp.bfloat16), gradients[0].astype(jnp.bfloat16), gradients[1], gradients[2], gradients[3], gradients[4], gradients[5], gradients[6], gradients[7], gradients[8], gradients[9], gradients[10], gradients[11], gradients[12], gradients[13])
```

```python
import jax
import jax.numpy as jnp
from jax import lax
from jax.sharding import PartitionSpec as P

NOPE = 128
ROPE = 64
VDIM = 128
LAT = 512
TOPK = 6

EPSILON = 1e-06
F32 = jnp.float32
BF16 = jnp.bfloat16


def rotate(value, position, orient):
    half_width = value.shape[-1] // 2
    frequency = 10000.0 ** (-jnp.arange(half_width, dtype=F32) / half_width)
    angles = position.astype(F32)[:, None] * frequency[None, :]
    shape_out = (value.shape[0],) + (1,) * (value.ndim - 2) + (half_width,)
    cosine = jnp.cos(angles).reshape(shape_out)
    sine_part = jnp.sin(angles).reshape(shape_out)
    first_half = value[..., :half_width]
    second = value[..., half_width:]
    return jnp.concatenate(
        [
            first_half * cosine - orient * second * sine_part,
            second * cosine + orient * first_half * sine_part,
        ],
        axis=-1,
    )


def documents(lengths_row, row_count):
    doc_ends = jnp.cumsum(lengths_row)
    starts = doc_ends - lengths_row
    row_number = jnp.arange(row_count, dtype=jnp.int32)
    document = jnp.sum((row_number[:, None] >= doc_ends[None, :]).astype(jnp.int32), axis=1)
    onehot = document[:, None] == jnp.arange(lengths_row.shape[0], dtype=jnp.int32)[None, :]
    position = row_number - jnp.sum(jnp.where(onehot, starts[None, :], 0), axis=1)
    return (document, position)


def silu_parts(value):
    sigmoid_value = jax.nn.sigmoid(value)
    activation = value * sigmoid_value
    activ_slope = sigmoid_value * (1.0 + value * (1.0 - sigmoid_value))
    return (activation, activ_slope)


def norm_back(grad_normed, unit_rows, row_scale, gain_vector):
    scaled = grad_normed * gain_vector
    row_inner = jnp.mean(scaled * unit_rows, axis=-1, keepdims=True)
    return (row_scale * (scaled - unit_rows * row_inner), jnp.sum(grad_normed * unit_rows, axis=0))


def dot(left, right):
    return jnp.dot(left, right, preferred_element_type=F32)


def dot_nt(left, right):
    return lax.dot_general(left, right, (((1,), (1,)), ((), ())), preferred_element_type=F32)


def dot_tn(left, right):
    return lax.dot_general(left, right, (((0,), (0,)), ((), ())), preferred_element_type=F32)


def line_scatter(value, axis):
    count = lax.axis_size("row")
    index = lax.axis_index("row")
    width = value.shape[axis] // count

    def block(j):
        return lax.dynamic_slice_in_dim(value, jnp.clip(j, 0, count - 1) * width, width, axis)

    right, left = None, None
    for step in range(1, count):
        right_out, left_out = block(index + count - step), block(index - count + step)
        if right is not None:
            right_out = (right_out.astype(F32) + right.astype(F32)).astype(BF16)
            left_out = (left_out.astype(F32) + left.astype(F32)).astype(BF16)
        right = lax.ppermute(right_out, "row", [(j, j + 1) for j in range(0, step)])
        left = lax.ppermute(left_out, "row", [(j, j - 1) for j in range(count - step, count)])
    return block(index).astype(F32) + right.astype(F32) + left.astype(F32)


def swap(value, bit):
    return lax.ppermute(value, "col", [(j, j ^ bit) for j in range(lax.axis_size("col"))])


def chip_bits():
    return [1 << b for b in range(1, (lax.axis_size("col") - 1).bit_length())]


def cube_gather(block, axis):
    count = lax.axis_size("col")
    index = lax.axis_index("col")
    bits = chip_bits()
    half = block.shape[0] // 2
    kept, swapped = [], []
    for part, order in ((block[:half], bits), (block[half:], bits[::-1])):
        held, keys = part[None], [0]
        for bit in order:
            held = jnp.concatenate([held, swap(held, bit)], axis=0)
            keys = keys + [key ^ bit for key in keys]
        order_of = [keys.index(key) for key in range(0, count, 2)]
        kept.append((held, order_of))
    swapped = [swap(held, 1) for held, order_of in kept]
    out = []
    for j in range(count):
        rel = jnp.bitwise_xor(index, j)
        halves = []
        for (held, order_of), other in zip(kept, swapped):
            place = jnp.array(order_of, jnp.int32)[rel // 2]
            mine = lax.dynamic_index_in_dim(held, place, 0, False)
            theirs = lax.dynamic_index_in_dim(other, place, 0, False)
            halves.append(jnp.where(rel % 2 == 0, mine, theirs))
        out.append(jnp.concatenate(halves, axis=0))
    return jnp.concatenate(out, axis=axis)


def cube_scatter(value):
    count = lax.axis_size("col")
    index = lax.axis_index("col")
    bits = chip_bits()
    rows = value.shape[0] // count
    half = rows // 2
    evens = list(range(0, count, 2))

    def blocks(me):
        return jnp.stack(
            [
                lax.dynamic_slice_in_dim(value, jnp.bitwise_xor(me, key) * rows, rows, 0)
                for key in evens
            ]
        )

    got = swap(blocks(jnp.bitwise_xor(index, 1)), 1)
    total = (blocks(index).astype(F32) + got.astype(F32)).astype(BF16)
    parts = []
    for part, order in ((total[:, :half], bits), (total[:, half:], bits[::-1])):
        held = {key: part[n] for n, key in enumerate(evens)}
        for bit in order:
            leaving = [key for key in held if key & bit]
            arrived = swap(jnp.stack([held[key] for key in leaving]), bit)
            held = {
                key: (held[key].astype(F32) + arrived[leaving.index(key ^ bit)].astype(F32))
                for key in held
                if not key & bit
            }
            if len(held) > 1:
                held = {key: item.astype(BF16) for key, item in held.items()}
        parts.append(held[0])
    return jnp.concatenate(parts, axis=0)


def row_gather(shard, axis):
    return lax.all_gather(shard, "row", axis=axis, tiled=True)


def after(values, earlier):
    out = lax.optimization_barrier(tuple(values) + tuple(earlier))
    return out[: len(values)]


def col_gather(value, axis=0):
    return lax.all_gather(value, "col", axis=axis, tiled=True)


def col_scatter(value):
    return lax.psum_scatter(value, "col", scatter_dimension=0, tiled=True).astype(F32)


def body(
    tokens,
    cotangent,
    dealing,
    doc_lengths,
    routes,
    gate_weights,
    attn_gain,
    w_query,
    w_latent,
    latent_gain,
    w_expand,
    w_output,
    ffn_gain,
    shared_gate,
    shared_up,
    shared_down,
    expert_gate,
    expert_up,
    expert_down,
):
    group_rows = routes.shape[0]
    row_count = lax.axis_size("row")
    col_count = lax.axis_size("col")
    row_index = lax.axis_index("row")
    col_index = lax.axis_index("col")
    part_rows = group_rows // col_count
    local_count = expert_gate.shape[0]
    capacity = 4 * group_rows * TOPK // (3 * local_count * col_count)

    def my_part(value):
        return lax.dynamic_slice_in_dim(value, col_index * part_rows, part_rows, 0)

    my_order = lax.dynamic_slice_in_dim(dealing, row_index * group_rows, group_rows)
    token_ids = jnp.arange(group_rows, dtype=jnp.int32)
    given_ids = row_index * group_rows + token_ids
    my_inverse = jnp.sum(
        jnp.where(
            dealing[None, :] == given_ids[:, None],
            jnp.arange(dealing.shape[0], dtype=jnp.int32)[None, :],
            0,
        ),
        axis=1,
    )
    picks, weights = [], []
    slot_ids = jnp.arange(capacity, dtype=jnp.int32)
    for number in range(local_count):
        named = routes == (col_index * local_count + number)
        named_any = jnp.any(named, axis=1)
        running = jnp.cumsum(named_any.astype(jnp.int32))
        place = jnp.where(named_any, running - 1, -1)
        pick = place[None, :] == slot_ids[:, None]
        token_weight = jnp.sum(jnp.where(named, gate_weights, 0.0), axis=1)
        picks.append(pick.astype(BF16))
        weights.append(jnp.sum(jnp.where(pick, token_weight[None, :], 0.0), axis=1))
    document, position = documents(doc_lengths[0], group_rows)

    rows_in, dim = w_query.shape[0], w_query.shape[0] * row_count
    wide = attn_gain.shape[0]
    lat_width = latent_gain.shape[0]
    given_x = row_gather(tokens, 0)
    dealt_x = jnp.take(given_x, my_order, axis=0)
    gains = row_gather(jnp.concatenate([attn_gain, ffn_gain, latent_gain])[None], 0)
    gain_one = gains[:, :wide].reshape(-1).astype(F32)
    gain_two = gains[:, wide : 2 * wide].reshape(-1).astype(F32)
    latent_g = gains[:, 2 * wide :].reshape(-1).astype(F32)
    lat_rows = rows_in // col_count
    w_latent_s = lax.dynamic_slice_in_dim(w_latent, col_index * lat_rows, lat_rows, 0)
    latent_w = cube_gather(row_gather(w_latent_s, 0), 0)
    latent_w = latent_w.reshape(col_count, row_count, lat_rows, -1).transpose(1, 0, 2, 3)
    latent_w = latent_w.reshape(dim, -1)
    full_x = cube_gather(dealt_x, 1)

    (w_query_s, w_output_s, w_expand_s) = after((w_query, w_output, w_expand), (given_x,))
    query_w = row_gather(w_query_s, 0)
    expand_w = row_gather(w_expand_s, 0)
    output_w = row_gather(w_output_s, 1)
    (cotangent_s,) = after((cotangent,), (given_x,))
    given_dy = row_gather(cotangent_s, 0)
    dealt_dy = jnp.take(given_dy, my_order, axis=0)
    full_dy = cube_gather(dealt_dy, 1)

    expert_w = []
    earlier = [output_w, given_dy]
    for number in range(local_count):
        gu_s = jnp.concatenate([expert_gate[number], expert_up[number]], axis=1)
        (gu_s,) = after((gu_s,), (earlier[-2],))
        gate_up_w = row_gather(gu_s, 0)
        earlier.append(gate_up_w)
        (d_s,) = after((expert_down[number],), (earlier[-2],))
        down_w = row_gather(d_s, 1)
        earlier.append(down_w)
        expert_w.append((gate_up_w, down_w))
        if number == 0:
            sgu_s = jnp.concatenate([shared_gate, shared_up], axis=1)
            (sgu_s,) = after((sgu_s,), (earlier[-2],))
            shared_gu_w = row_gather(sgu_s, 0)
            earlier.append(shared_gu_w)
            (sd_s,) = after((shared_down,), (earlier[-2],))
            shared_d_w = row_gather(sd_s, 1)
            earlier.append(shared_d_w)

    head_count = query_w.shape[1] // (NOPE + ROPE)
    softmax_scale = (NOPE + ROPE) ** (-0.5)
    block_rows = min(512, group_rows)
    row_number = token_ids
    residual = full_x.astype(F32)
    scale_one = lax.rsqrt(jnp.mean(residual * residual, axis=-1, keepdims=True) + EPSILON)
    normed_one = (residual * scale_one * gain_one).astype(BF16)
    query_raw = dot(normed_one, query_w)
    query_raw = query_raw.reshape(group_rows, head_count, NOPE + ROPE)
    query_heads = jnp.concatenate(
        [query_raw[..., :NOPE], rotate(query_raw[..., NOPE:], position, 1.0)], axis=-1
    ).astype(BF16)
    latent = dot(normed_one, latent_w)
    latent_front = latent[:, :LAT]
    scale_lat = lax.rsqrt(jnp.mean(latent_front * latent_front, axis=-1, keepdims=True) + EPSILON)
    unit_lat = latent_front * scale_lat
    compressed = (unit_lat * latent_g).astype(BF16)
    rope_key = rotate(latent[:, LAT:], position, 1.0).astype(BF16)
    expanded = dot(compressed, expand_w).astype(BF16)
    expanded = expanded.reshape(group_rows, head_count, NOPE + VDIM)
    key_heads = jnp.concatenate(
        [
            expanded[..., :NOPE],
            jnp.broadcast_to(rope_key[:, None, :], (group_rows, head_count, ROPE)),
        ],
        axis=-1,
    )
    value_heads = expanded[..., NOPE:]

    def block_scores(first_row, last_row):
        raw_scores = (
            jnp.einsum(
                "qhd,khd->hqk",
                query_heads[first_row:last_row],
                key_heads[:last_row],
                preferred_element_type=F32,
            )
            * softmax_scale
        )
        allowed = (document[first_row:last_row, None] == document[None, :last_row]) & (
            row_number[first_row:last_row, None] >= row_number[None, :last_row]
        )
        return jnp.where(allowed[None], raw_scores, -1e30)

    mixed_blocks = []
    lse_blocks = []
    for first_row in range(0, group_rows, block_rows):
        last_row = first_row + block_rows
        scores = block_scores(first_row, last_row)
        row_top = jnp.max(scores, axis=-1, keepdims=True)
        exp_scores = jnp.exp(scores - row_top)
        row_total = jnp.sum(exp_scores, axis=-1, keepdims=True)
        probs_low = (exp_scores / row_total).astype(BF16)
        lse_blocks.append(row_top[..., 0] + jnp.log(row_total[..., 0]))
        mixed_blocks.append(
            jnp.einsum(
                "hqk,khd->qhd",
                probs_low,
                value_heads[:last_row],
                preferred_element_type=F32,
            )
        )
    mixed = (
        jnp.concatenate(mixed_blocks, axis=0).reshape(group_rows, head_count * VDIM).astype(BF16)
    )
    attn_part = cube_scatter(dot(mixed, output_w).astype(BF16))
    x_part = my_part(full_x).astype(F32)
    hidden_part = x_part + attn_part
    scale_two = lax.rsqrt(jnp.mean(hidden_part * hidden_part, axis=-1, keepdims=True) + EPSILON)
    unit_two = hidden_part * scale_two
    normed_two = cube_gather((unit_two * gain_two).astype(BF16), 0)

    def branch(rows, grad_result, gate_up_w, down_w):
        width = gate_up_w.shape[1] // 2
        gate_up = dot(rows, gate_up_w)
        gate_out, up_out = gate_up[:, :width], gate_up[:, width:]
        act, slope = silu_parts(gate_out)
        hidden = (act * up_out).astype(BF16)
        grad_hidden = dot_nt(grad_result, down_w)
        grad_gate_up = jnp.concatenate(
            [(grad_hidden * up_out * slope).astype(BF16), (grad_hidden * act).astype(BF16)], axis=1
        )
        result_rows = dot(hidden, down_w)
        grad_rows = dot_nt(grad_gate_up, gate_up_w)
        grad_down = line_scatter(dot_tn(hidden, grad_result).astype(BF16), 1)
        grad_gu = line_scatter(dot_tn(rows, grad_gate_up).astype(BF16), 0)
        return result_rows, grad_rows, grad_gu[:, :width], grad_gu[:, width:], grad_down

    moe_terms, grad_two, grad_shared_gate, grad_shared_up, grad_shared_down = branch(
        normed_two, full_dy, shared_gu_w, shared_d_w
    )
    grad_gates, grad_ups, grad_downs = [], [], []
    for number in range(local_count):
        gate_up_w, down_w = expert_w[number]
        pick, weight = picks[number], weights[number]
        rows = dot(pick, normed_two).astype(BF16)
        grad_result = (weight[:, None] * dot(pick, full_dy)).astype(BF16)
        result_rows, grad_rows, grad_gate, grad_up, grad_down = branch(
            rows, grad_result, gate_up_w, down_w
        )
        grad_gates.append(grad_gate)
        grad_ups.append(grad_up)
        grad_downs.append(grad_down)
        moe_terms = moe_terms + dot_tn(pick, (weight[:, None] * result_rows).astype(BF16))
        grad_two = grad_two + dot_tn(pick, grad_rows.astype(BF16))

    grad_two_part = col_scatter(grad_two.astype(BF16))
    dy_part = my_part(full_dy).astype(F32)
    hidden_back, gain_two_grad = norm_back(grad_two_part, unit_two, scale_two, gain_two)
    grad_hidden_part = dy_part + hidden_back
    grad_attn = col_gather(grad_hidden_part.astype(BF16))

    moe_part = col_scatter(moe_terms.astype(BF16))
    result_part = (hidden_part + moe_part).astype(BF16)
    result_slice = lax.all_to_all(result_part, "col", split_axis=1, concat_axis=0, tiled=True)
    back_result = lax.all_gather(result_slice, "row", axis=0, tiled=True)
    result = jnp.take(back_result, my_inverse, axis=0)

    grad_output_w = line_scatter(dot_tn(mixed, grad_attn).astype(BF16), 1)
    grad_mixed = dot_nt(grad_attn, output_w).astype(BF16)
    grad_mixed = grad_mixed.reshape(group_rows, head_count, VDIM)
    grad_query_blocks = []
    grad_keys = jnp.zeros((group_rows, head_count, NOPE + ROPE), F32)
    grad_values = jnp.zeros((group_rows, head_count, VDIM), F32)
    for block_number, first_row in enumerate(range(0, group_rows, block_rows)):
        last_row = first_row + block_rows
        scores = block_scores(first_row, last_row)
        probs_f = jnp.exp(scores - lse_blocks[block_number][..., None])
        probs_low = probs_f.astype(BF16)
        grad_block = grad_mixed[first_row:last_row]
        grad_probs = jnp.einsum(
            "qhd,khd->hqk", grad_block, value_heads[:last_row], preferred_element_type=F32
        )
        row_inner = jnp.sum(probs_f * grad_probs, axis=-1, keepdims=True)
        grad_scores = (probs_f * (grad_probs - row_inner)).astype(BF16)
        grad_values = grad_values.at[:last_row].add(
            jnp.einsum("hqk,qhd->khd", probs_low, grad_block, preferred_element_type=F32)
        )
        grad_query_blocks.append(
            softmax_scale
            * jnp.einsum(
                "hqk,khd->qhd", grad_scores, key_heads[:last_row], preferred_element_type=F32
            )
        )
        grad_keys = grad_keys.at[:last_row].add(
            softmax_scale
            * jnp.einsum(
                "hqk,qhd->khd",
                grad_scores,
                query_heads[first_row:last_row],
                preferred_element_type=F32,
            )
        )
    grad_query = jnp.concatenate(grad_query_blocks, axis=0)
    grad_query_raw = (
        jnp.concatenate(
            [grad_query[..., :NOPE], rotate(grad_query[..., NOPE:], position, -1.0)], axis=-1
        )
        .astype(BF16)
        .reshape(group_rows, head_count * (NOPE + ROPE))
    )
    grad_one = col_scatter(dot_nt(grad_query_raw, query_w).astype(BF16))
    grad_expanded = jnp.concatenate([grad_keys[..., :NOPE], grad_values], axis=-1).astype(BF16)
    grad_expanded = grad_expanded.reshape(group_rows, head_count * (NOPE + VDIM))
    grad_compressed = dot_nt(grad_expanded, expand_w)
    grad_rope_key = rotate(jnp.sum(grad_keys[..., NOPE:], axis=1), position, -1.0)
    grad_latent_part = col_scatter(
        jnp.concatenate([grad_compressed, grad_rope_key], axis=1).astype(BF16)
    )
    grad_front, latent_gain_grad = norm_back(
        grad_latent_part[:, :LAT], my_part(unit_lat), my_part(scale_lat), latent_g
    )
    grad_latent_part = jnp.concatenate([grad_front, grad_latent_part[:, LAT:]], axis=1).astype(BF16)
    latent_term = dot_nt(grad_latent_part, latent_w)
    grad_one = grad_one + latent_term
    scale_one_part = my_part(scale_one)
    input_back, gain_one_grad = norm_back(
        grad_one, x_part * scale_one_part, scale_one_part, gain_one
    )
    grad_input = (grad_hidden_part + input_back).astype(BF16)
    grad_slice = lax.all_to_all(grad_input, "col", split_axis=1, concat_axis=0, tiled=True)
    back_grad = lax.all_gather(grad_slice, "row", axis=0, tiled=True)
    tokens_grad = jnp.take(back_grad, my_inverse, axis=0)

    grad_query_w = line_scatter(dot_tn(normed_one, grad_query_raw).astype(BF16), 0)
    grad_expand_w = line_scatter(dot_tn(compressed, grad_expanded).astype(BF16), 0)
    grad_latent = col_gather(grad_latent_part)
    my_columns = lax.dynamic_index_in_dim(
        normed_one.reshape(group_rows, row_count, col_count, lat_rows), col_index, 2, False
    ).reshape(group_rows, row_count * lat_rows)
    grad_latent_w = col_gather(line_scatter(dot_tn(my_columns, grad_latent).astype(BF16), 0))
    gain_grads = lax.psum(
        jnp.concatenate([gain_one_grad, gain_two_grad, latent_gain_grad]), ("row", "col")
    )
    width_two = gain_one_grad.shape[0]
    width_lat = latent_gain_grad.shape[0]

    def my_rows(value):
        width = value.shape[0] // row_count
        return lax.dynamic_slice_in_dim(value, row_index * width, width, 0)

    return (
        result,
        tokens_grad,
        my_rows(gain_grads[:width_two]),
        grad_query_w,
        grad_latent_w,
        my_rows(gain_grads[2 * width_two : 2 * width_two + width_lat]),
        grad_expand_w,
        grad_output_w,
        my_rows(gain_grads[width_two : 2 * width_two]),
        grad_shared_gate,
        grad_shared_up,
        grad_shared_down,
        jnp.stack(grad_gates),
        jnp.stack(grad_ups),
        jnp.stack(grad_downs),
    )


def solution(mesh):
    return jax.shard_map(
        body,
        mesh=mesh,
        in_specs=(
            P("row", "col"),
            P("row", "col"),
            P(),
            P("row", None),
            P("row", None),
            P("row", None),
            P("row"),
            P("row", "col"),
            P("row", None),
            P("row"),
            P("row", "col"),
            P("col", "row"),
            P("row"),
            P("row", "col"),
            P("row", "col"),
            P("col", "row"),
            P("col", "row", None),
            P("col", "row", None),
            P("col", None, "row"),
        ),
        out_specs=(
            P("row", "col"),
            P("row", "col"),
            P("row"),
            P("row", "col"),
            P("row", None),
            P("row"),
            P("row", "col"),
            P("col", "row"),
            P("row"),
            P("row", "col"),
            P("row", "col"),
            P("col", "row"),
            P("col", "row", None),
            P("col", "row", None),
            P("col", None, "row"),
        ),
        check_vma=False,
    )
```

```python
import jax
import jax.numpy as jnp
from jax import lax
from jax.sharding import PartitionSpec as P

NOPE = 128
ROPE = 64
VDIM = 128
LAT = 512
TOPK = 6

EPSILON = 1e-06
F32 = jnp.float32
BF16 = jnp.bfloat16


def rotate(value, position, orient):
    half_width = value.shape[-1] // 2
    frequency = 10000.0 ** (-jnp.arange(half_width, dtype=F32) / half_width)
    angles = position.astype(F32)[:, None] * frequency[None, :]
    shape_out = (value.shape[0],) + (1,) * (value.ndim - 2) + (half_width,)
    cosine = jnp.cos(angles).reshape(shape_out)
    sine_part = jnp.sin(angles).reshape(shape_out)
    first_half = value[..., :half_width]
    second = value[..., half_width:]
    return jnp.concatenate(
        [
            first_half * cosine - orient * second * sine_part,
            second * cosine + orient * first_half * sine_part,
        ],
        axis=-1,
    )


def documents(lengths_row, row_count):
    doc_ends = jnp.cumsum(lengths_row)
    starts = doc_ends - lengths_row
    row_number = jnp.arange(row_count, dtype=jnp.int32)
    document = jnp.sum((row_number[:, None] >= doc_ends[None, :]).astype(jnp.int32), axis=1)
    onehot = document[:, None] == jnp.arange(lengths_row.shape[0], dtype=jnp.int32)[None, :]
    position = row_number - jnp.sum(jnp.where(onehot, starts[None, :], 0), axis=1)
    return (document, position)


def silu_parts(value):
    sigmoid_value = jax.nn.sigmoid(value)
    activation = value * sigmoid_value
    activ_slope = sigmoid_value * (1.0 + value * (1.0 - sigmoid_value))
    return (activation, activ_slope)


def norm_back(grad_normed, unit_rows, row_scale, gain_vector):
    scaled = grad_normed * gain_vector
    row_inner = jnp.mean(scaled * unit_rows, axis=-1, keepdims=True)
    return (row_scale * (scaled - unit_rows * row_inner), jnp.sum(grad_normed * unit_rows, axis=0))


def dot(left, right):
    return jnp.dot(left, right, preferred_element_type=F32)


def dot_nt(left, right):
    return lax.dot_general(left, right, (((1,), (1,)), ((), ())), preferred_element_type=F32)


def dot_tn(left, right):
    return lax.dot_general(left, right, (((0,), (0,)), ((), ())), preferred_element_type=F32)


def line_gather(shard, axis):
    count = lax.axis_size("row")
    index = lax.axis_index("row")
    width = shard.shape[axis]
    right, left = shard, shard
    rights, lefts = [], []
    for step in range(1, count):
        right = lax.ppermute(right, "row", [(j, j + 1) for j in range(step - 1, count - 1)])
        left = lax.ppermute(left, "row", [(j, j - 1) for j in range(1, count - step + 1)])
        rights.append(right)
        lefts.append(left)
    shape = list(shard.shape)
    shape[axis] = width * count
    out = lax.dynamic_update_slice_in_dim(
        jnp.zeros(shape, shard.dtype), shard, index * width, axis
    )
    for k in range(1, count):
        piece = jnp.where(index >= k, rights[k - 1], lefts[count - k - 1])
        out = lax.dynamic_update_slice_in_dim(
            out, piece, lax.rem(index - k + count, count) * width, axis
        )
    return out


def swap(value, bit):
    return lax.ppermute(value, "col", [(j, j ^ bit) for j in range(lax.axis_size("col"))])


def chip_bits():
    return [1 << b for b in range(1, (lax.axis_size("col") - 1).bit_length())]


def cube_gather(block, axis):
    count = lax.axis_size("col")
    index = lax.axis_index("col")
    bits = chip_bits()
    half = block.shape[0] // 2
    kept, swapped = [], []
    for part, order in ((block[:half], bits), (block[half:], bits[::-1])):
        held, keys = part[None], [0]
        for bit in order:
            held = jnp.concatenate([held, swap(held, bit)], axis=0)
            keys = keys + [key ^ bit for key in keys]
        order_of = [keys.index(key) for key in range(0, count, 2)]
        kept.append((held, order_of))
    swapped = [swap(held, 1) for held, order_of in kept]
    out = []
    for j in range(count):
        rel = jnp.bitwise_xor(index, j)
        halves = []
        for (held, order_of), other in zip(kept, swapped):
            place = jnp.array(order_of, jnp.int32)[rel // 2]
            mine = lax.dynamic_index_in_dim(held, place, 0, False)
            theirs = lax.dynamic_index_in_dim(other, place, 0, False)
            halves.append(jnp.where(rel % 2 == 0, mine, theirs))
        out.append(jnp.concatenate(halves, axis=0))
    return jnp.concatenate(out, axis=axis)


def cube_scatter(value):
    count = lax.axis_size("col")
    index = lax.axis_index("col")
    bits = chip_bits()
    rows = value.shape[0] // count
    half = rows // 2
    evens = list(range(0, count, 2))

    def blocks(me):
        return jnp.stack(
            [
                lax.dynamic_slice_in_dim(value, jnp.bitwise_xor(me, key) * rows, rows, 0)
                for key in evens
            ]
        )

    got = swap(blocks(jnp.bitwise_xor(index, 1)), 1)
    total = (blocks(index).astype(F32) + got.astype(F32)).astype(BF16)
    parts = []
    for part, order in ((total[:, :half], bits), (total[:, half:], bits[::-1])):
        held = {key: part[n] for n, key in enumerate(evens)}
        for bit in order:
            leaving = [key for key in held if key & bit]
            arrived = swap(jnp.stack([held[key] for key in leaving]), bit)
            held = {
                key: (held[key].astype(F32) + arrived[leaving.index(key ^ bit)].astype(F32))
                for key in held
                if not key & bit
            }
            if len(held) > 1:
                held = {key: item.astype(BF16) for key, item in held.items()}
        parts.append(held[0])
    return jnp.concatenate(parts, axis=0)


def row_gather(shard, axis):
    return lax.all_gather(shard, "row", axis=axis, tiled=True)


def after(values, earlier):
    out = lax.optimization_barrier(tuple(values) + tuple(earlier))
    return out[: len(values)]


def row_scatter(value, axis):
    return lax.psum_scatter(
        value.astype(BF16), "row", scatter_dimension=axis, tiled=True
    ).astype(F32)


def small_sum(value):
    for bit in [1] + chip_bits():
        value = value + swap(value, bit)
    count = lax.axis_size("row")
    total = value
    for k in range(1, count):
        total = total + lax.ppermute(value, "row", [(j, (j + k) % count) for j in range(count)])
    return total


def exchange(value, here, there):
    count = lax.axis_size("row")
    sent = dot(here, value).astype(BF16).reshape(count, -1, value.shape[1])
    got = lax.all_to_all(sent, "row", split_axis=0, concat_axis=0, tiled=True)
    return dot_tn(there, got.reshape(-1, value.shape[1])).astype(BF16)


def body(
    tokens,
    cotangent,
    dealing,
    doc_lengths,
    routes,
    gate_weights,
    attn_gain,
    w_query,
    w_latent,
    latent_gain,
    w_expand,
    w_output,
    ffn_gain,
    shared_gate,
    shared_up,
    shared_down,
    expert_gate,
    expert_up,
    expert_down,
):
    group_rows = routes.shape[0]
    row_count = lax.axis_size("row")
    col_count = lax.axis_size("col")
    row_index = lax.axis_index("row")
    col_index = lax.axis_index("col")
    part_rows = group_rows // col_count
    local_count = expert_gate.shape[0]
    capacity = 4 * group_rows * TOPK // (3 * local_count * col_count)

    def my_part(value):
        return lax.dynamic_slice_in_dim(value, col_index * part_rows, part_rows, 0)

    token_ids = jnp.arange(group_rows, dtype=jnp.int32)
    room = max(16, 5 * group_rows // (16 * row_count) * 4)
    lists = dealing.reshape(row_count, group_rows)
    source = lists // group_rows
    place_in = lists - source * group_rows
    from_here = source == row_index
    rank_here = jnp.where(from_here, jnp.cumsum(from_here.astype(jnp.int32), axis=1) - 1, -1)
    my_source = lax.dynamic_index_in_dim(source, row_index, 0, False)
    by_source = my_source[None, :] == jnp.arange(row_count, dtype=jnp.int32)[:, None]
    count_in = jnp.cumsum(by_source.astype(jnp.int32), axis=1)
    my_rank = jnp.sum(jnp.where(by_source, count_in, 0), axis=0) - 1
    all_counts = jnp.sum(
        (source[:, None, :] == jnp.arange(row_count, dtype=jnp.int32)[None, :, None]).astype(
            jnp.int32
        ),
        axis=2,
    )
    rounds = (jnp.max(all_counts) + room - 1) // room

    def maps(step):
        places = step * room + jnp.arange(room, dtype=jnp.int32)
        hit = rank_here[:, None, :] == places[None, :, None]
        token = jnp.sum(jnp.where(hit, place_in[:, None, :] + 1, 0), axis=2).reshape(-1) - 1
        here = (token[:, None] == token_ids[None, :]).astype(BF16)
        slot = my_rank - step * room
        slot = jnp.where((slot >= 0) & (slot < room), my_source * room + slot, -1)
        there = (jnp.arange(row_count * room, dtype=jnp.int32)[:, None] == slot[None, :]).astype(
            BF16
        )
        return here, there

    here, there = maps(0)

    def more_dealt(carry):
        step, total = carry
        here_more, there_more = maps(step)
        given = jnp.concatenate([tokens, cotangent], axis=1)
        return step + 1, total + exchange(given, here_more, there_more)

    picks, weights = [], []
    slot_ids = jnp.arange(capacity, dtype=jnp.int32)
    for number in range(local_count):
        named = routes == (col_index * local_count + number)
        named_any = jnp.any(named, axis=1)
        running = jnp.cumsum(named_any.astype(jnp.int32))
        place = jnp.where(named_any, running - 1, -1)
        pick = place[None, :] == slot_ids[:, None]
        token_weight = jnp.sum(jnp.where(named, gate_weights, 0.0), axis=1)
        picks.append(pick.astype(BF16))
        weights.append(jnp.sum(jnp.where(pick, token_weight[None, :], 0.0), axis=1))
    document, position = documents(doc_lengths[0], group_rows)

    rows_in, dim = w_query.shape[0], w_query.shape[0] * row_count
    wide = attn_gain.shape[0]
    slice_width = tokens.shape[1]
    more = lax.while_loop(
        lambda carry: carry[0] < rounds,
        more_dealt,
        (jnp.int32(1), jnp.zeros((group_rows, 2 * slice_width), BF16)),
    )[1]
    dealt_x = exchange(tokens, here, there) + more[:, :slice_width]
    full_x = cube_gather(dealt_x, 1)

    query_width = w_query.shape[1]
    lat_rows = rows_in // col_count
    w_latent_s = lax.dynamic_slice_in_dim(w_latent, col_index * lat_rows, lat_rows, 0)
    lat_wide = w_latent.shape[1]
    first_s = jnp.concatenate(
        [
            w_query,
            w_latent_s.reshape(-1, query_width),
            jnp.concatenate([attn_gain, ffn_gain, latent_gain]).reshape(-1, query_width),
        ],
        axis=0,
    )
    first_s = jnp.pad(first_s, ((0, -first_s.shape[0] % 16), (0, 0)))
    first_w = row_gather(first_s[None], 0)
    query_w = first_w[:, :rows_in].reshape(dim, query_width)
    lat_end = rows_in + lat_rows * lat_wide // query_width
    latent_w = cube_gather(first_w[:, rows_in:lat_end].reshape(row_count * lat_rows, lat_wide), 0)
    latent_w = latent_w.reshape(col_count, row_count, lat_rows, lat_wide).transpose(1, 0, 2, 3)
    latent_w = latent_w.reshape(dim, lat_wide)
    gains = first_w[:, lat_end:].reshape(row_count, -1)
    gain_one = gains[:, :wide].reshape(-1).astype(F32)
    gain_two = gains[:, wide : 2 * wide].reshape(-1).astype(F32)
    latent_g = gains[:, 2 * wide : 2 * wide + latent_gain.shape[0]].reshape(-1).astype(F32)

    (cotangent_s,) = after((cotangent,), (dealt_x,))
    dealt_dy = exchange(cotangent_s, here, there) + more[:, slice_width:]
    full_dy = cube_gather(dealt_dy, 1)

    out_rows = w_output.shape[0]
    rest_s = jnp.concatenate([w_output.reshape(-1, w_expand.shape[1]), w_expand])
    (rest_s,) = after((rest_s,), (dealt_x,))
    rest_w = row_gather(rest_s[None], 0)
    out_count = w_output.size // w_expand.shape[1]
    output_w = rest_w[:, :out_count].reshape(row_count, out_rows, -1)
    output_w = output_w.transpose(1, 0, 2).reshape(out_rows, dim)
    expand_w = rest_w[:, out_count:].reshape(-1, w_expand.shape[1])

    expert_w = []
    earlier = [first_w, rest_w]
    for number in range(local_count):
        gather = row_gather if number % 2 == 0 else line_gather
        gu_s = jnp.concatenate([expert_gate[number], expert_up[number]], axis=1)
        (gu_s,) = after((gu_s,), (earlier[-2],))
        gate_up_w = gather(gu_s, 0)
        (d_s,) = after((expert_down[number],), (earlier[-1],))
        down_w = gather(d_s, 1)
        expert_w.append((gate_up_w, down_w))
        earlier += [gate_up_w, down_w]
        if number == 0:
            sgu_s = jnp.concatenate([shared_gate, shared_up], axis=1)
            (sgu_s,) = after((sgu_s,), (gate_up_w,))
            shared_gu_w = row_gather(sgu_s, 0)
            (sd_s,) = after((shared_down,), (down_w,))
            shared_d_w = row_gather(sd_s, 1)

    head_count = query_w.shape[1] // (NOPE + ROPE)
    softmax_scale = (NOPE + ROPE) ** (-0.5)
    block_rows = min(512, group_rows)
    row_number = token_ids
    residual = full_x.astype(F32)
    scale_one = lax.rsqrt(jnp.mean(residual * residual, axis=-1, keepdims=True) + EPSILON)
    normed_one = (residual * scale_one * gain_one).astype(BF16)
    query_raw = dot(normed_one, query_w)
    query_raw = query_raw.reshape(group_rows, head_count, NOPE + ROPE)
    query_heads = jnp.concatenate(
        [query_raw[..., :NOPE], rotate(query_raw[..., NOPE:], position, 1.0)], axis=-1
    ).astype(BF16)
    latent = dot(normed_one, latent_w)
    latent_front = latent[:, :LAT]
    scale_lat = lax.rsqrt(jnp.mean(latent_front * latent_front, axis=-1, keepdims=True) + EPSILON)
    unit_lat = latent_front * scale_lat
    compressed = (unit_lat * latent_g).astype(BF16)
    rope_key = rotate(latent[:, LAT:], position, 1.0).astype(BF16)
    expanded = dot(compressed, expand_w).astype(BF16)
    expanded = expanded.reshape(group_rows, head_count, NOPE + VDIM)
    key_heads = jnp.concatenate(
        [
            expanded[..., :NOPE],
            jnp.broadcast_to(rope_key[:, None, :], (group_rows, head_count, ROPE)),
        ],
        axis=-1,
    )
    value_heads = expanded[..., NOPE:]

    def block_scores(first_row, last_row):
        raw_scores = (
            jnp.einsum(
                "qhd,khd->hqk",
                query_heads[first_row:last_row],
                key_heads[:last_row],
                preferred_element_type=F32,
            )
            * softmax_scale
        )
        allowed = (document[first_row:last_row, None] == document[None, :last_row]) & (
            row_number[first_row:last_row, None] >= row_number[None, :last_row]
        )
        return jnp.where(allowed[None], raw_scores, -1e30)

    mixed_blocks = []
    lse_blocks = []
    for first_row in range(0, group_rows, block_rows):
        last_row = first_row + block_rows
        scores = block_scores(first_row, last_row)
        row_top = jnp.max(scores, axis=-1, keepdims=True)
        exp_scores = jnp.exp(scores - row_top)
        row_total = jnp.sum(exp_scores, axis=-1, keepdims=True)
        probs_low = (exp_scores / row_total).astype(BF16)
        lse_blocks.append(row_top[..., 0] + jnp.log(row_total[..., 0]))
        mixed_blocks.append(
            jnp.einsum(
                "hqk,khd->qhd",
                probs_low,
                value_heads[:last_row],
                preferred_element_type=F32,
            )
        )
    mixed = (
        jnp.concatenate(mixed_blocks, axis=0).reshape(group_rows, head_count * VDIM).astype(BF16)
    )
    attn_part = cube_scatter(dot(mixed, output_w).astype(BF16))
    x_part = my_part(full_x).astype(F32)
    hidden_part = x_part + attn_part
    scale_two = lax.rsqrt(jnp.mean(hidden_part * hidden_part, axis=-1, keepdims=True) + EPSILON)
    unit_two = hidden_part * scale_two
    normed_two = cube_gather((unit_two * gain_two).astype(BF16), 0)

    def branch(rows, grad_result, gate_up_w, down_w):
        width = gate_up_w.shape[1] // 2
        gate_up = dot(rows, gate_up_w)
        gate_out, up_out = gate_up[:, :width], gate_up[:, width:]
        act, slope = silu_parts(gate_out)
        hidden = (act * up_out).astype(BF16)
        grad_hidden = dot_nt(grad_result, down_w)
        grad_gate_up = jnp.concatenate(
            [(grad_hidden * up_out * slope).astype(BF16), (grad_hidden * act).astype(BF16)], axis=1
        )
        result_rows = dot(hidden, down_w)
        grad_rows = dot_nt(grad_gate_up, gate_up_w)
        grad_down = dot_tn(hidden, grad_result).astype(BF16)
        grad_gu = dot_tn(rows, grad_gate_up).astype(BF16)
        return result_rows, grad_rows, grad_gu, grad_down

    moe_terms, grad_two, grad_sgu, grad_sd = branch(normed_two, full_dy, shared_gu_w, shared_d_w)
    grad_gus, grad_downs = [], []
    for number in range(local_count):
        gate_up_w, down_w = expert_w[number]
        if number > 0:
            gate_up_w, down_w = after((gate_up_w, down_w), (grad_gus[-1], grad_downs[-1]))
        pick, weight = picks[number], weights[number]
        rows = dot(pick, normed_two).astype(BF16)
        grad_result = (weight[:, None] * dot(pick, full_dy)).astype(BF16)
        result_rows, grad_rows, grad_gu, grad_down = branch(rows, grad_result, gate_up_w, down_w)
        grad_gus.append(grad_gu)
        grad_downs.append(grad_down)
        moe_terms = moe_terms + dot_tn(pick, (weight[:, None] * result_rows).astype(BF16))
        grad_two = grad_two + dot_tn(pick, grad_rows.astype(BF16))
    grad_gus = [row_scatter(item, 0) for item in grad_gus]
    grad_downs = [row_scatter(item, 1) for item in grad_downs]
    grad_sgu = row_scatter(grad_sgu, 0)
    grad_sd = row_scatter(grad_sd, 1)

    grad_two_part = cube_scatter(grad_two.astype(BF16))
    dy_part = my_part(full_dy).astype(F32)
    hidden_back, gain_two_grad = norm_back(grad_two_part, unit_two, scale_two, gain_two)
    grad_hidden_part = dy_part + hidden_back
    grad_attn = cube_gather(grad_hidden_part.astype(BF16), 0)

    moe_part = cube_scatter(moe_terms.astype(BF16))
    result_part = (hidden_part + moe_part).astype(BF16)
    result_slice = lax.all_to_all(result_part, "col", split_axis=1, concat_axis=0, tiled=True)
    result = exchange(result_slice, there, here)

    grad_output_w = row_scatter(dot_tn(mixed, grad_attn), 1)
    grad_mixed = dot_nt(grad_attn, output_w).astype(BF16)
    grad_mixed = grad_mixed.reshape(group_rows, head_count, VDIM)
    grad_query_blocks = []
    grad_keys = jnp.zeros((group_rows, head_count, NOPE + ROPE), F32)
    grad_values = jnp.zeros((group_rows, head_count, VDIM), F32)
    for block_number, first_row in enumerate(range(0, group_rows, block_rows)):
        last_row = first_row + block_rows
        scores = block_scores(first_row, last_row)
        probs_f = jnp.exp(scores - lse_blocks[block_number][..., None])
        probs_low = probs_f.astype(BF16)
        grad_block = grad_mixed[first_row:last_row]
        grad_probs = jnp.einsum(
            "qhd,khd->hqk", grad_block, value_heads[:last_row], preferred_element_type=F32
        )
        row_inner = jnp.sum(probs_f * grad_probs, axis=-1, keepdims=True)
        grad_scores = (probs_f * (grad_probs - row_inner)).astype(BF16)
        grad_values = grad_values.at[:last_row].add(
            jnp.einsum("hqk,qhd->khd", probs_low, grad_block, preferred_element_type=F32)
        )
        grad_query_blocks.append(
            softmax_scale
            * jnp.einsum(
                "hqk,khd->qhd", grad_scores, key_heads[:last_row], preferred_element_type=F32
            )
        )
        grad_keys = grad_keys.at[:last_row].add(
            softmax_scale
            * jnp.einsum(
                "hqk,qhd->khd",
                grad_scores,
                query_heads[first_row:last_row],
                preferred_element_type=F32,
            )
        )
    grad_query = jnp.concatenate(grad_query_blocks, axis=0)
    grad_query_raw = (
        jnp.concatenate(
            [grad_query[..., :NOPE], rotate(grad_query[..., NOPE:], position, -1.0)], axis=-1
        )
        .astype(BF16)
        .reshape(group_rows, head_count * (NOPE + ROPE))
    )
    grad_one = cube_scatter(dot_nt(grad_query_raw, query_w).astype(BF16))
    grad_expanded = jnp.concatenate([grad_keys[..., :NOPE], grad_values], axis=-1).astype(BF16)
    grad_expanded = grad_expanded.reshape(group_rows, head_count * (NOPE + VDIM))
    grad_compressed = dot_nt(grad_expanded, expand_w)
    grad_rope_key = rotate(jnp.sum(grad_keys[..., NOPE:], axis=1), position, -1.0)
    grad_latent_part = cube_scatter(
        jnp.concatenate([grad_compressed, grad_rope_key], axis=1).astype(BF16)
    )
    grad_front, latent_gain_grad = norm_back(
        grad_latent_part[:, :LAT], my_part(unit_lat), my_part(scale_lat), latent_g
    )
    grad_latent_part = jnp.concatenate([grad_front, grad_latent_part[:, LAT:]], axis=1).astype(BF16)
    latent_term = dot_nt(grad_latent_part, latent_w)
    grad_one = grad_one + latent_term
    scale_one_part = my_part(scale_one)
    input_back, gain_one_grad = norm_back(
        grad_one, x_part * scale_one_part, scale_one_part, gain_one
    )
    grad_input = (grad_hidden_part + input_back).astype(BF16)
    grad_slice = lax.all_to_all(grad_input, "col", split_axis=1, concat_axis=0, tiled=True)
    tokens_grad = exchange(grad_slice, there, here)

    def more_back(carry):
        step, total = carry
        here_more, there_more = maps(step)
        dealt = jnp.concatenate([result_slice, grad_slice], axis=1)
        return step + 1, total + exchange(dealt, there_more, here_more)

    more = lax.while_loop(
        lambda carry: carry[0] < rounds,
        more_back,
        (jnp.int32(1), jnp.concatenate([result, tokens_grad], axis=1)),
    )[1]
    result, tokens_grad = more[:, :slice_width], more[:, slice_width:]

    grad_query_w = row_scatter(dot_tn(normed_one, grad_query_raw), 0)
    grad_expand_w = row_scatter(dot_tn(compressed, grad_expanded), 0)
    grad_latent = cube_gather(grad_latent_part, 0)
    my_columns = lax.dynamic_index_in_dim(
        normed_one.reshape(group_rows, row_count, col_count, lat_rows), col_index, 2, False
    ).reshape(group_rows, row_count * lat_rows)
    grad_latent_w = cube_gather(row_scatter(dot_tn(my_columns, grad_latent), 0).astype(BF16), 0)
    grad_latent_w = grad_latent_w.astype(F32)
    gain_grads = small_sum(jnp.concatenate([gain_one_grad, gain_two_grad, latent_gain_grad]))
    width_two = gain_one_grad.shape[0]
    width_lat = latent_gain_grad.shape[0]

    def my_rows(value):
        width = value.shape[0] // row_count
        return lax.dynamic_slice_in_dim(value, row_index * width, width, 0)

    return (
        result,
        tokens_grad,
        my_rows(gain_grads[:width_two]),
        grad_query_w,
        grad_latent_w,
        my_rows(gain_grads[2 * width_two : 2 * width_two + width_lat]),
        grad_expand_w,
        grad_output_w,
        my_rows(gain_grads[width_two : 2 * width_two]),
        grad_sgu[:, : shared_gate.shape[1]],
        grad_sgu[:, shared_gate.shape[1] :],
        grad_sd,
        jnp.stack([item[:, : expert_gate.shape[2]] for item in grad_gus]),
        jnp.stack([item[:, expert_gate.shape[2] :] for item in grad_gus]),
        jnp.stack(grad_downs),
    )


def solution(mesh):
    return jax.shard_map(
        body,
        mesh=mesh,
        in_specs=(
            P("row", "col"),
            P("row", "col"),
            P(),
            P("row", None),
            P("row", None),
            P("row", None),
            P("row"),
            P("row", "col"),
            P("row", None),
            P("row"),
            P("row", "col"),
            P("col", "row"),
            P("row"),
            P("row", "col"),
            P("row", "col"),
            P("col", "row"),
            P("col", "row", None),
            P("col", "row", None),
            P("col", None, "row"),
        ),
        out_specs=(
            P("row", "col"),
            P("row", "col"),
            P("row"),
            P("row", "col"),
            P("row", None),
            P("row"),
            P("row", "col"),
            P("col", "row"),
            P("row"),
            P("row", "col"),
            P("row", "col"),
            P("col", "row"),
            P("col", "row", None),
            P("col", "row", None),
            P("col", None, "row"),
        ),
        check_vma=False,
    )
```

```python
import jax
import jax.numpy as jnp
from jax import lax
from jax.sharding import PartitionSpec as P

NOPE = 128
ROPE = 64
VDIM = 128
LAT = 512
TOPK = 6

EPSILON = 1e-06
F32 = jnp.float32
BF16 = jnp.bfloat16


def rotate(value, position, orient):
    half_width = value.shape[-1] // 2
    frequency = 10000.0 ** (-jnp.arange(half_width, dtype=F32) / half_width)
    angles = position.astype(F32)[:, None] * frequency[None, :]
    shape_out = (value.shape[0],) + (1,) * (value.ndim - 2) + (half_width,)
    cosine = jnp.cos(angles).reshape(shape_out)
    sine_part = jnp.sin(angles).reshape(shape_out)
    first_half = value[..., :half_width]
    second = value[..., half_width:]
    return jnp.concatenate(
        [
            first_half * cosine - orient * second * sine_part,
            second * cosine + orient * first_half * sine_part,
        ],
        axis=-1,
    )


def documents(lengths_row, row_count):
    doc_ends = jnp.cumsum(lengths_row)
    starts = doc_ends - lengths_row
    row_number = jnp.arange(row_count, dtype=jnp.int32)
    document = jnp.sum((row_number[:, None] >= doc_ends[None, :]).astype(jnp.int32), axis=1)
    onehot = document[:, None] == jnp.arange(lengths_row.shape[0], dtype=jnp.int32)[None, :]
    position = row_number - jnp.sum(jnp.where(onehot, starts[None, :], 0), axis=1)
    return (document, position)


def silu_parts(value):
    sigmoid_value = jax.nn.sigmoid(value)
    activation = value * sigmoid_value
    activ_slope = sigmoid_value * (1.0 + value * (1.0 - sigmoid_value))
    return (activation, activ_slope)


def norm_back(grad_normed, unit_rows, row_scale, gain_vector):
    scaled = grad_normed * gain_vector
    row_inner = jnp.mean(scaled * unit_rows, axis=-1, keepdims=True)
    return (row_scale * (scaled - unit_rows * row_inner), jnp.sum(grad_normed * unit_rows, axis=0))


def dot(left, right):
    return jnp.dot(left, right, preferred_element_type=F32)


def dot_nt(left, right):
    return lax.dot_general(left, right, (((1,), (1,)), ((), ())), preferred_element_type=F32)


def dot_tn(left, right):
    return lax.dot_general(left, right, (((0,), (0,)), ((), ())), preferred_element_type=F32)


def line_scatter(values):
    count = lax.axis_size("row")
    index = lax.axis_index("row")

    def block(j):
        place = jnp.clip(j, 0, count - 1)
        return jnp.concatenate(
            [
                lax.dynamic_slice_in_dim(
                    value, place * (value.shape[0] // count), value.shape[0] // count, 0
                )
                for value in values
            ],
            axis=1,
        )

    right, left = None, None
    for step in range(1, count):
        right_out, left_out = block(index + count - step), block(index - count + step)
        if right is not None:
            right_out = (right_out.astype(F32) + right.astype(F32)).astype(BF16)
            left_out = (left_out.astype(F32) + left.astype(F32)).astype(BF16)
        yield right_out, left_out
        right = lax.ppermute(right_out, "row", [(j, j + 1) for j in range(0, step)])
        left = lax.ppermute(left_out, "row", [(j, j - 1) for j in range(count - step, count)])
    yield block(index).astype(F32) + right.astype(F32) + left.astype(F32)


def swap(value, bit):
    return lax.ppermute(value, "col", [(j, j ^ bit) for j in range(lax.axis_size("col"))])


def chip_bits():
    return [1 << b for b in range(1, (lax.axis_size("col") - 1).bit_length())]


def chip_swap(value, step):
    bits = chip_bits()
    other = bits[::-1]
    return lax.ppermute(
        value,
        "col",
        [(j, j ^ (other if j % 2 else bits)[step]) for j in range(lax.axis_size("col"))],
    )


def block_at(device, place):
    bits = chip_bits()
    even = sum(bit for n, bit in enumerate(bits) if place >> n & 1)
    odd = sum(bit for n, bit in enumerate(bits[::-1]) if place >> n & 1)
    return jnp.bitwise_xor(device, jnp.where(device % 2 == 0, even, odd))


def cube_gather(block, axis):
    count = lax.axis_size("col")
    index = lax.axis_index("col")
    width = block.shape[axis]
    shape = list(block.shape)
    shape[axis] = width * count
    out = jnp.zeros(shape, block.dtype)
    held = block[None]
    sibling = jnp.bitwise_xor(index, 1)
    done = 0
    for step in range(len(chip_bits()) + 1):
        theirs = swap(held[done:], 1)
        for place in range(done, held.shape[0]):
            for item, owner in ((held[place], index), (theirs[place - done], sibling)):
                out = lax.dynamic_update_slice_in_dim(
                    out, item, block_at(owner, place) * width, axis
                )
        done = held.shape[0]
        if step < len(chip_bits()):
            held = jnp.concatenate([held, chip_swap(held, step)], axis=0)
    return out


def cube_scatter(value):
    count = lax.axis_size("col")
    index = lax.axis_index("col")
    rows = value.shape[0] // count

    def blocks(device):
        return jnp.stack(
            [
                lax.dynamic_slice_in_dim(value, block_at(device, place) * rows, rows, 0)
                for place in range(count // 2)
            ]
        )

    got = swap(blocks(jnp.bitwise_xor(index, 1)), 1)
    held = blocks(index).astype(F32) + got.astype(F32)
    for step in range(len(chip_bits()) - 1, -1, -1):
        held = held.astype(BF16)
        half = held.shape[0] // 2
        got = chip_swap(held[half:], step)
        held = held[:half].astype(F32) + got.astype(F32)
    return held[0]


def row_gather(shard, axis):
    return lax.all_gather(shard, "row", axis=axis, tiled=True)


def after(values, earlier):
    out = lax.optimization_barrier(tuple(values) + tuple(earlier))
    return out[: len(values)]


def row_scatter(value, axis):
    return lax.psum_scatter(value, "row", scatter_dimension=axis, tiled=True)


def small_sum(value):
    for bit in [1] + chip_bits():
        value = value + swap(value, bit)
    count = lax.axis_size("row")
    total = value
    for k in range(1, count):
        total = total + lax.ppermute(value, "row", [(j, (j + k) % count) for j in range(count)])
    return total


def exchange(value, here, there):
    count = lax.axis_size("row")
    sent = dot(here, value).astype(BF16).reshape(count, -1, value.shape[1])
    got = lax.all_to_all(sent, "row", split_axis=0, concat_axis=0, tiled=True)
    return dot_tn(there, got.reshape(-1, value.shape[1])).astype(BF16)


def body(
    tokens,
    cotangent,
    dealing,
    doc_lengths,
    routes,
    gate_weights,
    attn_gain,
    w_query,
    w_latent,
    latent_gain,
    w_expand,
    w_output,
    ffn_gain,
    shared_gate,
    shared_up,
    shared_down,
    expert_gate,
    expert_up,
    expert_down,
):
    group_rows = routes.shape[0]
    row_count = lax.axis_size("row")
    col_count = lax.axis_size("col")
    row_index = lax.axis_index("row")
    col_index = lax.axis_index("col")
    part_rows = group_rows // col_count
    local_count = expert_gate.shape[0]
    capacity = 4 * group_rows * TOPK // (3 * local_count * col_count)

    def my_part(value):
        return lax.dynamic_slice_in_dim(value, col_index * part_rows, part_rows, 0)

    token_ids = jnp.arange(group_rows, dtype=jnp.int32)
    room = max(16, 5 * group_rows // (16 * row_count) * 4)
    lists = dealing.reshape(row_count, group_rows)
    source = lists // group_rows
    place_in = lists - source * group_rows
    from_here = source == row_index
    rank_here = jnp.where(from_here, jnp.cumsum(from_here.astype(jnp.int32), axis=1) - 1, -1)
    my_source = lax.dynamic_index_in_dim(source, row_index, 0, False)
    by_source = my_source[None, :] == jnp.arange(row_count, dtype=jnp.int32)[:, None]
    count_in = jnp.cumsum(by_source.astype(jnp.int32), axis=1)
    my_rank = jnp.sum(jnp.where(by_source, count_in, 0), axis=0) - 1
    all_counts = jnp.sum(
        (source[:, None, :] == jnp.arange(row_count, dtype=jnp.int32)[None, :, None]).astype(
            jnp.int32
        ),
        axis=2,
    )
    rounds = (jnp.max(all_counts) + room - 1) // room

    def maps(step):
        places = step * room + jnp.arange(room, dtype=jnp.int32)
        hit = rank_here[:, None, :] == places[None, :, None]
        token = jnp.sum(jnp.where(hit, place_in[:, None, :] + 1, 0), axis=2).reshape(-1) - 1
        here = (token[:, None] == token_ids[None, :]).astype(BF16)
        slot = my_rank - step * room
        slot = jnp.where((slot >= 0) & (slot < room), my_source * room + slot, -1)
        there = (jnp.arange(row_count * room, dtype=jnp.int32)[:, None] == slot[None, :]).astype(
            BF16
        )
        return here, there

    here, there = maps(0)

    def more_dealt(carry):
        step, total = carry
        here_more, there_more = maps(step)
        given = jnp.concatenate([tokens, cotangent], axis=1)
        return step + 1, total + exchange(given, here_more, there_more)

    picks, weights = [], []
    slot_ids = jnp.arange(capacity, dtype=jnp.int32)
    for number in range(local_count):
        named = routes == (col_index * local_count + number)
        named_any = jnp.any(named, axis=1)
        running = jnp.cumsum(named_any.astype(jnp.int32))
        place = jnp.where(named_any, running - 1, -1)
        pick = place[None, :] == slot_ids[:, None]
        token_weight = jnp.sum(jnp.where(named, gate_weights, 0.0), axis=1)
        picks.append(pick.astype(BF16))
        weights.append(jnp.sum(jnp.where(pick, token_weight[None, :], 0.0), axis=1))
    document, position = documents(doc_lengths[0], group_rows)

    rows_in, dim = w_query.shape[0], w_query.shape[0] * row_count
    wide = attn_gain.shape[0]
    slice_width = tokens.shape[1]
    more = lax.while_loop(
        lambda carry: carry[0] < rounds,
        more_dealt,
        (jnp.int32(1), jnp.zeros((group_rows, 2 * slice_width), BF16)),
    )[1]
    dealt_x = exchange(tokens, here, there) + more[:, :slice_width]
    full_x = cube_gather(dealt_x, 1)

    query_width = w_query.shape[1]
    lat_rows = rows_in // col_count
    w_latent_s = lax.dynamic_slice_in_dim(w_latent, col_index * lat_rows, lat_rows, 0)
    lat_wide = w_latent.shape[1]
    first_s = jnp.concatenate(
        [
            w_query,
            w_latent_s.reshape(-1, query_width),
            jnp.concatenate([attn_gain, ffn_gain, latent_gain]).reshape(-1, query_width),
        ],
        axis=0,
    )
    first_s = jnp.pad(first_s, ((0, -first_s.shape[0] % 16), (0, 0)))
    first_w = row_gather(first_s[None], 0)
    query_w = first_w[:, :rows_in].reshape(dim, query_width)
    lat_end = rows_in + lat_rows * lat_wide // query_width
    latent_w = cube_gather(first_w[:, rows_in:lat_end].reshape(row_count * lat_rows, lat_wide), 0)
    latent_w = latent_w.reshape(col_count, row_count, lat_rows, lat_wide).transpose(1, 0, 2, 3)
    latent_w = latent_w.reshape(dim, lat_wide)
    gains = first_w[:, lat_end:].reshape(row_count, -1)
    gain_one = gains[:, :wide].reshape(-1).astype(F32)
    gain_two = gains[:, wide : 2 * wide].reshape(-1).astype(F32)
    latent_g = gains[:, 2 * wide : 2 * wide + latent_gain.shape[0]].reshape(-1).astype(F32)

    (cotangent_s,) = after((cotangent,), (dealt_x,))
    dealt_dy = exchange(cotangent_s, here, there) + more[:, slice_width:]
    full_dy = cube_gather(dealt_dy, 1)

    out_rows = w_output.shape[0]
    rest_s = jnp.concatenate([w_output.reshape(-1, w_expand.shape[1]), w_expand])
    (rest_s,) = after((rest_s,), (dealt_x,))
    rest_w = row_gather(rest_s[None], 0)
    out_count = w_output.size // w_expand.shape[1]
    output_w = rest_w[:, :out_count].reshape(row_count, out_rows, -1)
    output_w = output_w.transpose(1, 0, 2).reshape(out_rows, dim)
    expand_w = rest_w[:, out_count:].reshape(-1, w_expand.shape[1])

    queue = [first_w, rest_w]

    def queued(shard, axis):
        (shard,) = after((shard,), (queue[-2],))
        queue.append(row_gather(shard, axis))
        return queue[-1]

    expert_w = []
    for number in range(local_count):
        gate_up_s = jnp.concatenate([expert_gate[number], expert_up[number]], axis=1)
        expert_w.append((queued(gate_up_s, 0), queued(expert_down[number], 1)))
        if number == 0:
            shared_gu_w = queued(jnp.concatenate([shared_gate, shared_up], axis=1), 0)
            shared_d_w = queued(shared_down, 1)

    head_count = query_w.shape[1] // (NOPE + ROPE)
    softmax_scale = (NOPE + ROPE) ** (-0.5)
    block_rows = min(512, group_rows)
    row_number = token_ids
    residual = full_x.astype(F32)
    scale_one = lax.rsqrt(jnp.mean(residual * residual, axis=-1, keepdims=True) + EPSILON)
    normed_one = (residual * scale_one * gain_one).astype(BF16)
    query_raw = dot(normed_one, query_w)
    query_raw = query_raw.reshape(group_rows, head_count, NOPE + ROPE)
    query_heads = jnp.concatenate(
        [query_raw[..., :NOPE], rotate(query_raw[..., NOPE:], position, 1.0)], axis=-1
    ).astype(BF16)
    latent = dot(normed_one, latent_w)
    latent_front = latent[:, :LAT]
    scale_lat = lax.rsqrt(jnp.mean(latent_front * latent_front, axis=-1, keepdims=True) + EPSILON)
    unit_lat = latent_front * scale_lat
    compressed = (unit_lat * latent_g).astype(BF16)
    rope_key = rotate(latent[:, LAT:], position, 1.0).astype(BF16)
    expanded = dot(compressed, expand_w).astype(BF16)
    expanded = expanded.reshape(group_rows, head_count, NOPE + VDIM)
    key_heads = jnp.concatenate(
        [
            expanded[..., :NOPE],
            jnp.broadcast_to(rope_key[:, None, :], (group_rows, head_count, ROPE)),
        ],
        axis=-1,
    )
    value_heads = expanded[..., NOPE:]

    def block_scores(first_row, last_row):
        raw_scores = (
            jnp.einsum(
                "qhd,khd->hqk",
                query_heads[first_row:last_row],
                key_heads[:last_row],
                preferred_element_type=F32,
            )
            * softmax_scale
        )
        allowed = (document[first_row:last_row, None] == document[None, :last_row]) & (
            row_number[first_row:last_row, None] >= row_number[None, :last_row]
        )
        return jnp.where(allowed[None], raw_scores, -1e30)

    mixed_blocks = []
    lse_blocks = []
    for first_row in range(0, group_rows, block_rows):
        last_row = first_row + block_rows
        scores = block_scores(first_row, last_row)
        row_top = jnp.max(scores, axis=-1, keepdims=True)
        exp_scores = jnp.exp(scores - row_top)
        row_total = jnp.sum(exp_scores, axis=-1, keepdims=True)
        probs_low = (exp_scores / row_total).astype(BF16)
        lse_blocks.append(row_top[..., 0] + jnp.log(row_total[..., 0]))
        mixed_blocks.append(
            jnp.einsum(
                "hqk,khd->qhd",
                probs_low,
                value_heads[:last_row],
                preferred_element_type=F32,
            )
        )
    mixed = (
        jnp.concatenate(mixed_blocks, axis=0).reshape(group_rows, head_count * VDIM).astype(BF16)
    )
    attn_part = cube_scatter(dot(mixed, output_w).astype(BF16))
    x_part = my_part(full_x).astype(F32)
    hidden_part = x_part + attn_part
    scale_two = lax.rsqrt(jnp.mean(hidden_part * hidden_part, axis=-1, keepdims=True) + EPSILON)
    unit_two = hidden_part * scale_two
    normed_two = cube_gather((unit_two * gain_two).astype(BF16), 0)

    def forward(rows, gate_up_w):
        width = gate_up_w.shape[1] // 2
        gate_up = dot(rows, gate_up_w)
        gate_out, up_out = gate_up[:, :width], gate_up[:, width:]
        act, slope = silu_parts(gate_out)
        hidden = (act * up_out).astype(BF16)
        return hidden, act, up_out * slope

    def backward(grad_hidden, act, up_slope):
        return jnp.concatenate(
            [(grad_hidden * up_slope).astype(BF16), (grad_hidden * act).astype(BF16)], axis=1
        )

    lines = []
    grad_two, moe_terms = None, None
    for number in range(local_count):
        gate_up_w, down_w = expert_w[number]
        pick, weight = picks[number], weights[number]
        rows = dot(pick, normed_two).astype(BF16)
        grad_result = (weight[:, None] * dot(pick, full_dy)).astype(BF16)
        for line in lines:
            (gate_up_w,) = after((gate_up_w,), next(line))
        hidden, act, up_slope = forward(rows, gate_up_w)
        grad_gate_up = backward(dot_nt(grad_result, down_w), act, up_slope)
        for line in lines:
            (grad_gate_up,) = after((grad_gate_up,), next(line))
        grad_rows = dot_nt(grad_gate_up, gate_up_w).astype(BF16)
        term = dot_tn(pick, grad_rows)
        grad_two = term if grad_two is None else grad_two + term
        if number + 1 < local_count:
            grad_gu = dot_tn(rows, grad_gate_up).astype(BF16)
            grad_down = dot_tn(grad_result, hidden).astype(BF16)
            line = line_scatter([grad_gu, grad_down])
            messages = next(line)
            lines.append(line)
            shared_in, full_dy_s = after((normed_two, full_dy), messages)
            term = dot_tn(pick, (weight[:, None] * dot(hidden, down_w)).astype(BF16))
            moe_terms = term if moe_terms is None else moe_terms + term
        if number == 0:
            shared_hidden, shared_act, shared_us = forward(shared_in, shared_gu_w)
            grad_shared_gu = backward(dot_nt(full_dy_s, shared_d_w), shared_act, shared_us)
            grad_two = grad_two + dot_nt(grad_shared_gu, shared_gu_w)
            moe_terms = moe_terms + dot(shared_hidden, shared_d_w)
            grad_sgu = dot_tn(shared_in, grad_shared_gu).astype(BF16)
            grad_sd = dot_tn(shared_hidden, full_dy_s).astype(BF16)
    ordered = []

    def queued_sum(value, axis):
        if len(ordered) > 1:
            (value,) = after((value,), (ordered[-2],))
        ordered.append(row_scatter(value.astype(BF16), axis))
        return ordered[-1]

    grad_sgu = queued_sum(grad_sgu, 0)
    grad_sd = queued_sum(grad_sd, 1)
    last_gu = queued_sum(dot_tn(rows, grad_gate_up), 0)
    last_down = queued_sum(dot_tn(hidden, grad_result), 1)
    grad_two = grad_two.astype(BF16)
    (hidden_late, weight_late) = after((hidden, weight), (grad_two,))
    term = dot_tn(pick, (weight_late[:, None] * dot(hidden_late, down_w)).astype(BF16))
    moe_terms = (moe_terms + term).astype(BF16)

    grad_two_part = cube_scatter(grad_two)
    dy_part = my_part(full_dy).astype(F32)
    hidden_back, gain_two_grad = norm_back(grad_two_part, unit_two, scale_two, gain_two)
    grad_hidden_part = dy_part + hidden_back
    grad_attn = cube_gather(grad_hidden_part.astype(BF16), 0)

    (moe_terms,) = after((moe_terms,), (grad_attn,))
    moe_part = cube_scatter(moe_terms)
    result_part = (hidden_part + moe_part).astype(BF16)
    result_slice = lax.all_to_all(result_part, "col", split_axis=1, concat_axis=0, tiled=True)
    result = exchange(result_slice, there, here)

    line_sums = [list(line)[-1] for line in lines]
    grad_attn, *line_sums = after((grad_attn, *line_sums), ())
    grad_output_w = queued_sum(dot_tn(mixed, grad_attn), 1)
    grad_mixed = dot_nt(grad_attn, output_w).astype(BF16)
    grad_mixed = grad_mixed.reshape(group_rows, head_count, VDIM)
    grad_query_blocks = []
    grad_keys = jnp.zeros((group_rows, head_count, NOPE + ROPE), F32)
    grad_values = jnp.zeros((group_rows, head_count, VDIM), F32)
    for block_number, first_row in enumerate(range(0, group_rows, block_rows)):
        last_row = first_row + block_rows
        scores = block_scores(first_row, last_row)
        probs_f = jnp.exp(scores - lse_blocks[block_number][..., None])
        probs_low = probs_f.astype(BF16)
        grad_block = grad_mixed[first_row:last_row]
        grad_probs = jnp.einsum(
            "qhd,khd->hqk", grad_block, value_heads[:last_row], preferred_element_type=F32
        )
        row_inner = jnp.sum(probs_f * grad_probs, axis=-1, keepdims=True)
        grad_scores = (probs_f * (grad_probs - row_inner)).astype(BF16)
        grad_values = grad_values.at[:last_row].add(
            jnp.einsum("hqk,qhd->khd", probs_low, grad_block, preferred_element_type=F32)
        )
        grad_query_blocks.append(
            softmax_scale
            * jnp.einsum(
                "hqk,khd->qhd", grad_scores, key_heads[:last_row], preferred_element_type=F32
            )
        )
        grad_keys = grad_keys.at[:last_row].add(
            softmax_scale
            * jnp.einsum(
                "hqk,qhd->khd",
                grad_scores,
                query_heads[first_row:last_row],
                preferred_element_type=F32,
            )
        )
    grad_query = jnp.concatenate(grad_query_blocks, axis=0)
    grad_query_raw = (
        jnp.concatenate(
            [grad_query[..., :NOPE], rotate(grad_query[..., NOPE:], position, -1.0)], axis=-1
        )
        .astype(BF16)
        .reshape(group_rows, head_count * (NOPE + ROPE))
    )
    grad_one = cube_scatter(dot_nt(grad_query_raw, query_w).astype(BF16))
    grad_expanded = jnp.concatenate([grad_keys[..., :NOPE], grad_values], axis=-1).astype(BF16)
    grad_expanded = grad_expanded.reshape(group_rows, head_count * (NOPE + VDIM))
    grad_compressed = dot_nt(grad_expanded, expand_w)
    grad_rope_key = rotate(jnp.sum(grad_keys[..., NOPE:], axis=1), position, -1.0)
    grad_latent_part = cube_scatter(
        jnp.concatenate([grad_compressed, grad_rope_key], axis=1).astype(BF16)
    )
    grad_front, latent_gain_grad = norm_back(
        grad_latent_part[:, :LAT], my_part(unit_lat), my_part(scale_lat), latent_g
    )
    grad_latent_part = jnp.concatenate([grad_front, grad_latent_part[:, LAT:]], axis=1).astype(BF16)
    latent_term = dot_nt(grad_latent_part, latent_w)
    grad_one = grad_one + latent_term
    scale_one_part = my_part(scale_one)
    input_back, gain_one_grad = norm_back(
        grad_one, x_part * scale_one_part, scale_one_part, gain_one
    )
    grad_input = (grad_hidden_part + input_back).astype(BF16)
    grad_slice = lax.all_to_all(grad_input, "col", split_axis=1, concat_axis=0, tiled=True)
    tokens_grad = exchange(grad_slice, there, here)

    def more_back(carry):
        step, total = carry
        here_more, there_more = maps(step)
        dealt = jnp.concatenate([result_slice, grad_slice], axis=1)
        return step + 1, total + exchange(dealt, there_more, here_more)

    more = lax.while_loop(
        lambda carry: carry[0] < rounds,
        more_back,
        (jnp.int32(1), jnp.concatenate([result, tokens_grad], axis=1)),
    )[1]
    result, tokens_grad = more[:, :slice_width], more[:, slice_width:]

    grad_expand_w = queued_sum(dot_tn(compressed, grad_expanded), 0)
    grad_query_w = queued_sum(dot_tn(normed_one, grad_query_raw), 0)
    grad_latent = cube_gather(grad_latent_part, 0)
    my_columns = lax.dynamic_index_in_dim(
        normed_one.reshape(group_rows, row_count, col_count, lat_rows), col_index, 2, False
    ).reshape(group_rows, row_count * lat_rows)
    grad_latent_w = cube_gather(queued_sum(dot_tn(my_columns, grad_latent), 0), 0)
    gain_grads = small_sum(jnp.concatenate([gain_one_grad, gain_two_grad, latent_gain_grad]))
    width_ff = expert_gate.shape[2]
    grad_gus = line_sums + [last_gu]
    grad_downs = [item[:, 2 * width_ff :].T for item in line_sums] + [last_down]
    width_two = gain_one_grad.shape[0]
    width_lat = latent_gain_grad.shape[0]

    def my_rows(value):
        width = value.shape[0] // row_count
        return lax.dynamic_slice_in_dim(value, row_index * width, width, 0)

    return (
        result,
        tokens_grad,
        my_rows(gain_grads[:width_two]),
        grad_query_w.astype(F32),
        grad_latent_w.astype(F32),
        my_rows(gain_grads[2 * width_two : 2 * width_two + width_lat]),
        grad_expand_w.astype(F32),
        grad_output_w.astype(F32),
        my_rows(gain_grads[width_two : 2 * width_two]),
        grad_sgu[:, : shared_gate.shape[1]].astype(F32),
        grad_sgu[:, shared_gate.shape[1] :].astype(F32),
        grad_sd.astype(F32),
        jnp.stack([item[:, :width_ff] for item in grad_gus]).astype(F32),
        jnp.stack([item[:, width_ff : 2 * width_ff] for item in grad_gus]).astype(F32),
        jnp.stack(grad_downs).astype(F32),
    )


def solution(mesh):
    return jax.shard_map(
        body,
        mesh=mesh,
        in_specs=(
            P("row", "col"),
            P("row", "col"),
            P(),
            P("row", None),
            P("row", None),
            P("row", None),
            P("row"),
            P("row", "col"),
            P("row", None),
            P("row"),
            P("row", "col"),
            P("col", "row"),
            P("row"),
            P("row", "col"),
            P("row", "col"),
            P("col", "row"),
            P("col", "row", None),
            P("col", "row", None),
            P("col", None, "row"),
        ),
        out_specs=(
            P("row", "col"),
            P("row", "col"),
            P("row"),
            P("row", "col"),
            P("row", None),
            P("row"),
            P("row", "col"),
            P("col", "row"),
            P("row"),
            P("row", "col"),
            P("row", "col"),
            P("col", "row"),
            P("col", "row", None),
            P("col", "row", None),
            P("col", None, "row"),
        ),
        check_vma=False,
    )
```

```python
import jax
import jax.numpy as jnp
from jax import lax
from jax.experimental.layout import Layout, with_layout_constraint
from jax.sharding import PartitionSpec as P

NOPE = 128
ROPE = 64
VDIM = 128
LAT = 512
TOPK = 6

EPSILON = 1e-06
F32 = jnp.float32
BF16 = jnp.bfloat16


def rotate(value, position, orient):
    half_width = value.shape[-1] // 2
    frequency = 10000.0 ** (-jnp.arange(half_width, dtype=F32) / half_width)
    angles = position.astype(F32)[:, None] * frequency[None, :]
    shape_out = (value.shape[0],) + (1,) * (value.ndim - 2) + (half_width,)
    cosine = jnp.cos(angles).reshape(shape_out)
    sine_part = jnp.sin(angles).reshape(shape_out)
    first_half = value[..., :half_width]
    second = value[..., half_width:]
    return jnp.concatenate(
        [
            first_half * cosine - orient * second * sine_part,
            second * cosine + orient * first_half * sine_part,
        ],
        axis=-1,
    )


def documents(lengths_row, row_count):
    doc_ends = jnp.cumsum(lengths_row)
    starts = doc_ends - lengths_row
    row_number = jnp.arange(row_count, dtype=jnp.int32)
    document = jnp.sum((row_number[:, None] >= doc_ends[None, :]).astype(jnp.int32), axis=1)
    onehot = document[:, None] == jnp.arange(lengths_row.shape[0], dtype=jnp.int32)[None, :]
    position = row_number - jnp.sum(jnp.where(onehot, starts[None, :], 0), axis=1)
    return (document, position)


def silu_parts(value):
    sigmoid_value = jax.nn.sigmoid(value)
    activation = value * sigmoid_value
    activ_slope = sigmoid_value * (1.0 + value * (1.0 - sigmoid_value))
    return (activation, activ_slope)


def norm_back(grad_normed, unit_rows, row_scale, gain_vector):
    scaled = grad_normed * gain_vector
    row_inner = jnp.mean(scaled * unit_rows, axis=-1, keepdims=True)
    return (row_scale * (scaled - unit_rows * row_inner), jnp.sum(grad_normed * unit_rows, axis=0))


def dot(left, right):
    return jnp.dot(left, right, preferred_element_type=F32)


def dot_nt(left, right):
    return lax.dot_general(left, right, (((1,), (1,)), ((), ())), preferred_element_type=F32)


def dot_tn(left, right):
    return lax.dot_general(left, right, (((0,), (0,)), ((), ())), preferred_element_type=F32)


def row_major(value):
    return with_layout_constraint(value, Layout(tuple(range(value.ndim))))


def row_swap(value, bit):
    return lax.ppermute(value, "row", [(j, j ^ bit) for j in range(lax.axis_size("row"))])


def mate(value):
    return row_swap(value, lax.axis_size("row") // 2)


def half_bits():
    return [1 << b for b in range((lax.axis_size("row") // 2).bit_length() - 1)]


def expert_gather(kept, given, axis):
    count = lax.axis_size("row")
    index = lax.axis_index("row")
    width = kept.shape[axis]
    shape = list(kept.shape)
    shape[axis] = width * count
    out = jnp.zeros(shape, kept.dtype)
    for first, item in ((0, kept), (count // 2, mate(given))):
        items = {first: item}
        for bit in half_bits():
            items.update({key ^ bit: row_swap(items[key], bit) for key in list(items)})
        for key, piece in items.items():
            out = lax.dynamic_update_slice_in_dim(
                out, piece, jnp.bitwise_xor(index, key) * width, axis
            )
    return out


def expert_scatter(value, axis):
    count = lax.axis_size("row")
    index = lax.axis_index("row")
    width = value.shape[axis] // count
    sums = []
    for first in (count // 2, 0):
        items = {
            key: lax.dynamic_slice_in_dim(
                value, jnp.bitwise_xor(index, key ^ first) * width, width, axis
            )
            for key in range(count // 2)
        }
        for bit in half_bits()[::-1]:
            items = {
                key: (
                    items[key].astype(F32) + row_swap(items[key ^ bit], bit).astype(F32)
                ).astype(BF16)
                for key in items
                if key < bit
            }
        sums.append(items[0])
    return sums[1], sums[0]


def swap(value, bit):
    return lax.ppermute(value, "col", [(j, j ^ bit) for j in range(lax.axis_size("col"))])


def chip_bits():
    return [1 << b for b in range(1, (lax.axis_size("col") - 1).bit_length())]


def chip_swap(value, step):
    bits = chip_bits()
    other = bits[::-1]
    return lax.ppermute(
        value,
        "col",
        [(j, j ^ (other if j % 2 else bits)[step]) for j in range(lax.axis_size("col"))],
    )


def block_at(device, place):
    bits = chip_bits()
    even = sum(bit for n, bit in enumerate(bits) if place >> n & 1)
    odd = sum(bit for n, bit in enumerate(bits[::-1]) if place >> n & 1)
    return jnp.bitwise_xor(device, jnp.where(device % 2 == 0, even, odd))


def cube_gather(block, axis):
    count = lax.axis_size("col")
    index = lax.axis_index("col")
    width = block.shape[axis]
    shape = list(block.shape)
    shape[axis] = width * count
    out = jnp.zeros(shape, block.dtype)
    held = row_major(block)[None]
    sibling = jnp.bitwise_xor(index, 1)
    done = 0
    for step in range(len(chip_bits()) + 1):
        theirs = swap(held[done:], 1)
        for place in range(done, held.shape[0]):
            for item, owner in ((held[place], index), (theirs[place - done], sibling)):
                out = lax.dynamic_update_slice_in_dim(
                    out, item, block_at(owner, place) * width, axis
                )
        done = held.shape[0]
        if step < len(chip_bits()):
            held = jnp.concatenate([held, chip_swap(held, step)], axis=0)
    return out


def cube_scatter(value):
    count = lax.axis_size("col")
    index = lax.axis_index("col")
    rows = value.shape[0] // count
    value = row_major(value)

    def blocks(device):
        return jnp.stack(
            [
                lax.dynamic_slice_in_dim(value, block_at(device, place) * rows, rows, 0)
                for place in range(count // 2)
            ]
        )

    got = swap(blocks(jnp.bitwise_xor(index, 1)), 1)
    held = blocks(index).astype(F32) + got.astype(F32)
    for step in range(len(chip_bits()) - 1, -1, -1):
        held = held.astype(BF16)
        half = held.shape[0] // 2
        got = chip_swap(held[half:], step)
        held = held[:half].astype(F32) + got.astype(F32)
    return held[0]


def row_gather(shard, axis):
    return lax.all_gather(shard, "row", axis=axis, tiled=True)


def after(values, earlier):
    out = lax.optimization_barrier(tuple(values) + tuple(earlier))
    return out[: len(values)]


def row_scatter(value, axis):
    return lax.psum_scatter(value, "row", scatter_dimension=axis, tiled=True)


def small_sum(value):
    for bit in [1] + chip_bits():
        value = value + swap(value, bit)
    count = lax.axis_size("row")
    total = value
    for k in range(1, count):
        total = total + lax.ppermute(value, "row", [(j, (j + k) % count) for j in range(count)])
    return total


def onehot(index, width):
    return (index[:, None] == jnp.arange(width, dtype=jnp.int32)[None, :]).astype(BF16)


def exchange(value, sent_of, slot_of):
    count = lax.axis_size("row")
    sent = row_major(dot(onehot(sent_of, value.shape[0]), value).astype(BF16))
    sent = sent.reshape(count, -1, value.shape[1])
    got = lax.all_to_all(sent, "row", split_axis=0, concat_axis=0, tiled=True)
    got = got.reshape(-1, value.shape[1])
    return row_major(dot(onehot(slot_of, got.shape[0]), got).astype(BF16))


def body(
    tokens,
    cotangent,
    dealing,
    doc_lengths,
    routes,
    gate_weights,
    attn_gain,
    w_query,
    w_latent,
    latent_gain,
    w_expand,
    w_output,
    ffn_gain,
    shared_gate,
    shared_up,
    shared_down,
    expert_gate,
    expert_up,
    expert_down,
):
    group_rows = routes.shape[0]
    row_count = lax.axis_size("row")
    col_count = lax.axis_size("col")
    row_index = lax.axis_index("row")
    col_index = lax.axis_index("col")
    part_rows = group_rows // col_count
    local_count = expert_gate.shape[0]
    capacity = 4 * group_rows * TOPK // (3 * local_count * col_count)

    def my_part(value):
        return lax.dynamic_slice_in_dim(value, col_index * part_rows, part_rows, 0)

    token_ids = jnp.arange(group_rows, dtype=jnp.int32)
    room = max(16, 5 * group_rows // (16 * row_count) * 4)
    lists = dealing.reshape(row_count, group_rows)
    source = lists // group_rows
    place_in = lists - source * group_rows
    from_here = source == row_index
    rank_here = jnp.where(from_here, jnp.cumsum(from_here.astype(jnp.int32), axis=1) - 1, -1)
    my_source = lax.dynamic_index_in_dim(source, row_index, 0, False)
    by_source = my_source[None, :] == jnp.arange(row_count, dtype=jnp.int32)[:, None]
    count_in = jnp.cumsum(by_source.astype(jnp.int32), axis=1)
    my_rank = jnp.sum(jnp.where(by_source, count_in, 0), axis=0) - 1
    all_counts = jnp.sum(
        (source[:, None, :] == jnp.arange(row_count, dtype=jnp.int32)[None, :, None]).astype(
            jnp.int32
        ),
        axis=2,
    )
    rounds = (jnp.max(all_counts) + room - 1) // room

    inverse_group = jnp.arange(row_count, dtype=jnp.int32)[:, None, None]
    here_hit = (place_in[:, :, None] == token_ids[None, None, :]) & from_here[:, :, None]
    rank_of = jnp.sum(jnp.where(here_hit, rank_here[:, :, None], 0), axis=(0, 1))
    group_of = jnp.sum(jnp.where(here_hit, inverse_group, 0), axis=(0, 1))

    def maps(step):
        places = step * room + jnp.arange(room, dtype=jnp.int32)

        def listed(row_of, rank):
            hit = (rank[None, None, :] == places[None, :, None]) & (
                row_of[None, None, :] == jnp.arange(row_count, dtype=jnp.int32)[:, None, None]
            )
            return jnp.sum(jnp.where(hit, token_ids[None, None, :] + 1, 0), axis=2).reshape(-1) - 1

        def slots(row_of, rank):
            inside = (rank >= places[0]) & (rank < places[0] + room)
            return jnp.where(inside, row_of * room + rank - places[0], -1)

        hit = rank_here[:, None, :] == places[None, :, None]
        out_tokens = jnp.sum(jnp.where(hit, place_in[:, None, :] + 1, 0), axis=2).reshape(-1) - 1
        dealt = (my_source, my_rank)
        return out_tokens, slots(*dealt), listed(*dealt), slots(group_of, rank_of)

    out_list, in_slots, back_list, back_slots = maps(0)

    def more_dealt(carry):
        step, total = carry
        out_more, in_more, _, _ = maps(step)
        given = jnp.concatenate([tokens, cotangent], axis=1)
        return step + 1, total + exchange(given, out_more, in_more)

    host = row_index // (row_count // 2)
    expert = col_index * local_count + host

    def chosen(group_routes, group_gates):
        named = group_routes == expert
        named_any = jnp.any(named, axis=1)
        running = jnp.cumsum(named_any.astype(jnp.int32))
        place = jnp.where(named_any, running - 1, -1)
        pick = place[None, :] == jnp.arange(capacity, dtype=jnp.int32)[:, None]
        token_weight = jnp.sum(jnp.where(named, group_gates, 0.0), axis=1)
        return pick.astype(BF16), jnp.sum(jnp.where(pick, token_weight[None, :], 0.0), axis=1)

    pick, weight = chosen(routes, gate_weights)
    mate_pick, mate_weight = chosen(mate(routes), mate(gate_weights))
    document, position = documents(doc_lengths[0], group_rows)

    rows_in, dim = w_query.shape[0], w_query.shape[0] * row_count
    wide = attn_gain.shape[0]
    slice_width = tokens.shape[1]
    more = lax.while_loop(
        lambda carry: carry[0] < rounds,
        more_dealt,
        (jnp.int32(1), jnp.zeros((group_rows, 2 * slice_width), BF16)),
    )[1]
    dealt_x = exchange(tokens, out_list, in_slots) + more[:, :slice_width]
    full_x = cube_gather(dealt_x, 1)

    query_width = w_query.shape[1]
    lat_rows = rows_in // col_count
    w_latent_s = lax.dynamic_slice_in_dim(w_latent, col_index * lat_rows, lat_rows, 0)
    lat_wide = w_latent.shape[1]
    first_s = jnp.concatenate(
        [
            w_query,
            w_latent_s.reshape(-1, query_width),
            jnp.concatenate([attn_gain, ffn_gain, latent_gain]).reshape(-1, query_width),
        ],
        axis=0,
    )
    first_s = jnp.pad(first_s, ((0, -first_s.shape[0] % 16), (0, 0)))
    (first_s,) = after((first_s,), (dealt_x,))
    first_w = row_gather(first_s[None], 0)
    query_w = first_w[:, :rows_in].reshape(dim, query_width)
    lat_end = rows_in + lat_rows * lat_wide // query_width
    latent_w = cube_gather(first_w[:, rows_in:lat_end].reshape(row_count * lat_rows, lat_wide), 0)
    latent_w = latent_w.reshape(col_count, row_count, lat_rows, lat_wide).transpose(1, 0, 2, 3)
    latent_w = latent_w.reshape(dim, lat_wide)
    gains = first_w[:, lat_end:].reshape(row_count, -1)
    gain_one = gains[:, :wide].reshape(-1).astype(F32)
    gain_two = gains[:, wide : 2 * wide].reshape(-1).astype(F32)
    latent_g = gains[:, 2 * wide : 2 * wide + latent_gain.shape[0]].reshape(-1).astype(F32)

    (cotangent_s,) = after((cotangent,), (dealt_x,))
    dealt_dy = exchange(cotangent_s, out_list, in_slots) + more[:, slice_width:]
    both_dy = cube_gather(jnp.concatenate([dealt_dy, mate(dealt_dy)], axis=0), 1)
    full_dy, mate_dy = both_dy[:group_rows], both_dy[group_rows:]

    out_rows = w_output.shape[0]
    rest_s = jnp.concatenate([w_output.reshape(-1, w_expand.shape[1]), w_expand])
    (rest_s,) = after((rest_s,), (dealt_x,))
    rest_w = row_gather(rest_s[None], 0)
    out_count = w_output.size // w_expand.shape[1]
    output_w = rest_w[:, :out_count].reshape(row_count, out_rows, -1)
    output_w = output_w.transpose(1, 0, 2).reshape(out_rows, dim)
    expand_w = rest_w[:, out_count:].reshape(-1, w_expand.shape[1])

    (shared_gu_s,) = after((jnp.concatenate([shared_gate, shared_up], axis=1),), (first_w,))
    shared_gu_w = row_gather(shared_gu_s, 0)
    (shared_d_s,) = after((shared_down,), (rest_w,))
    shared_d_w = row_gather(shared_d_s, 1)

    def of_expert(value, number):
        return lax.dynamic_index_in_dim(value, number, 0, False)

    def both_parts(number):
        return jnp.concatenate([of_expert(expert_gate, number), of_expert(expert_up, number)], 1)

    kept, given = after((both_parts(host), both_parts(1 - host)), (dealt_dy,))
    gate_up_w = expert_gather(kept, given, 0)
    kept, given = after((of_expert(expert_down, host), of_expert(expert_down, 1 - host)), (dealt_dy,))
    down_w = expert_gather(kept, given, 1)

    head_count = query_w.shape[1] // (NOPE + ROPE)
    softmax_scale = (NOPE + ROPE) ** (-0.5)
    block_rows = min(512, group_rows)
    row_number = token_ids
    residual = full_x.astype(F32)
    scale_one = lax.rsqrt(jnp.mean(residual * residual, axis=-1, keepdims=True) + EPSILON)
    normed_one = (residual * scale_one * gain_one).astype(BF16)
    query_raw = dot(normed_one, query_w)
    query_raw = query_raw.reshape(group_rows, head_count, NOPE + ROPE)
    query_heads = jnp.concatenate(
        [query_raw[..., :NOPE], rotate(query_raw[..., NOPE:], position, 1.0)], axis=-1
    ).astype(BF16)
    latent = dot(normed_one, latent_w)
    latent_front = latent[:, :LAT]
    scale_lat = lax.rsqrt(jnp.mean(latent_front * latent_front, axis=-1, keepdims=True) + EPSILON)
    unit_lat = latent_front * scale_lat
    compressed = (unit_lat * latent_g).astype(BF16)
    rope_key = rotate(latent[:, LAT:], position, 1.0).astype(BF16)
    expanded = dot(compressed, expand_w).astype(BF16)
    expanded = expanded.reshape(group_rows, head_count, NOPE + VDIM)
    key_heads = jnp.concatenate(
        [
            expanded[..., :NOPE],
            jnp.broadcast_to(rope_key[:, None, :], (group_rows, head_count, ROPE)),
        ],
        axis=-1,
    )
    value_heads = expanded[..., NOPE:]

    def block_scores(first_row, last_row):
        raw_scores = (
            jnp.einsum(
                "qhd,khd->hqk",
                query_heads[first_row:last_row],
                key_heads[:last_row],
                preferred_element_type=F32,
            )
            * softmax_scale
        )
        allowed = (document[first_row:last_row, None] == document[None, :last_row]) & (
            row_number[first_row:last_row, None] >= row_number[None, :last_row]
        )
        return jnp.where(allowed[None], raw_scores, -1e30)

    mixed_blocks = []
    lse_blocks = []
    for first_row in range(0, group_rows, block_rows):
        last_row = first_row + block_rows
        scores = block_scores(first_row, last_row)
        row_top = jnp.max(scores, axis=-1, keepdims=True)
        exp_scores = jnp.exp(scores - row_top)
        row_total = jnp.sum(exp_scores, axis=-1, keepdims=True)
        probs_low = (exp_scores / row_total).astype(BF16)
        lse_blocks.append(row_top[..., 0] + jnp.log(row_total[..., 0]))
        mixed_blocks.append(
            jnp.einsum(
                "hqk,khd->qhd",
                probs_low,
                value_heads[:last_row],
                preferred_element_type=F32,
            )
        )
    mixed = (
        jnp.concatenate(mixed_blocks, axis=0).reshape(group_rows, head_count * VDIM).astype(BF16)
    )
    attn_part = cube_scatter(dot(mixed, output_w).astype(BF16))
    x_part = my_part(full_x).astype(F32)
    hidden_part = x_part + attn_part
    scale_two = lax.rsqrt(jnp.mean(hidden_part * hidden_part, axis=-1, keepdims=True) + EPSILON)
    unit_two = hidden_part * scale_two
    normed_part = (unit_two * gain_two).astype(BF16)
    mate_part = mate(normed_part)
    normed_two = cube_gather(normed_part, 0)
    (mate_part,) = after((mate_part,), (normed_two,))
    mate_two = cube_gather(mate_part, 0)

    def forward(rows, gate_up_w):
        width = gate_up_w.shape[1] // 2
        gate_up = dot(rows, gate_up_w)
        gate_out, up_out = gate_up[:, :width], gate_up[:, width:]
        act, slope = silu_parts(gate_out)
        hidden = (act * up_out).astype(BF16)
        return hidden, act, up_out * slope

    def backward(grad_hidden, act, up_slope):
        return jnp.concatenate(
            [(grad_hidden * up_slope).astype(BF16), (grad_hidden * act).astype(BF16)], axis=1
        )

    ordered = []

    def queued_sum(value, axis):
        if len(ordered) > 1:
            (value,) = after((value,), (ordered[-2],))
        ordered.append(row_scatter(value.astype(BF16), axis))
        return ordered[-1]

    shared_hidden, shared_act, shared_us = forward(normed_two, shared_gu_w)
    grad_shared_gu = backward(dot_nt(full_dy, shared_d_w), shared_act, shared_us)
    grad_two = dot_nt(grad_shared_gu, shared_gu_w)
    moe_terms = dot(shared_hidden, shared_d_w)
    grad_sgu = queued_sum(dot_tn(normed_two, grad_shared_gu), 0)
    grad_sd = queued_sum(dot_tn(shared_hidden, full_dy), 1)

    rows = jnp.concatenate(
        [dot(pick, normed_two).astype(BF16), dot(mate_pick, mate_two).astype(BF16)], axis=0
    )
    grad_result = jnp.concatenate(
        [
            (weight[:, None] * dot(pick, full_dy)).astype(BF16),
            (mate_weight[:, None] * dot(mate_pick, mate_dy)).astype(BF16),
        ],
        axis=0,
    )
    hidden, act, up_slope = forward(rows, gate_up_w)
    grad_gate_up = backward(dot_nt(grad_result, down_w), act, up_slope)
    mate_rows = dot_nt(grad_gate_up[capacity:], gate_up_w).astype(BF16)
    mate_grad = dot_tn(mate_pick, mate_rows).astype(BF16)
    (own_gate_up,) = after((grad_gate_up[:capacity],), (mate_grad,))
    own_rows = dot_nt(own_gate_up, gate_up_w).astype(BF16)
    grad_two = (grad_two + dot_tn(pick, own_rows)).astype(BF16)
    mate_grad = mate(cube_scatter(mate_grad).astype(BF16))
    grad_gu = dot_tn(rows, grad_gate_up).astype(BF16)
    grad_down = dot_tn(hidden, grad_result).astype(BF16)

    grad_two_part = cube_scatter(grad_two) + mate_grad.astype(F32)
    dy_part = my_part(full_dy).astype(F32)
    hidden_back, gain_two_grad = norm_back(grad_two_part, unit_two, scale_two, gain_two)
    grad_hidden_part = dy_part + hidden_back
    grad_attn = cube_gather(grad_hidden_part.astype(BF16), 0)

    (hidden_late,) = after((hidden,), (grad_two,))
    weights = jnp.concatenate([weight, mate_weight])
    result_rows = (weights[:, None] * dot(hidden_late, down_w)).astype(BF16)
    mate_terms = dot_tn(mate_pick, result_rows[capacity:]).astype(BF16)
    moe_terms = (moe_terms + dot_tn(pick, result_rows[:capacity])).astype(BF16)
    mate_terms, moe_terms = after((mate_terms, moe_terms), (grad_attn,))
    mate_terms = mate(cube_scatter(mate_terms).astype(BF16))
    moe_part = cube_scatter(moe_terms) + mate_terms.astype(F32)
    result_part = (hidden_part + moe_part).astype(BF16)
    result_slice = lax.all_to_all(result_part, "col", split_axis=1, concat_axis=0, tiled=True)
    result = exchange(result_slice, back_list, back_slots)

    grad_output_w = queued_sum(dot_tn(mixed, grad_attn), 1)
    grad_mixed = dot_nt(grad_attn, output_w).astype(BF16)
    grad_mixed = grad_mixed.reshape(group_rows, head_count, VDIM)
    grad_query_blocks = []
    grad_keys = jnp.zeros((group_rows, head_count, NOPE + ROPE), F32)
    grad_values = jnp.zeros((group_rows, head_count, VDIM), F32)
    for block_number, first_row in enumerate(range(0, group_rows, block_rows)):
        last_row = first_row + block_rows
        scores = block_scores(first_row, last_row)
        probs_f = jnp.exp(scores - lse_blocks[block_number][..., None])
        probs_low = probs_f.astype(BF16)
        grad_block = grad_mixed[first_row:last_row]
        grad_probs = jnp.einsum(
            "qhd,khd->hqk", grad_block, value_heads[:last_row], preferred_element_type=F32
        )
        row_inner = jnp.sum(probs_f * grad_probs, axis=-1, keepdims=True)
        grad_scores = (probs_f * (grad_probs - row_inner)).astype(BF16)
        grad_values = grad_values.at[:last_row].add(
            jnp.einsum("hqk,qhd->khd", probs_low, grad_block, preferred_element_type=F32)
        )
        grad_query_blocks.append(
            softmax_scale
            * jnp.einsum(
                "hqk,khd->qhd", grad_scores, key_heads[:last_row], preferred_element_type=F32
            )
        )
        grad_keys = grad_keys.at[:last_row].add(
            softmax_scale
            * jnp.einsum(
                "hqk,qhd->khd",
                grad_scores,
                query_heads[first_row:last_row],
                preferred_element_type=F32,
            )
        )
    grad_query = jnp.concatenate(grad_query_blocks, axis=0)
    grad_query_raw = (
        jnp.concatenate(
            [grad_query[..., :NOPE], rotate(grad_query[..., NOPE:], position, -1.0)], axis=-1
        )
        .astype(BF16)
        .reshape(group_rows, head_count * (NOPE + ROPE))
    )
    own_gu, mate_gu = expert_scatter(grad_gu, 0)
    own_down, mate_down = expert_scatter(grad_down, 1)
    grad_query_raw, mate_gu = after((grad_query_raw, mate_gu), ())
    grad_one = cube_scatter(dot_nt(grad_query_raw, query_w).astype(BF16))
    grad_expanded = jnp.concatenate([grad_keys[..., :NOPE], grad_values], axis=-1).astype(BF16)
    grad_expanded = grad_expanded.reshape(group_rows, head_count * (NOPE + VDIM))
    grad_compressed = dot_nt(grad_expanded, expand_w)
    grad_rope_key = rotate(jnp.sum(grad_keys[..., NOPE:], axis=1), position, -1.0)
    grad_latent_part = cube_scatter(
        jnp.concatenate([grad_compressed, grad_rope_key], axis=1).astype(BF16)
    )
    grad_front, latent_gain_grad = norm_back(
        grad_latent_part[:, :LAT], my_part(unit_lat), my_part(scale_lat), latent_g
    )
    grad_latent_part = jnp.concatenate([grad_front, grad_latent_part[:, LAT:]], axis=1).astype(BF16)
    latent_term = dot_nt(grad_latent_part, latent_w)
    grad_one = grad_one + latent_term
    scale_one_part = my_part(scale_one)
    input_back, gain_one_grad = norm_back(
        grad_one, x_part * scale_one_part, scale_one_part, gain_one
    )
    grad_input = (grad_hidden_part + input_back).astype(BF16)
    grad_slice = lax.all_to_all(grad_input, "col", split_axis=1, concat_axis=0, tiled=True)
    tokens_grad = exchange(grad_slice, back_list, back_slots)

    def more_back(carry):
        step, total = carry
        _, _, back_more, slots_more = maps(step)
        dealt = jnp.concatenate([result_slice, grad_slice], axis=1)
        return step + 1, total + exchange(dealt, back_more, slots_more)

    more = lax.while_loop(
        lambda carry: carry[0] < rounds,
        more_back,
        (jnp.int32(1), jnp.concatenate([result, tokens_grad], axis=1)),
    )[1]
    result, tokens_grad = more[:, :slice_width], more[:, slice_width:]

    grad_expand_w = queued_sum(dot_tn(compressed, grad_expanded), 0)
    grad_query_w = queued_sum(dot_tn(normed_one, grad_query_raw), 0)
    grad_latent = cube_gather(grad_latent_part, 0)
    my_columns = lax.dynamic_index_in_dim(
        normed_one.reshape(group_rows, row_count, col_count, lat_rows), col_index, 2, False
    ).reshape(group_rows, row_count * lat_rows)
    grad_latent_w = cube_gather(queued_sum(dot_tn(my_columns, grad_latent), 0), 0)
    gain_grads = small_sum(jnp.concatenate([gain_one_grad, gain_two_grad, latent_gain_grad]))
    width_ff = expert_gate.shape[2]
    other_gu, other_down = mate(mate_gu), mate(mate_down)

    def in_order(own, other):
        return jnp.stack([jnp.where(host == 0, own, other), jnp.where(host == 0, other, own)])

    width_two = gain_one_grad.shape[0]
    width_lat = latent_gain_grad.shape[0]

    def my_rows(value):
        width = value.shape[0] // row_count
        return lax.dynamic_slice_in_dim(value, row_index * width, width, 0)

    return (
        result,
        tokens_grad,
        my_rows(gain_grads[:width_two]),
        grad_query_w.astype(F32),
        grad_latent_w.astype(F32),
        my_rows(gain_grads[2 * width_two : 2 * width_two + width_lat]),
        grad_expand_w.astype(F32),
        grad_output_w.astype(F32),
        my_rows(gain_grads[width_two : 2 * width_two]),
        grad_sgu[:, : shared_gate.shape[1]].astype(F32),
        grad_sgu[:, shared_gate.shape[1] :].astype(F32),
        grad_sd.astype(F32),
        in_order(own_gu[:, :width_ff], other_gu[:, :width_ff]).astype(F32),
        in_order(own_gu[:, width_ff:], other_gu[:, width_ff:]).astype(F32),
        in_order(own_down, other_down).astype(F32),
    )


def solution(mesh):
    return jax.shard_map(
        body,
        mesh=mesh,
        in_specs=(
            P("row", "col"),
            P("row", "col"),
            P(),
            P("row", None),
            P("row", None),
            P("row", None),
            P("row"),
            P("row", "col"),
            P("row", None),
            P("row"),
            P("row", "col"),
            P("col", "row"),
            P("row"),
            P("row", "col"),
            P("row", "col"),
            P("col", "row"),
            P("col", "row", None),
            P("col", "row", None),
            P("col", None, "row"),
        ),
        out_specs=(
            P("row", "col"),
            P("row", "col"),
            P("row"),
            P("row", "col"),
            P("row", None),
            P("row"),
            P("row", "col"),
            P("col", "row"),
            P("row"),
            P("row", "col"),
            P("row", "col"),
            P("col", "row"),
            P("col", "row", None),
            P("col", "row", None),
            P("col", None, "row"),
        ),
        check_vma=False,
    )
```

```python
import jax
import jax.numpy as jnp
from jax import lax
from jax.experimental.layout import Layout, with_layout_constraint
from jax.sharding import PartitionSpec as P

NOPE = 128
ROPE = 64
VDIM = 128
LAT = 512
TOPK = 6

EPSILON = 1e-06
F32 = jnp.float32
BF16 = jnp.bfloat16


def rotate(value, position, orient):
    half_width = value.shape[-1] // 2
    frequency = 10000.0 ** (-jnp.arange(half_width, dtype=F32) / half_width)
    angles = position.astype(F32)[:, None] * frequency[None, :]
    shape_out = (value.shape[0],) + (1,) * (value.ndim - 2) + (half_width,)
    cosine = jnp.cos(angles).reshape(shape_out)
    sine_part = jnp.sin(angles).reshape(shape_out)
    first_half = value[..., :half_width]
    second = value[..., half_width:]
    return jnp.concatenate(
        [
            first_half * cosine - orient * second * sine_part,
            second * cosine + orient * first_half * sine_part,
        ],
        axis=-1,
    )


def documents(lengths_row, row_count):
    doc_ends = jnp.cumsum(lengths_row)
    starts = doc_ends - lengths_row
    row_number = jnp.arange(row_count, dtype=jnp.int32)
    document = jnp.sum((row_number[:, None] >= doc_ends[None, :]).astype(jnp.int32), axis=1)
    onehot = document[:, None] == jnp.arange(lengths_row.shape[0], dtype=jnp.int32)[None, :]
    position = row_number - jnp.sum(jnp.where(onehot, starts[None, :], 0), axis=1)
    return (document, position)


def silu_parts(value):
    sigmoid_value = jax.nn.sigmoid(value)
    activation = value * sigmoid_value
    activ_slope = sigmoid_value * (1.0 + value * (1.0 - sigmoid_value))
    return (activation, activ_slope)


def norm_back(grad_normed, unit_rows, row_scale, gain_vector):
    scaled = grad_normed * gain_vector
    row_inner = jnp.mean(scaled * unit_rows, axis=-1, keepdims=True)
    return (row_scale * (scaled - unit_rows * row_inner), jnp.sum(grad_normed * unit_rows, axis=0))


def dot(left, right):
    return jnp.dot(left, right, preferred_element_type=F32)


def dot_nt(left, right):
    return lax.dot_general(left, right, (((1,), (1,)), ((), ())), preferred_element_type=F32)


def dot_tn(left, right):
    return lax.dot_general(left, right, (((0,), (0,)), ((), ())), preferred_element_type=F32)


def row_major(value):
    return with_layout_constraint(value, Layout(tuple(range(value.ndim))))


def row_swap(value, bit):
    return lax.ppermute(value, "row", [(j, j ^ bit) for j in range(lax.axis_size("row"))])


def mate(value):
    return row_swap(value, lax.axis_size("row") // 2)


def half_bits():
    return [1 << b for b in range((lax.axis_size("row") // 2).bit_length() - 1)]


def expert_gather(kept, given, axis, hold):
    count = lax.axis_size("row")
    index = lax.axis_index("row")
    width = kept.shape[axis]
    shape = list(kept.shape)
    shape[axis] = width * count
    out = jnp.zeros(shape, kept.dtype)
    (arrived,) = after((mate(given),), hold)
    for first, item in ((count // 2, arrived), (0, kept)):
        items = {first: item}
        for bit in half_bits():
            new = after([row_swap(items[key], bit) for key in items], hold)
            items.update({key ^ bit: piece for key, piece in zip(list(items), new)})
        for key, piece in items.items():
            out = lax.dynamic_update_slice_in_dim(
                out, piece, jnp.bitwise_xor(index, key) * width, axis
            )
    return out


def expert_scatter(value, axis, holds):
    count = lax.axis_size("row")
    index = lax.axis_index("row")
    width = value.shape[axis] // count
    sums = []
    for first, hold in zip((count // 2, 0), holds):
        items = {
            key: lax.dynamic_slice_in_dim(
                value, jnp.bitwise_xor(index, key ^ first) * width, width, axis
            )
            for key in range(count // 2)
        }
        for bit in half_bits()[::-1]:
            keys = [key for key in items if key < bit]
            new = after([row_swap(items[key ^ bit], bit) for key in keys], hold)
            items = {
                key: (items[key].astype(F32) + piece.astype(F32)).astype(BF16)
                for key, piece in zip(keys, new)
            }
        sums.append(items[0])
    return sums[1], sums[0]


def swap(value, bit):
    return lax.ppermute(value, "col", [(j, j ^ bit) for j in range(lax.axis_size("col"))])


def chip_bits():
    return [1 << b for b in range(1, (lax.axis_size("col") - 1).bit_length())]


def chip_swap(value, step):
    bits = chip_bits()
    other = bits[::-1]
    return lax.ppermute(
        value,
        "col",
        [(j, j ^ (other if j % 2 else bits)[step]) for j in range(lax.axis_size("col"))],
    )


def block_at(device, place):
    bits = chip_bits()
    even = sum(bit for n, bit in enumerate(bits) if place >> n & 1)
    odd = sum(bit for n, bit in enumerate(bits[::-1]) if place >> n & 1)
    return jnp.bitwise_xor(device, jnp.where(device % 2 == 0, even, odd))


def cube_gather(block, axis):
    count = lax.axis_size("col")
    index = lax.axis_index("col")
    width = block.shape[axis]
    shape = list(block.shape)
    shape[axis] = width * count
    out = jnp.zeros(shape, block.dtype)
    held = row_major(block)[None]
    sibling = jnp.bitwise_xor(index, 1)
    done = 0
    for step in range(len(chip_bits()) + 1):
        theirs = swap(held[done:], 1)
        for place in range(done, held.shape[0]):
            for item, owner in ((held[place], index), (theirs[place - done], sibling)):
                out = lax.dynamic_update_slice_in_dim(
                    out, item, block_at(owner, place) * width, axis
                )
        done = held.shape[0]
        if step < len(chip_bits()):
            held = jnp.concatenate([held, chip_swap(held, step)], axis=0)
    return out


def cube_scatter(value):
    count = lax.axis_size("col")
    index = lax.axis_index("col")
    rows = value.shape[0] // count
    value = row_major(value)

    def blocks(device):
        return jnp.stack(
            [
                lax.dynamic_slice_in_dim(value, block_at(device, place) * rows, rows, 0)
                for place in range(count // 2)
            ]
        )

    got = swap(blocks(jnp.bitwise_xor(index, 1)), 1)
    held = blocks(index).astype(F32) + got.astype(F32)
    for step in range(len(chip_bits()) - 1, -1, -1):
        held = held.astype(BF16)
        half = held.shape[0] // 2
        got = chip_swap(held[half:], step)
        held = held[:half].astype(F32) + got.astype(F32)
    return held[0]


def row_gather(shard, axis):
    return lax.all_gather(shard, "row", axis=axis, tiled=True)


def after(values, earlier):
    out = lax.optimization_barrier(tuple(values) + tuple(earlier))
    return out[: len(values)]


def row_scatter(value, axis):
    return lax.psum_scatter(value, "row", scatter_dimension=axis, tiled=True)


def small_sum(value):
    for bit in [1] + chip_bits():
        value = value + swap(value, bit)
    count = lax.axis_size("row")
    total = value
    for k in range(1, count):
        total = total + lax.ppermute(value, "row", [(j, (j + k) % count) for j in range(count)])
    return total


def onehot(index, width):
    return (index[:, None] == jnp.arange(width, dtype=jnp.int32)[None, :]).astype(BF16)


def exchange(value, sent_of, slot_of, hold=()):
    count = lax.axis_size("row")
    sent = row_major(dot(onehot(sent_of, value.shape[0]), value).astype(BF16))
    sent = sent.reshape(count, -1, value.shape[1])
    got = lax.all_to_all(sent, "row", split_axis=0, concat_axis=0, tiled=True)
    (got,) = after((got.reshape(-1, value.shape[1]),), hold)
    return row_major(dot(onehot(slot_of, got.shape[0]), got).astype(BF16))


def body(
    tokens,
    cotangent,
    dealing,
    doc_lengths,
    routes,
    gate_weights,
    attn_gain,
    w_query,
    w_latent,
    latent_gain,
    w_expand,
    w_output,
    ffn_gain,
    shared_gate,
    shared_up,
    shared_down,
    expert_gate,
    expert_up,
    expert_down,
):
    group_rows = routes.shape[0]
    row_count = lax.axis_size("row")
    col_count = lax.axis_size("col")
    row_index = lax.axis_index("row")
    col_index = lax.axis_index("col")
    part_rows = group_rows // col_count
    local_count = expert_gate.shape[0]
    capacity = 4 * group_rows * TOPK // (3 * local_count * col_count)

    def my_part(value):
        return lax.dynamic_slice_in_dim(value, col_index * part_rows, part_rows, 0)

    token_ids = jnp.arange(group_rows, dtype=jnp.int32)
    room = max(16, 5 * group_rows // (16 * row_count) * 4)
    lists = dealing.reshape(row_count, group_rows)
    source = lists // group_rows
    place_in = lists - source * group_rows
    from_here = source == row_index
    rank_here = jnp.where(from_here, jnp.cumsum(from_here.astype(jnp.int32), axis=1) - 1, -1)
    my_source = lax.dynamic_index_in_dim(source, row_index, 0, False)
    by_source = my_source[None, :] == jnp.arange(row_count, dtype=jnp.int32)[:, None]
    count_in = jnp.cumsum(by_source.astype(jnp.int32), axis=1)
    my_rank = jnp.sum(jnp.where(by_source, count_in, 0), axis=0) - 1
    all_counts = jnp.sum(
        (source[:, None, :] == jnp.arange(row_count, dtype=jnp.int32)[None, :, None]).astype(
            jnp.int32
        ),
        axis=2,
    )
    rounds = (jnp.max(all_counts) + room - 1) // room

    def maps_out(step):
        places = step * room + jnp.arange(room, dtype=jnp.int32)
        hit = rank_here[:, None, :] == places[None, :, None]
        listed = jnp.sum(jnp.where(hit, place_in[:, None, :] + 1, 0), axis=2).reshape(-1) - 1
        slot = my_rank - step * room
        inside = (slot >= 0) & (slot < room)
        return listed, jnp.where(inside, my_source * room + slot, -1)

    out_list, in_slots = maps_out(0)

    def more_dealt(carry):
        step, total = carry
        out_more, in_more = maps_out(step)
        given = jnp.concatenate([tokens, cotangent], axis=1)
        return step + 1, total + exchange(given, out_more, in_more)

    host = row_index // (row_count // 2)
    expert = col_index * local_count + host

    def chosen(group_routes, group_gates):
        named = group_routes == expert
        named_any = jnp.any(named, axis=1)
        running = jnp.cumsum(named_any.astype(jnp.int32))
        place = jnp.where(named_any, running - 1, -1)
        pick = place[None, :] == jnp.arange(capacity, dtype=jnp.int32)[:, None]
        token_weight = jnp.sum(jnp.where(named, group_gates, 0.0), axis=1)
        return pick.astype(BF16), jnp.sum(jnp.where(pick, token_weight[None, :], 0.0), axis=1)

    document, position = documents(doc_lengths[0], group_rows)

    rows_in, dim = w_query.shape[0], w_query.shape[0] * row_count
    wide = attn_gain.shape[0]
    slice_width = tokens.shape[1]
    more = lax.while_loop(
        lambda carry: carry[0] < rounds,
        more_dealt,
        (jnp.int32(1), jnp.zeros((group_rows, 2 * slice_width), BF16)),
    )[1]
    dealt_x = exchange(tokens, out_list, in_slots) + more[:, :slice_width]
    routes_late, gates_late = after((routes, gate_weights), (dealt_x,))
    pick, weight = chosen(routes_late, gates_late)
    mate_pick, mate_weight = chosen(mate(routes_late), mate(gates_late))
    full_x = cube_gather(dealt_x, 1)

    query_width = w_query.shape[1]
    lat_rows = rows_in // col_count
    w_latent_s = lax.dynamic_slice_in_dim(w_latent, col_index * lat_rows, lat_rows, 0)
    lat_wide = w_latent.shape[1]
    first_s = jnp.concatenate(
        [
            w_query,
            w_latent_s.reshape(-1, query_width),
            jnp.concatenate([attn_gain, ffn_gain, latent_gain]).reshape(-1, query_width),
        ],
        axis=0,
    )
    first_s = jnp.pad(first_s, ((0, -first_s.shape[0] % 16), (0, 0)))
    (first_s,) = after((first_s,), (dealt_x,))
    first_w = row_gather(first_s[None], 0)
    query_w = first_w[:, :rows_in].reshape(dim, query_width)
    lat_end = rows_in + lat_rows * lat_wide // query_width
    latent_w = cube_gather(first_w[:, rows_in:lat_end].reshape(row_count * lat_rows, lat_wide), 0)
    latent_w = latent_w.reshape(col_count, row_count, lat_rows, lat_wide).transpose(1, 0, 2, 3)
    latent_w = latent_w.reshape(dim, lat_wide)
    gains = first_w[:, lat_end:].reshape(row_count, -1)
    gain_one = gains[:, :wide].reshape(-1).astype(F32)
    gain_two = gains[:, wide : 2 * wide].reshape(-1).astype(F32)
    latent_g = gains[:, 2 * wide : 2 * wide + latent_gain.shape[0]].reshape(-1).astype(F32)

    out_rows = w_output.shape[0]
    rest_s = jnp.concatenate([w_output.reshape(-1, w_expand.shape[1]), w_expand])
    (rest_s,) = after((rest_s,), (dealt_x,))
    rest_w = row_gather(rest_s[None], 0)
    out_count = w_output.size // w_expand.shape[1]
    output_w = rest_w[:, :out_count].reshape(row_count, out_rows, -1)
    output_w = output_w.transpose(1, 0, 2).reshape(out_rows, dim)
    expand_w = rest_w[:, out_count:].reshape(-1, w_expand.shape[1])

    def of_expert(value, number):
        return lax.dynamic_index_in_dim(value, number, 0, False)

    def both_parts(number):
        return jnp.concatenate([of_expert(expert_gate, number), of_expert(expert_up, number)], 1)

    gate_up_parts = after((both_parts(host), both_parts(1 - host)), (first_w,))
    down_parts = after(
        (of_expert(expert_down, host), of_expert(expert_down, 1 - host)), (first_w, rest_w)
    )

    head_count = query_w.shape[1] // (NOPE + ROPE)
    softmax_scale = (NOPE + ROPE) ** (-0.5)
    block_rows = min(512, group_rows)
    row_number = token_ids
    residual = full_x.astype(F32)
    scale_one = lax.rsqrt(jnp.mean(residual * residual, axis=-1, keepdims=True) + EPSILON)
    normed_one = (residual * scale_one * gain_one).astype(BF16)
    (cotangent_s,) = after((cotangent,), (normed_one,))
    query_raw = dot(normed_one, query_w)
    query_raw = query_raw.reshape(group_rows, head_count, NOPE + ROPE)
    query_heads = jnp.concatenate(
        [query_raw[..., :NOPE], rotate(query_raw[..., NOPE:], position, 1.0)], axis=-1
    ).astype(BF16)
    latent = dot(normed_one, latent_w)
    latent_front = latent[:, :LAT]
    scale_lat = lax.rsqrt(jnp.mean(latent_front * latent_front, axis=-1, keepdims=True) + EPSILON)
    unit_lat = latent_front * scale_lat
    compressed = (unit_lat * latent_g).astype(BF16)
    rope_key = rotate(latent[:, LAT:], position, 1.0).astype(BF16)
    expanded = dot(compressed, expand_w).astype(BF16)
    expanded = expanded.reshape(group_rows, head_count, NOPE + VDIM)
    key_heads = jnp.concatenate(
        [
            expanded[..., :NOPE],
            jnp.broadcast_to(rope_key[:, None, :], (group_rows, head_count, ROPE)),
        ],
        axis=-1,
    )
    value_heads = expanded[..., NOPE:]
    dealt_dy = exchange(cotangent_s, out_list, in_slots, (expanded,)) + more[:, slice_width:]
    full_dy = cube_gather(dealt_dy, 1)

    def block_scores(first_row, last_row):
        raw_scores = (
            jnp.einsum(
                "qhd,khd->hqk",
                query_heads[first_row:last_row],
                key_heads[:last_row],
                preferred_element_type=F32,
            )
            * softmax_scale
        )
        allowed = (document[first_row:last_row, None] == document[None, :last_row]) & (
            row_number[first_row:last_row, None] >= row_number[None, :last_row]
        )
        return jnp.where(allowed[None], raw_scores, -1e30)

    mixed_blocks = []
    lse_blocks = []
    for first_row in range(0, group_rows, block_rows):
        last_row = first_row + block_rows
        scores = block_scores(first_row, last_row)
        row_top = jnp.max(scores, axis=-1, keepdims=True)
        exp_scores = jnp.exp(scores - row_top)
        row_total = jnp.sum(exp_scores, axis=-1, keepdims=True)
        probs_low = (exp_scores / row_total).astype(BF16)
        lse_blocks.append(row_top[..., 0] + jnp.log(row_total[..., 0]))
        mixed_blocks.append(
            jnp.einsum(
                "hqk,khd->qhd",
                probs_low,
                value_heads[:last_row],
                preferred_element_type=F32,
            )
        )
    mixed = (
        jnp.concatenate(mixed_blocks, axis=0).reshape(group_rows, head_count * VDIM).astype(BF16)
    )
    attn_part = cube_scatter(dot(mixed, output_w).astype(BF16))
    x_part = my_part(full_x).astype(F32)
    hidden_part = x_part + attn_part
    scale_two = lax.rsqrt(jnp.mean(hidden_part * hidden_part, axis=-1, keepdims=True) + EPSILON)
    unit_two = hidden_part * scale_two
    normed_part = (unit_two * gain_two).astype(BF16)
    mate_part = mate(normed_part)
    normed_two = cube_gather(normed_part, 0)
    (mate_part,) = after((mate_part,), (normed_two,))
    mate_two = cube_gather(mate_part, 0)
    (dealt_mate_dy,) = after((mate(dealt_dy),), (normed_part,))
    mate_dy = cube_gather(dealt_mate_dy, 1)
    gate_up_w = expert_gather(*gate_up_parts, 0, (normed_part,))
    down_w = expert_gather(*down_parts, 1, (normed_part,))
    shared_gu_s, shared_d_s = after(
        (jnp.concatenate([shared_gate, shared_up], axis=1), shared_down), (normed_part,)
    )
    shared_gu_w = row_gather(shared_gu_s, 0)
    shared_d_w = row_gather(shared_d_s, 1)

    place_late, rank_late, here_late, source_late, my_rank_late = after(
        (place_in, rank_here, from_here, my_source, my_rank), (normed_part,)
    )
    hit = (place_late[:, :, None] == token_ids[None, None, :]) & here_late[:, :, None]
    rank_of = jnp.sum(jnp.where(hit, rank_late[:, :, None], 0), axis=(0, 1))
    groups = jnp.arange(row_count, dtype=jnp.int32)
    group_of = jnp.sum(jnp.where(hit, groups[:, None, None], 0), axis=(0, 1))

    def maps_back(step):
        places = step * room + jnp.arange(room, dtype=jnp.int32)
        hit = (my_rank_late[None, None, :] == places[None, :, None]) & (
            source_late[None, None, :] == groups[:, None, None]
        )
        listed = jnp.sum(jnp.where(hit, token_ids[None, None, :] + 1, 0), axis=2).reshape(-1) - 1
        slot = rank_of - step * room
        inside = (slot >= 0) & (slot < room)
        return listed, jnp.where(inside, group_of * room + slot, -1)

    back_list, back_slots = maps_back(0)
    gate_up_w, back_list, back_slots = after((gate_up_w, back_list, back_slots), ())

    def forward(rows, gate_up_w):
        width = gate_up_w.shape[1] // 2
        gate_up = dot(rows, gate_up_w)
        gate_out, up_out = gate_up[:, :width], gate_up[:, width:]
        act, slope = silu_parts(gate_out)
        hidden = (act * up_out).astype(BF16)
        return hidden, act, up_out * slope

    def backward(grad_hidden, act, up_slope):
        return jnp.concatenate(
            [(grad_hidden * up_slope).astype(BF16), (grad_hidden * act).astype(BF16)], axis=1
        )

    def queued_sum(value, axis):
        return row_scatter(value.astype(BF16), axis)

    rows = jnp.concatenate(
        [dot(pick, normed_two).astype(BF16), dot(mate_pick, mate_two).astype(BF16)], axis=0
    )
    grad_result = jnp.concatenate(
        [
            (weight[:, None] * dot(pick, full_dy)).astype(BF16),
            (mate_weight[:, None] * dot(mate_pick, mate_dy)).astype(BF16),
        ],
        axis=0,
    )
    hidden, act, up_slope = forward(rows, gate_up_w)
    grad_gate_up = backward(dot_nt(grad_result, down_w), act, up_slope)
    mate_rows = dot_nt(grad_gate_up[capacity:], gate_up_w).astype(BF16)
    mate_grad = dot_tn(mate_pick, mate_rows).astype(BF16)
    mate_grad_part = mate(cube_scatter(mate_grad).astype(BF16))
    own_gate_up, normed_s, dy_s = after(
        (grad_gate_up[:capacity], normed_two, full_dy), (mate_grad,)
    )
    own_rows = dot_nt(own_gate_up, gate_up_w).astype(BF16)
    shared_hidden, shared_act, shared_us = forward(normed_s, shared_gu_w)
    grad_shared_gu = backward(dot_nt(dy_s, shared_d_w), shared_act, shared_us)
    grad_two = dot_nt(grad_shared_gu, shared_gu_w)
    grad_two = (grad_two + dot_tn(pick, own_rows)).astype(BF16)
    grad_two_part = cube_scatter(grad_two)
    late = after((rows, grad_gate_up, hidden, grad_result), (grad_two,))
    grad_gu = dot_tn(late[0], late[1]).astype(BF16)
    grad_down = dot_tn(late[2], late[3]).astype(BF16)
    late = after((normed_two, grad_shared_gu, shared_hidden, full_dy), (grad_two,))
    grad_sgu = queued_sum(dot_tn(late[0], late[1]), 0)
    grad_sd = queued_sum(dot_tn(late[2], late[3]), 1)

    (mate_grad_part,) = after((mate_grad_part,), (grad_two_part,))
    grad_two_part = grad_two_part + mate_grad_part.astype(F32)
    dy_part = my_part(full_dy).astype(F32)
    hidden_back, gain_two_grad = norm_back(grad_two_part, unit_two, scale_two, gain_two)
    grad_hidden_part = dy_part + hidden_back
    grad_attn = cube_gather(grad_hidden_part.astype(BF16), 0)

    hidden_late, shared_late = after((hidden, shared_hidden), (grad_hidden_part,))
    weights = jnp.concatenate([weight, mate_weight])
    result_rows = (weights[:, None] * dot(hidden_late, down_w)).astype(BF16)
    mate_terms = dot_tn(mate_pick, result_rows[capacity:]).astype(BF16)
    moe_terms = dot(shared_late, shared_d_w) + dot_tn(pick, result_rows[:capacity])
    mate_terms, moe_terms = after((mate_terms, moe_terms.astype(BF16)), (grad_attn,))
    mate_terms = mate(cube_scatter(mate_terms).astype(BF16))
    moe_part = cube_scatter(moe_terms)

    grad_output_w = queued_sum(dot_tn(mixed, grad_attn), 1)
    grad_mixed = dot_nt(grad_attn, output_w).astype(BF16)
    grad_mixed = grad_mixed.reshape(group_rows, head_count, VDIM)
    grad_query_blocks = []
    grad_keys = jnp.zeros((group_rows, head_count, NOPE + ROPE), F32)
    grad_values = jnp.zeros((group_rows, head_count, VDIM), F32)
    for block_number, first_row in enumerate(range(0, group_rows, block_rows)):
        last_row = first_row + block_rows
        scores = block_scores(first_row, last_row)
        probs_f = jnp.exp(scores - lse_blocks[block_number][..., None])
        probs_low = probs_f.astype(BF16)
        grad_block = grad_mixed[first_row:last_row]
        grad_probs = jnp.einsum(
            "qhd,khd->hqk", grad_block, value_heads[:last_row], preferred_element_type=F32
        )
        row_inner = jnp.sum(probs_f * grad_probs, axis=-1, keepdims=True)
        grad_scores = (probs_f * (grad_probs - row_inner)).astype(BF16)
        grad_values = grad_values.at[:last_row].add(
            jnp.einsum("hqk,qhd->khd", probs_low, grad_block, preferred_element_type=F32)
        )
        grad_query_blocks.append(
            softmax_scale
            * jnp.einsum(
                "hqk,khd->qhd", grad_scores, key_heads[:last_row], preferred_element_type=F32
            )
        )
        grad_keys = grad_keys.at[:last_row].add(
            softmax_scale
            * jnp.einsum(
                "hqk,qhd->khd",
                grad_scores,
                query_heads[first_row:last_row],
                preferred_element_type=F32,
            )
        )
    grad_query = jnp.concatenate(grad_query_blocks, axis=0)
    grad_query_raw = (
        jnp.concatenate(
            [grad_query[..., :NOPE], rotate(grad_query[..., NOPE:], position, -1.0)], axis=-1
        )
        .astype(BF16)
        .reshape(group_rows, head_count * (NOPE + ROPE))
    )
    grad_one = dot_nt(grad_query_raw, query_w).astype(BF16)

    mate_terms, moe_part = after((mate_terms, moe_part), (grad_one,))
    result_part = (hidden_part + (moe_part + mate_terms.astype(F32))).astype(BF16)
    result_slice = lax.all_to_all(result_part, "col", split_axis=1, concat_axis=0, tiled=True)

    grad_one = cube_scatter(grad_one)
    own_gu, mate_gu = expert_scatter(grad_gu, 0, ((grad_attn,), (grad_one,)))
    own_down, mate_down = expert_scatter(grad_down, 1, ((grad_attn,), (grad_one,)))
    grad_expanded = jnp.concatenate([grad_keys[..., :NOPE], grad_values], axis=-1).astype(BF16)
    grad_expanded = grad_expanded.reshape(group_rows, head_count * (NOPE + VDIM))
    grad_compressed = dot_nt(grad_expanded, expand_w)
    grad_rope_key = rotate(jnp.sum(grad_keys[..., NOPE:], axis=1), position, -1.0)
    grad_latent_part = cube_scatter(
        jnp.concatenate([grad_compressed, grad_rope_key], axis=1).astype(BF16)
    )
    grad_front, latent_gain_grad = norm_back(
        grad_latent_part[:, :LAT], my_part(unit_lat), my_part(scale_lat), latent_g
    )
    grad_latent_part = jnp.concatenate([grad_front, grad_latent_part[:, LAT:]], axis=1).astype(BF16)
    latent_term = dot_nt(grad_latent_part, latent_w)
    grad_one = grad_one + latent_term
    scale_one_part = my_part(scale_one)
    input_back, gain_one_grad = norm_back(
        grad_one, x_part * scale_one_part, scale_one_part, gain_one
    )
    grad_input = (grad_hidden_part + input_back).astype(BF16)
    grad_slice = lax.all_to_all(grad_input, "col", split_axis=1, concat_axis=0, tiled=True)
    result = exchange(result_slice, back_list, back_slots, (grad_input,))
    tokens_grad = exchange(grad_slice, back_list, back_slots)

    def more_back(carry):
        step, total = carry
        back_more, slots_more = maps_back(step)
        dealt = jnp.concatenate([result_slice, grad_slice], axis=1)
        return step + 1, total + exchange(dealt, back_more, slots_more)

    more = lax.while_loop(
        lambda carry: carry[0] < rounds,
        more_back,
        (jnp.int32(1), jnp.concatenate([result, tokens_grad], axis=1)),
    )[1]
    result, tokens_grad = more[:, :slice_width], more[:, slice_width:]

    grad_expand_w = queued_sum(dot_tn(compressed, grad_expanded), 0)
    grad_query_w = queued_sum(dot_tn(normed_one, grad_query_raw), 0)
    grad_latent = cube_gather(grad_latent_part, 0)
    my_columns = lax.dynamic_index_in_dim(
        normed_one.reshape(group_rows, row_count, col_count, lat_rows), col_index, 2, False
    ).reshape(group_rows, row_count * lat_rows)
    grad_latent_w = cube_gather(queued_sum(dot_tn(my_columns, grad_latent), 0), 0)
    gain_grads = small_sum(jnp.concatenate([gain_one_grad, gain_two_grad, latent_gain_grad]))
    width_ff = expert_gate.shape[2]
    other_gu, other_down = after((mate(mate_gu), mate(mate_down)), (grad_input,))

    def in_order(own, other):
        return jnp.stack([jnp.where(host == 0, own, other), jnp.where(host == 0, other, own)])

    width_two = gain_one_grad.shape[0]
    width_lat = latent_gain_grad.shape[0]

    def my_rows(value):
        width = value.shape[0] // row_count
        return lax.dynamic_slice_in_dim(value, row_index * width, width, 0)

    return (
        result,
        tokens_grad,
        my_rows(gain_grads[:width_two]),
        grad_query_w.astype(F32),
        grad_latent_w.astype(F32),
        my_rows(gain_grads[2 * width_two : 2 * width_two + width_lat]),
        grad_expand_w.astype(F32),
        grad_output_w.astype(F32),
        my_rows(gain_grads[width_two : 2 * width_two]),
        grad_sgu[:, : shared_gate.shape[1]].astype(F32),
        grad_sgu[:, shared_gate.shape[1] :].astype(F32),
        grad_sd.astype(F32),
        in_order(own_gu[:, :width_ff], other_gu[:, :width_ff]).astype(F32),
        in_order(own_gu[:, width_ff:], other_gu[:, width_ff:]).astype(F32),
        in_order(own_down, other_down).astype(F32),
    )


def solution(mesh):
    return jax.shard_map(
        body,
        mesh=mesh,
        in_specs=(
            P("row", "col"),
            P("row", "col"),
            P(),
            P("row", None),
            P("row", None),
            P("row", None),
            P("row"),
            P("row", "col"),
            P("row", None),
            P("row"),
            P("row", "col"),
            P("col", "row"),
            P("row"),
            P("row", "col"),
            P("row", "col"),
            P("col", "row"),
            P("col", "row", None),
            P("col", "row", None),
            P("col", None, "row"),
        ),
        out_specs=(
            P("row", "col"),
            P("row", "col"),
            P("row"),
            P("row", "col"),
            P("row", None),
            P("row"),
            P("row", "col"),
            P("col", "row"),
            P("row"),
            P("row", "col"),
            P("row", "col"),
            P("col", "row"),
            P("col", "row", None),
            P("col", "row", None),
            P("col", None, "row"),
        ),
        check_vma=False,
    )
```

```python
import jax
import jax.numpy as jnp
from jax import lax
from jax.experimental.layout import Layout, with_layout_constraint
from jax.sharding import PartitionSpec as P

NOPE = 128
ROPE = 64
VDIM = 128
LAT = 512
TOPK = 6

EPSILON = 1e-06
F32 = jnp.float32
BF16 = jnp.bfloat16


def rotate(value, position, orient):
    half_width = value.shape[-1] // 2
    frequency = 10000.0 ** (-jnp.arange(half_width, dtype=F32) / half_width)
    angles = position.astype(F32)[:, None] * frequency[None, :]
    shape_out = (value.shape[0],) + (1,) * (value.ndim - 2) + (half_width,)
    cosine = jnp.cos(angles).reshape(shape_out)
    sine_part = jnp.sin(angles).reshape(shape_out)
    first_half = value[..., :half_width]
    second = value[..., half_width:]
    return jnp.concatenate(
        [
            first_half * cosine - orient * second * sine_part,
            second * cosine + orient * first_half * sine_part,
        ],
        axis=-1,
    )


def documents(lengths_row, row_count):
    doc_ends = jnp.cumsum(lengths_row)
    starts = doc_ends - lengths_row
    row_number = jnp.arange(row_count, dtype=jnp.int32)
    document = jnp.sum((row_number[:, None] >= doc_ends[None, :]).astype(jnp.int32), axis=1)
    onehot = document[:, None] == jnp.arange(lengths_row.shape[0], dtype=jnp.int32)[None, :]
    position = row_number - jnp.sum(jnp.where(onehot, starts[None, :], 0), axis=1)
    return (document, position)


def silu_parts(value):
    sigmoid_value = jax.nn.sigmoid(value)
    activation = value * sigmoid_value
    activ_slope = sigmoid_value * (1.0 + value * (1.0 - sigmoid_value))
    return (activation, activ_slope)


def norm_back(grad_normed, unit_rows, row_scale, gain_vector):
    scaled = grad_normed * gain_vector
    row_inner = jnp.mean(scaled * unit_rows, axis=-1, keepdims=True)
    return (row_scale * (scaled - unit_rows * row_inner), jnp.sum(grad_normed * unit_rows, axis=0))


def dot(left, right):
    return jnp.dot(left, right, preferred_element_type=F32)


def dot_nt(left, right):
    return lax.dot_general(left, right, (((1,), (1,)), ((), ())), preferred_element_type=F32)


def dot_tn(left, right):
    return lax.dot_general(left, right, (((0,), (0,)), ((), ())), preferred_element_type=F32)


def row_major(value):
    return with_layout_constraint(value, Layout(tuple(range(value.ndim))))


def mate(value):
    count = lax.axis_size("row")
    return lax.ppermute(value, "row", [(j, j ^ (count // 2)) for j in range(count)])


def mates():
    half = lax.axis_size("row") // 2
    return [[j, j + half] for j in range(half)]


def halves():
    half = lax.axis_size("row") // 2
    return [list(range(half)), list(range(half, 2 * half))]


def mate_exchange(value):
    return lax.all_to_all(
        value, "row", split_axis=0, concat_axis=0, axis_index_groups=mates(), tiled=True
    )


def half_gather(value, axis):
    return lax.all_gather(value, "row", axis=axis, axis_index_groups=halves())


def half_sum(value, axis):
    return lax.psum_scatter(value, "row", scatter_dimension=axis, axis_index_groups=halves())


def swap(value, bit):
    return lax.ppermute(value, "col", [(j, j ^ bit) for j in range(lax.axis_size("col"))])


def chip_bits():
    return [1 << b for b in range(1, (lax.axis_size("col") - 1).bit_length())]


def chip_swap(value, step):
    bits = chip_bits()
    other = bits[::-1]
    return lax.ppermute(
        value,
        "col",
        [(j, j ^ (other if j % 2 else bits)[step]) for j in range(lax.axis_size("col"))],
    )


def block_at(device, place):
    bits = chip_bits()
    even = sum(bit for n, bit in enumerate(bits) if place >> n & 1)
    odd = sum(bit for n, bit in enumerate(bits[::-1]) if place >> n & 1)
    return jnp.bitwise_xor(device, jnp.where(device % 2 == 0, even, odd))


def cube_gather(block, axis):
    count = lax.axis_size("col")
    index = lax.axis_index("col")
    width = block.shape[axis]
    shape = list(block.shape)
    shape[axis] = width * count
    out = jnp.zeros(shape, block.dtype)
    held = row_major(block)[None]
    sibling = jnp.bitwise_xor(index, 1)
    done = 0
    for step in range(len(chip_bits()) + 1):
        theirs = swap(held[done:], 1)
        for place in range(done, held.shape[0]):
            for item, owner in ((held[place], index), (theirs[place - done], sibling)):
                out = lax.dynamic_update_slice_in_dim(
                    out, item, block_at(owner, place) * width, axis
                )
        done = held.shape[0]
        if step < len(chip_bits()):
            held = jnp.concatenate([held, chip_swap(held, step)], axis=0)
    return out


def cube_scatter(value, axis=0):
    count = lax.axis_size("col")
    index = lax.axis_index("col")
    rows = value.shape[axis] // count
    value = row_major(value)

    def blocks(device):
        return jnp.stack(
            [
                lax.dynamic_slice_in_dim(value, block_at(device, place) * rows, rows, axis)
                for place in range(count // 2)
            ]
        )

    got = swap(blocks(jnp.bitwise_xor(index, 1)), 1)
    held = blocks(index).astype(F32) + got.astype(F32)
    for step in range(len(chip_bits()) - 1, -1, -1):
        held = held.astype(BF16)
        half = held.shape[0] // 2
        got = chip_swap(held[half:], step)
        held = held[:half].astype(F32) + got.astype(F32)
    return held[0]


def row_gather(shard, axis):
    return lax.all_gather(shard, "row", axis=axis, tiled=True)


def after(values, earlier):
    out = lax.optimization_barrier(tuple(values) + tuple(earlier))
    return out[: len(values)]


def row_scatter(value, axis):
    return lax.psum_scatter(value, "row", scatter_dimension=axis, tiled=True)


def small_sum(value):
    for bit in [1] + chip_bits():
        value = value + swap(value, bit)
    count = lax.axis_size("row")
    total = value
    for k in range(1, count):
        total = total + lax.ppermute(value, "row", [(j, (j + k) % count) for j in range(count)])
    return total


def onehot(index, width):
    return (index[:, None] == jnp.arange(width, dtype=jnp.int32)[None, :]).astype(BF16)


def exchange(value, sent_of, slot_of, hold=()):
    count = lax.axis_size("row")
    sent = row_major(dot(onehot(sent_of, value.shape[0]), value).astype(BF16))
    sent = sent.reshape(count, -1, value.shape[1])
    got = lax.all_to_all(sent, "row", split_axis=0, concat_axis=0, tiled=True)
    (got,) = after((got.reshape(-1, value.shape[1]),), hold)
    return row_major(dot(onehot(slot_of, got.shape[0]), got).astype(BF16))


def body(
    tokens,
    cotangent,
    dealing,
    doc_lengths,
    routes,
    gate_weights,
    attn_gain,
    w_query,
    w_latent,
    latent_gain,
    w_expand,
    w_output,
    ffn_gain,
    shared_gate,
    shared_up,
    shared_down,
    expert_gate,
    expert_up,
    expert_down,
):
    group_rows = routes.shape[0]
    row_count = lax.axis_size("row")
    col_count = lax.axis_size("col")
    row_index = lax.axis_index("row")
    col_index = lax.axis_index("col")
    part_rows = group_rows // col_count
    local_count = expert_gate.shape[0]
    capacity = 4 * group_rows * TOPK // (3 * local_count * col_count)

    def my_part(value):
        return lax.dynamic_slice_in_dim(value, col_index * part_rows, part_rows, 0)

    token_ids = jnp.arange(group_rows, dtype=jnp.int32)
    room = max(16, 5 * group_rows // (16 * row_count) * 4)
    lists = dealing.reshape(row_count, group_rows)
    source = lists // group_rows
    place_in = lists - source * group_rows
    from_here = source == row_index
    rank_here = jnp.where(from_here, jnp.cumsum(from_here.astype(jnp.int32), axis=1) - 1, -1)
    my_source = lax.dynamic_index_in_dim(source, row_index, 0, False)
    by_source = my_source[None, :] == jnp.arange(row_count, dtype=jnp.int32)[:, None]
    count_in = jnp.cumsum(by_source.astype(jnp.int32), axis=1)
    my_rank = jnp.sum(jnp.where(by_source, count_in, 0), axis=0) - 1
    all_counts = jnp.sum(
        (source[:, None, :] == jnp.arange(row_count, dtype=jnp.int32)[None, :, None]).astype(
            jnp.int32
        ),
        axis=2,
    )
    rounds = (jnp.max(all_counts) + room - 1) // room

    def maps_out(step):
        places = step * room + jnp.arange(room, dtype=jnp.int32)
        hit = rank_here[:, None, :] == places[None, :, None]
        listed = jnp.sum(jnp.where(hit, place_in[:, None, :] + 1, 0), axis=2).reshape(-1) - 1
        slot = my_rank - step * room
        inside = (slot >= 0) & (slot < room)
        return listed, jnp.where(inside, my_source * room + slot, -1)

    out_list, in_slots = maps_out(0)

    def more_dealt(carry):
        step, total = carry
        out_more, in_more = maps_out(step)
        given = jnp.concatenate([tokens, cotangent], axis=1)
        return step + 1, total + exchange(given, out_more, in_more)

    host = row_index // (row_count // 2)
    expert = col_index * local_count + host

    def chosen(group_routes, group_gates):
        named = group_routes == expert
        named_any = jnp.any(named, axis=1)
        running = jnp.cumsum(named_any.astype(jnp.int32))
        place = jnp.where(named_any, running - 1, -1)
        pick = place[None, :] == jnp.arange(capacity, dtype=jnp.int32)[:, None]
        token_weight = jnp.sum(jnp.where(named, group_gates, 0.0), axis=1)
        return pick.astype(BF16), jnp.sum(jnp.where(pick, token_weight[None, :], 0.0), axis=1)

    document, position = documents(doc_lengths[0], group_rows)

    rows_in, dim = w_query.shape[0], w_query.shape[0] * row_count
    wide = attn_gain.shape[0]
    slice_width = tokens.shape[1]
    more = lax.while_loop(
        lambda carry: carry[0] < rounds,
        more_dealt,
        (jnp.int32(1), jnp.zeros((group_rows, 2 * slice_width), BF16)),
    )[1]
    dealt_x = exchange(tokens, out_list, in_slots) + more[:, :slice_width]
    routes_late, gates_late = after((routes, gate_weights), (dealt_x,))
    pick, weight = chosen(routes_late, gates_late)
    mate_pick, mate_weight = chosen(mate(routes_late), mate(gates_late))
    full_x = cube_gather(dealt_x, 1)

    query_width = w_query.shape[1]
    lat_rows = rows_in // col_count
    w_latent_s = lax.dynamic_slice_in_dim(w_latent, col_index * lat_rows, lat_rows, 0)
    parts = [
        w_query,
        w_latent_s.reshape(-1, query_width),
        jnp.concatenate([w_output, w_expand], axis=0).reshape(-1, query_width),
        jnp.concatenate([attn_gain, ffn_gain, latent_gain]).reshape(-1, query_width),
    ]
    first_s = jnp.concatenate(parts, axis=0)
    first_s = jnp.pad(first_s, ((0, -first_s.shape[0] % 16), (0, 0)))
    (first_s,) = after((first_s,), (dealt_x,))
    first_w = row_gather(first_s[None], 0)
    pieces, start = [], 0
    for part in parts:
        pieces.append(first_w[:, start : start + part.shape[0]])
        start += part.shape[0]
    query_w = pieces[0].reshape(dim, query_width)
    latent_w = cube_gather(pieces[1].reshape(row_count * lat_rows, w_latent.shape[1]), 0)
    latent_w = latent_w.reshape(col_count, row_count, lat_rows, -1).transpose(1, 0, 2, 3)
    latent_w = latent_w.reshape(dim, w_latent.shape[1])
    out_rows, out_width = w_output.shape
    rest_w = pieces[2].reshape(row_count, -1, out_width)
    output_w = rest_w[:, :out_rows].transpose(1, 0, 2).reshape(out_rows, dim)
    expand_w = rest_w[:, out_rows:].reshape(-1, out_width)
    gains = pieces[3].reshape(row_count, -1)
    gain_one = gains[:, :wide].reshape(-1).astype(F32)
    gain_two = gains[:, wide : 2 * wide].reshape(-1).astype(F32)
    latent_g = gains[:, 2 * wide :].reshape(-1).astype(F32)

    (gate_s, up_s, down_s) = after((expert_gate, expert_up, expert_down), (first_w,))
    gate_s, up_s, down_s = mate_exchange(gate_s), mate_exchange(up_s), mate_exchange(down_s)

    head_count = query_w.shape[1] // (NOPE + ROPE)
    softmax_scale = (NOPE + ROPE) ** (-0.5)
    block_rows = min(512, group_rows)
    row_number = token_ids
    residual = full_x.astype(F32)
    scale_one = lax.rsqrt(jnp.mean(residual * residual, axis=-1, keepdims=True) + EPSILON)
    normed_one = (residual * scale_one * gain_one).astype(BF16)
    (cotangent_s,) = after((cotangent,), (normed_one,))
    query_raw = dot(normed_one, query_w)
    query_raw = query_raw.reshape(group_rows, head_count, NOPE + ROPE)
    query_heads = jnp.concatenate(
        [query_raw[..., :NOPE], rotate(query_raw[..., NOPE:], position, 1.0)], axis=-1
    ).astype(BF16)
    latent = dot(normed_one, latent_w)
    latent_front = latent[:, :LAT]
    scale_lat = lax.rsqrt(jnp.mean(latent_front * latent_front, axis=-1, keepdims=True) + EPSILON)
    unit_lat = latent_front * scale_lat
    compressed = (unit_lat * latent_g).astype(BF16)
    rope_key = rotate(latent[:, LAT:], position, 1.0).astype(BF16)
    expanded = dot(compressed, expand_w).astype(BF16)
    expanded = expanded.reshape(group_rows, head_count, NOPE + VDIM)
    key_heads = jnp.concatenate(
        [
            expanded[..., :NOPE],
            jnp.broadcast_to(rope_key[:, None, :], (group_rows, head_count, ROPE)),
        ],
        axis=-1,
    )
    value_heads = expanded[..., NOPE:]
    dealt_dy = exchange(cotangent_s, out_list, in_slots, (expanded,)) + more[:, slice_width:]
    (gate_s,) = after((gate_s,), (query_heads,))
    gate_w = half_gather(gate_s, 1).reshape(dim, -1)

    def block_scores(first_row, last_row):
        raw_scores = (
            jnp.einsum(
                "qhd,khd->hqk",
                query_heads[first_row:last_row],
                key_heads[:last_row],
                preferred_element_type=F32,
            )
            * softmax_scale
        )
        allowed = (document[first_row:last_row, None] == document[None, :last_row]) & (
            row_number[first_row:last_row, None] >= row_number[None, :last_row]
        )
        return jnp.where(allowed[None], raw_scores, -1e30)

    mixed_blocks = []
    lse_blocks = []
    for first_row in range(0, group_rows, block_rows):
        last_row = first_row + block_rows
        scores = block_scores(first_row, last_row)
        row_top = jnp.max(scores, axis=-1, keepdims=True)
        exp_scores = jnp.exp(scores - row_top)
        row_total = jnp.sum(exp_scores, axis=-1, keepdims=True)
        probs_low = (exp_scores / row_total).astype(BF16)
        lse_blocks.append(row_top[..., 0] + jnp.log(row_total[..., 0]))
        mixed_blocks.append(
            jnp.einsum(
                "hqk,khd->qhd",
                probs_low,
                value_heads[:last_row],
                preferred_element_type=F32,
            )
        )
    mixed = (
        jnp.concatenate(mixed_blocks, axis=0).reshape(group_rows, head_count * VDIM).astype(BF16)
    )
    mate_dy = mate(dealt_dy)
    (up_s,) = after((up_s,), (mixed,))
    up_w = half_gather(up_s, 1).reshape(dim, -1)
    attn_part = cube_scatter(dot(mixed, output_w).astype(BF16))
    mate_dy, down_s = after((mate_dy, down_s), (attn_part,))
    both_dy = cube_gather(jnp.stack([dealt_dy, mate_dy]), 2)
    full_dy = both_dy[0]
    down_w = half_gather(down_s.transpose(1, 0, 2), 2).reshape(down_s.shape[1], dim)
    x_part = my_part(full_x).astype(F32)
    hidden_part = x_part + attn_part
    scale_two = lax.rsqrt(jnp.mean(hidden_part * hidden_part, axis=-1, keepdims=True) + EPSILON)
    unit_two = hidden_part * scale_two
    normed_part = (unit_two * gain_two).astype(BF16)
    both_normed = cube_gather(jnp.stack([normed_part, mate(normed_part)]), 1)
    normed_two = both_normed[0]
    shared_g_s, shared_d_s = after(
        (jnp.concatenate([shared_gate, shared_up], axis=1), shared_down), (normed_part,)
    )
    shared_gu_w = row_gather(shared_g_s, 0)
    shared_d_w = row_gather(shared_d_s, 1)

    place_late, rank_late, here_late, source_late, my_rank_late = after(
        (place_in, rank_here, from_here, my_source, my_rank), (normed_part,)
    )
    hit = (place_late[:, :, None] == token_ids[None, None, :]) & here_late[:, :, None]
    rank_of = jnp.sum(jnp.where(hit, rank_late[:, :, None], 0), axis=(0, 1))
    groups = jnp.arange(row_count, dtype=jnp.int32)
    group_of = jnp.sum(jnp.where(hit, groups[:, None, None], 0), axis=(0, 1))

    def maps_back(step):
        places = step * room + jnp.arange(room, dtype=jnp.int32)
        hit = (my_rank_late[None, None, :] == places[None, :, None]) & (
            source_late[None, None, :] == groups[:, None, None]
        )
        listed = jnp.sum(jnp.where(hit, token_ids[None, None, :] + 1, 0), axis=2).reshape(-1) - 1
        slot = rank_of - step * room
        inside = (slot >= 0) & (slot < room)
        return listed, jnp.where(inside, group_of * room + slot, -1)

    back_list, back_slots = maps_back(0)
    gate_w, back_list, back_slots = after((gate_w, back_list, back_slots), ())

    def forward(gate_out, up_out):
        act, slope = silu_parts(gate_out)
        return (act * up_out).astype(BF16), act, up_out * slope

    def backward(grad_hidden, act, up_slope):
        return (grad_hidden * up_slope).astype(BF16), (grad_hidden * act).astype(BF16)

    def picked(values):
        return lax.dot_general(
            both_picks, values, (((2,), (1,)), ((0,), (0,))), preferred_element_type=F32
        )

    both_picks = jnp.stack([pick, mate_pick])
    weights = jnp.concatenate([weight, mate_weight])[:, None]
    rows = picked(both_normed).astype(BF16).reshape(2 * capacity, dim)
    grad_result = (weights * picked(both_dy).reshape(2 * capacity, dim)).astype(BF16)
    hidden, act, up_slope = forward(dot(rows, gate_w), dot(rows, up_w))
    grad_gate, grad_up = backward(dot_nt(grad_result, down_w), act, up_slope)

    def row_grads(gate_part, up_part):
        return (dot_nt(gate_part, gate_w) + dot_nt(up_part, up_w)).astype(BF16)

    mate_rows = row_grads(grad_gate[capacity:], grad_up[capacity:])
    mate_grad = dot_tn(mate_pick, mate_rows).astype(BF16)
    mate_grad_part = mate(cube_scatter(mate_grad).astype(BF16))
    own_gate, own_up, normed_s, dy_s = after(
        (grad_gate[:capacity], grad_up[:capacity], normed_two, full_dy), (mate_grad,)
    )
    own_rows = row_grads(own_gate, own_up)
    shared_width = shared_gate.shape[1]
    shared_out = dot(normed_s, shared_gu_w)
    shared_hidden, shared_act, shared_us = forward(
        shared_out[:, :shared_width], shared_out[:, shared_width:]
    )
    grad_shared_gu = jnp.concatenate(
        backward(dot_nt(dy_s, shared_d_w), shared_act, shared_us), axis=1
    )
    grad_two = dot_nt(grad_shared_gu, shared_gu_w)
    grad_two = (grad_two + dot_tn(pick, own_rows)).astype(BF16)
    grad_two_part = cube_scatter(grad_two)

    def row_sum(value, axis):
        return row_scatter(value.astype(BF16), axis)

    def half_rows(value, axis):
        shape = value.shape[:axis] + (2, row_count // 2, -1) + value.shape[axis + 1 :]
        return half_sum(value.astype(BF16).reshape(shape), axis + 1)

    late_rows, late_result, late_hidden = after((rows, grad_result, hidden), (grad_two,))
    sum_down = half_rows(dot_tn(late_hidden, late_result), 1).transpose(1, 0, 2)
    sum_gate = half_rows(dot_tn(late_rows, grad_gate), 0)
    sum_up = half_rows(dot_tn(late_rows, grad_up), 0)
    late = after((normed_two, grad_shared_gu, shared_hidden, full_dy), (grad_two,))
    grad_sgu = row_sum(dot_tn(late[0], late[1]), 0)
    grad_sd = row_sum(dot_tn(late[2], late[3]), 1)

    (mate_grad_part,) = after((mate_grad_part,), (grad_two_part,))
    grad_two_part = grad_two_part + mate_grad_part.astype(F32)
    dy_part = my_part(full_dy).astype(F32)
    hidden_back, gain_two_grad = norm_back(grad_two_part, unit_two, scale_two, gain_two)
    grad_hidden_part = dy_part + hidden_back
    grad_attn = cube_gather(grad_hidden_part.astype(BF16), 0)

    hidden_late, shared_late = after((hidden, shared_hidden), (grad_hidden_part,))
    result_rows = (weights * dot(hidden_late, down_w)).astype(BF16)
    mate_terms = dot_tn(mate_pick, result_rows[capacity:])
    moe_terms = dot(shared_late, shared_d_w) + dot_tn(pick, result_rows[:capacity])
    (both_terms,) = after((jnp.stack([moe_terms.astype(BF16), mate_terms.astype(BF16)]),), (grad_attn,))
    both_terms = cube_scatter(both_terms, 1)
    moe_part, mate_terms = both_terms[0], mate(both_terms[1].astype(BF16))
    sum_down, sum_gate = after((sum_down, sum_gate), (grad_attn,))
    grad_down, grad_gate = mate_exchange(sum_down), mate_exchange(sum_gate)

    grad_output_w = row_sum(dot_tn(mixed, grad_attn), 1)
    grad_mixed = dot_nt(grad_attn, output_w).astype(BF16)
    grad_mixed = grad_mixed.reshape(group_rows, head_count, VDIM)
    grad_query_blocks = []
    grad_keys = jnp.zeros((group_rows, head_count, NOPE + ROPE), F32)
    grad_values = jnp.zeros((group_rows, head_count, VDIM), F32)
    for block_number, first_row in enumerate(range(0, group_rows, block_rows)):
        last_row = first_row + block_rows
        scores = block_scores(first_row, last_row)
        probs_f = jnp.exp(scores - lse_blocks[block_number][..., None])
        probs_low = probs_f.astype(BF16)
        grad_block = grad_mixed[first_row:last_row]
        grad_probs = jnp.einsum(
            "qhd,khd->hqk", grad_block, value_heads[:last_row], preferred_element_type=F32
        )
        row_inner = jnp.sum(probs_f * grad_probs, axis=-1, keepdims=True)
        grad_scores = (probs_f * (grad_probs - row_inner)).astype(BF16)
        grad_values = grad_values.at[:last_row].add(
            jnp.einsum("hqk,qhd->khd", probs_low, grad_block, preferred_element_type=F32)
        )
        grad_query_blocks.append(
            softmax_scale
            * jnp.einsum(
                "hqk,khd->qhd", grad_scores, key_heads[:last_row], preferred_element_type=F32
            )
        )
        grad_keys = grad_keys.at[:last_row].add(
            softmax_scale
            * jnp.einsum(
                "hqk,qhd->khd",
                grad_scores,
                query_heads[first_row:last_row],
                preferred_element_type=F32,
            )
        )
    grad_query = jnp.concatenate(grad_query_blocks, axis=0)
    grad_query_raw = (
        jnp.concatenate(
            [grad_query[..., :NOPE], rotate(grad_query[..., NOPE:], position, -1.0)], axis=-1
        )
        .astype(BF16)
        .reshape(group_rows, head_count * (NOPE + ROPE))
    )
    grad_one = dot_nt(grad_query_raw, query_w).astype(BF16)

    mate_terms, moe_part = after((mate_terms, moe_part), (grad_one,))
    result_part = (hidden_part + (moe_part + mate_terms.astype(F32))).astype(BF16)
    result_slice = lax.all_to_all(result_part, "col", split_axis=1, concat_axis=0, tiled=True)

    grad_one = cube_scatter(grad_one)
    (sum_up,) = after((sum_up,), (grad_one,))
    grad_up = mate_exchange(sum_up)
    grad_expanded = jnp.concatenate([grad_keys[..., :NOPE], grad_values], axis=-1).astype(BF16)
    grad_expanded = grad_expanded.reshape(group_rows, head_count * (NOPE + VDIM))
    grad_compressed = dot_nt(grad_expanded, expand_w)
    grad_rope_key = rotate(jnp.sum(grad_keys[..., NOPE:], axis=1), position, -1.0)
    grad_latent_part = cube_scatter(
        jnp.concatenate([grad_compressed, grad_rope_key], axis=1).astype(BF16)
    )
    grad_front, latent_gain_grad = norm_back(
        grad_latent_part[:, :LAT], my_part(unit_lat), my_part(scale_lat), latent_g
    )
    grad_latent_part = jnp.concatenate([grad_front, grad_latent_part[:, LAT:]], axis=1).astype(BF16)
    latent_term = dot_nt(grad_latent_part, latent_w)
    grad_one = grad_one + latent_term
    scale_one_part = my_part(scale_one)
    input_back, gain_one_grad = norm_back(
        grad_one, x_part * scale_one_part, scale_one_part, gain_one
    )
    grad_input = (grad_hidden_part + input_back).astype(BF16)
    grad_slice = lax.all_to_all(grad_input, "col", split_axis=1, concat_axis=0, tiled=True)
    result = exchange(result_slice, back_list, back_slots, (grad_input,))
    tokens_grad = exchange(grad_slice, back_list, back_slots)

    def more_back(carry):
        step, total = carry
        back_more, slots_more = maps_back(step)
        dealt = jnp.concatenate([result_slice, grad_slice], axis=1)
        return step + 1, total + exchange(dealt, back_more, slots_more)

    more = lax.while_loop(
        lambda carry: carry[0] < rounds,
        more_back,
        (jnp.int32(1), jnp.concatenate([result, tokens_grad], axis=1)),
    )[1]
    result, tokens_grad = more[:, :slice_width], more[:, slice_width:]

    grad_expand_w = row_sum(dot_tn(compressed, grad_expanded), 0)
    grad_query_w = row_sum(dot_tn(normed_one, grad_query_raw), 0)
    grad_latent = cube_gather(grad_latent_part, 0)
    my_columns = lax.dynamic_index_in_dim(
        normed_one.reshape(group_rows, row_count, col_count, lat_rows), col_index, 2, False
    ).reshape(group_rows, row_count * lat_rows)
    grad_latent_w = cube_gather(row_sum(dot_tn(my_columns, grad_latent), 0), 0)
    gain_grads = small_sum(jnp.concatenate([gain_one_grad, gain_two_grad, latent_gain_grad]))
    width_two = gain_one_grad.shape[0]
    width_lat = latent_gain_grad.shape[0]

    def my_rows(value):
        width = value.shape[0] // row_count
        return lax.dynamic_slice_in_dim(value, row_index * width, width, 0)

    return (
        result,
        tokens_grad,
        my_rows(gain_grads[:width_two]),
        grad_query_w.astype(F32),
        grad_latent_w.astype(F32),
        my_rows(gain_grads[2 * width_two : 2 * width_two + width_lat]),
        grad_expand_w.astype(F32),
        grad_output_w.astype(F32),
        my_rows(gain_grads[width_two : 2 * width_two]),
        grad_sgu[:, : shared_gate.shape[1]].astype(F32),
        grad_sgu[:, shared_gate.shape[1] :].astype(F32),
        grad_sd.astype(F32),
        grad_gate.astype(F32),
        grad_up.astype(F32),
        grad_down.astype(F32),
    )


def solution(mesh):
    return jax.shard_map(
        body,
        mesh=mesh,
        in_specs=(
            P("row", "col"),
            P("row", "col"),
            P(),
            P("row", None),
            P("row", None),
            P("row", None),
            P("row"),
            P("row", "col"),
            P("row", None),
            P("row"),
            P("row", "col"),
            P("col", "row"),
            P("row"),
            P("row", "col"),
            P("row", "col"),
            P("col", "row"),
            P("col", "row", None),
            P("col", "row", None),
            P("col", None, "row"),
        ),
        out_specs=(
            P("row", "col"),
            P("row", "col"),
            P("row"),
            P("row", "col"),
            P("row", None),
            P("row"),
            P("row", "col"),
            P("col", "row"),
            P("row"),
            P("row", "col"),
            P("row", "col"),
            P("col", "row"),
            P("col", "row", None),
            P("col", "row", None),
            P("col", None, "row"),
        ),
        check_vma=False,
    )
```

```python
import jax
import jax.numpy as jnp
from jax import lax
from jax.experimental.layout import Layout, with_layout_constraint
from jax.sharding import PartitionSpec as P

NOPE = 128
ROPE = 64
VDIM = 128
LAT = 512
TOPK = 6

EPSILON = 1e-06
F32 = jnp.float32
BF16 = jnp.bfloat16


def rotate(value, position, orient):
    half_width = value.shape[-1] // 2
    frequency = 10000.0 ** (-jnp.arange(half_width, dtype=F32) / half_width)
    angles = position.astype(F32)[:, None] * frequency[None, :]
    shape_out = (value.shape[0],) + (1,) * (value.ndim - 2) + (half_width,)
    cosine = jnp.cos(angles).reshape(shape_out)
    sine_part = jnp.sin(angles).reshape(shape_out)
    first_half = value[..., :half_width]
    second = value[..., half_width:]
    return jnp.concatenate(
        [
            first_half * cosine - orient * second * sine_part,
            second * cosine + orient * first_half * sine_part,
        ],
        axis=-1,
    )


def documents(lengths_row, row_count):
    doc_ends = jnp.cumsum(lengths_row)
    starts = doc_ends - lengths_row
    row_number = jnp.arange(row_count, dtype=jnp.int32)
    document = jnp.sum((row_number[:, None] >= doc_ends[None, :]).astype(jnp.int32), axis=1)
    onehot = document[:, None] == jnp.arange(lengths_row.shape[0], dtype=jnp.int32)[None, :]
    position = row_number - jnp.sum(jnp.where(onehot, starts[None, :], 0), axis=1)
    return (document, position)


def silu_parts(value):
    sigmoid_value = jax.nn.sigmoid(value)
    activation = value * sigmoid_value
    activ_slope = sigmoid_value * (1.0 + value * (1.0 - sigmoid_value))
    return (activation, activ_slope)


def norm_back(grad_normed, unit_rows, row_scale, gain_vector):
    scaled = grad_normed * gain_vector
    row_inner = jnp.mean(scaled * unit_rows, axis=-1, keepdims=True)
    return (row_scale * (scaled - unit_rows * row_inner), jnp.sum(grad_normed * unit_rows, axis=0))


def dot(left, right):
    return jnp.dot(left, right, preferred_element_type=F32)


def dot_nt(left, right):
    return lax.dot_general(left, right, (((1,), (1,)), ((), ())), preferred_element_type=F32)


def dot_tn(left, right):
    return lax.dot_general(left, right, (((0,), (0,)), ((), ())), preferred_element_type=F32)


def row_major(value):
    return with_layout_constraint(value, Layout(tuple(range(value.ndim))))


def mate(value):
    count = lax.axis_size("row")
    return lax.ppermute(value, "row", [(j, j ^ (count // 2)) for j in range(count)])


def mates():
    half = lax.axis_size("row") // 2
    return [[j, j + half] for j in range(half)]


def halves():
    half = lax.axis_size("row") // 2
    return [list(range(half)), list(range(half, 2 * half))]


def mate_swap(value):
    host = lax.axis_index("row") // (lax.axis_size("row") // 2)
    slot = jnp.arange(2, dtype=jnp.int32).reshape((2,) + (1,) * (value.ndim - 1))
    masked = jnp.where(slot == host, jnp.zeros((), value.dtype), value)
    return lax.psum_scatter(masked, "row", scatter_dimension=0, axis_index_groups=mates())


def in_order(own, other):
    first = lax.axis_index("row") // (lax.axis_size("row") // 2) == 0
    return jnp.stack([jnp.where(first, own, other), jnp.where(first, other, own)])


def own_slot(value):
    host = lax.axis_index("row") // (lax.axis_size("row") // 2)
    return lax.dynamic_index_in_dim(value, host, 0, False)


def half_gather(value, axis):
    return lax.all_gather(value, "row", axis=axis, axis_index_groups=halves())


def half_sum(value, axis):
    return lax.psum_scatter(value, "row", scatter_dimension=axis, axis_index_groups=halves())


def swap(value, bit):
    return lax.ppermute(value, "col", [(j, j ^ bit) for j in range(lax.axis_size("col"))])


def chip_bits():
    return [1 << b for b in range(1, (lax.axis_size("col") - 1).bit_length())]


def chip_swap(value, step):
    bits = chip_bits()
    other = bits[::-1]
    return lax.ppermute(
        value,
        "col",
        [(j, j ^ (other if j % 2 else bits)[step]) for j in range(lax.axis_size("col"))],
    )


def block_at(device, place):
    bits = chip_bits()
    even = sum(bit for n, bit in enumerate(bits) if place >> n & 1)
    odd = sum(bit for n, bit in enumerate(bits[::-1]) if place >> n & 1)
    return jnp.bitwise_xor(device, jnp.where(device % 2 == 0, even, odd))


def cube_gather(block, axis):
    count = lax.axis_size("col")
    index = lax.axis_index("col")
    width = block.shape[axis]
    shape = list(block.shape)
    shape[axis] = width * count
    out = jnp.zeros(shape, block.dtype)
    held = row_major(block)[None]
    sibling = jnp.bitwise_xor(index, 1)
    done = 0
    for step in range(len(chip_bits()) + 1):
        theirs = swap(held[done:], 1)
        for place in range(done, held.shape[0]):
            for item, owner in ((held[place], index), (theirs[place - done], sibling)):
                out = lax.dynamic_update_slice_in_dim(
                    out, item, block_at(owner, place) * width, axis
                )
        done = held.shape[0]
        if step < len(chip_bits()):
            held = jnp.concatenate([held, chip_swap(held, step)], axis=0)
    return out


def cube_scatter(value, axis=0):
    count = lax.axis_size("col")
    index = lax.axis_index("col")
    rows = value.shape[axis] // count
    value = row_major(value)

    def blocks(device):
        return jnp.stack(
            [
                lax.dynamic_slice_in_dim(value, block_at(device, place) * rows, rows, axis)
                for place in range(count // 2)
            ]
        )

    got = swap(blocks(jnp.bitwise_xor(index, 1)), 1)
    held = blocks(index).astype(F32) + got.astype(F32)
    for step in range(len(chip_bits()) - 1, -1, -1):
        held = held.astype(BF16)
        half = held.shape[0] // 2
        got = chip_swap(held[half:], step)
        held = held[:half].astype(F32) + got.astype(F32)
    return held[0]


def row_gather(shard, axis):
    return lax.all_gather(shard, "row", axis=axis, tiled=True)


def after(values, earlier):
    out = lax.optimization_barrier(tuple(values) + tuple(earlier))
    return out[: len(values)]


def row_scatter(value, axis):
    return lax.psum_scatter(value, "row", scatter_dimension=axis, tiled=True)


def small_sum(value):
    for bit in [1] + chip_bits():
        value = value + swap(value, bit)
    count = lax.axis_size("row")
    total = value
    for k in range(1, count):
        total = total + lax.ppermute(value, "row", [(j, (j + k) % count) for j in range(count)])
    return total


def onehot(index, width):
    return (index[:, None] == jnp.arange(width, dtype=jnp.int32)[None, :]).astype(BF16)


def exchange(value, sent_of, slot_of, hold=()):
    count = lax.axis_size("row")
    sent = row_major(dot(onehot(sent_of, value.shape[0]), value).astype(BF16))
    sent = sent.reshape(count, -1, value.shape[1])
    got = lax.all_to_all(sent, "row", split_axis=0, concat_axis=0, tiled=True)
    (got,) = after((got.reshape(-1, value.shape[1]),), hold)
    return row_major(dot(onehot(slot_of, got.shape[0]), got).astype(BF16))


def body(
    tokens,
    cotangent,
    dealing,
    doc_lengths,
    routes,
    gate_weights,
    attn_gain,
    w_query,
    w_latent,
    latent_gain,
    w_expand,
    w_output,
    ffn_gain,
    shared_gate,
    shared_up,
    shared_down,
    expert_gate,
    expert_up,
    expert_down,
):
    group_rows = routes.shape[0]
    row_count = lax.axis_size("row")
    col_count = lax.axis_size("col")
    row_index = lax.axis_index("row")
    col_index = lax.axis_index("col")
    part_rows = group_rows // col_count
    local_count = expert_gate.shape[0]
    capacity = 4 * group_rows * TOPK // (3 * local_count * col_count)

    def my_part(value):
        return lax.dynamic_slice_in_dim(value, col_index * part_rows, part_rows, 0)

    token_ids = jnp.arange(group_rows, dtype=jnp.int32)
    room = max(16, 5 * group_rows // (16 * row_count) * 4)
    lists = dealing.reshape(row_count, group_rows)
    source = lists // group_rows
    place_in = lists - source * group_rows
    from_here = source == row_index
    rank_here = jnp.where(from_here, jnp.cumsum(from_here.astype(jnp.int32), axis=1) - 1, -1)
    my_source = lax.dynamic_index_in_dim(source, row_index, 0, False)
    by_source = my_source[None, :] == jnp.arange(row_count, dtype=jnp.int32)[:, None]
    count_in = jnp.cumsum(by_source.astype(jnp.int32), axis=1)
    my_rank = jnp.sum(jnp.where(by_source, count_in, 0), axis=0) - 1
    all_counts = jnp.sum(
        (source[:, None, :] == jnp.arange(row_count, dtype=jnp.int32)[None, :, None]).astype(
            jnp.int32
        ),
        axis=2,
    )
    rounds = (jnp.max(all_counts) + room - 1) // room

    def maps_out(step):
        places = step * room + jnp.arange(room, dtype=jnp.int32)
        hit = rank_here[:, None, :] == places[None, :, None]
        listed = jnp.sum(jnp.where(hit, place_in[:, None, :] + 1, 0), axis=2).reshape(-1) - 1
        slot = my_rank - step * room
        inside = (slot >= 0) & (slot < room)
        return listed, jnp.where(inside, my_source * room + slot, -1)

    out_list, in_slots = maps_out(0)

    def more_dealt(carry):
        step, total = carry
        out_more, in_more = maps_out(step)
        given = jnp.concatenate([tokens, cotangent], axis=1)
        return step + 1, total + exchange(given, out_more, in_more)

    host = row_index // (row_count // 2)
    expert = col_index * local_count + host

    def chosen(group_routes, group_gates):
        named = group_routes == expert
        named_any = jnp.any(named, axis=1)
        running = jnp.cumsum(named_any.astype(jnp.int32))
        place = jnp.where(named_any, running - 1, -1)
        pick = place[None, :] == jnp.arange(capacity, dtype=jnp.int32)[:, None]
        token_weight = jnp.sum(jnp.where(named, group_gates, 0.0), axis=1)
        return pick.astype(BF16), jnp.sum(jnp.where(pick, token_weight[None, :], 0.0), axis=1)

    document, position = documents(doc_lengths[0], group_rows)

    rows_in, dim = w_query.shape[0], w_query.shape[0] * row_count
    wide = attn_gain.shape[0]
    slice_width = tokens.shape[1]
    more = lax.while_loop(
        lambda carry: carry[0] < rounds,
        more_dealt,
        (jnp.int32(1), jnp.zeros((group_rows, 2 * slice_width), BF16)),
    )[1]
    dealt_x = exchange(tokens, out_list, in_slots) + more[:, :slice_width]
    dealt_x, mate_routes, mate_gates = after((dealt_x, mate(routes), mate(gate_weights)), ())
    routes_late, gates_late = after((routes, gate_weights), (dealt_x,))
    pick, weight = chosen(routes_late, gates_late)
    mate_pick, mate_weight = chosen(mate_routes, mate_gates)
    full_x = cube_gather(dealt_x, 1)

    query_width = w_query.shape[1]
    lat_rows = rows_in // col_count
    w_latent_s = lax.dynamic_slice_in_dim(w_latent, col_index * lat_rows, lat_rows, 0)
    parts = [
        w_query,
        w_latent_s.reshape(-1, query_width),
        jnp.concatenate([w_output, w_expand], axis=0).reshape(-1, query_width),
        jnp.concatenate([attn_gain, ffn_gain, latent_gain]).reshape(-1, query_width),
    ]
    first_s = jnp.concatenate(parts, axis=0)
    first_s = jnp.pad(first_s, ((0, -first_s.shape[0] % 16), (0, 0)))
    (first_s,) = after((first_s,), (dealt_x,))
    first_w = row_gather(first_s[None], 0)
    pieces, start = [], 0
    for part in parts:
        pieces.append(first_w[:, start : start + part.shape[0]])
        start += part.shape[0]
    query_w = pieces[0].reshape(dim, query_width)
    latent_w = cube_gather(pieces[1].reshape(row_count * lat_rows, w_latent.shape[1]), 0)
    latent_w = latent_w.reshape(col_count, row_count, lat_rows, -1).transpose(1, 0, 2, 3)
    latent_w = latent_w.reshape(dim, w_latent.shape[1])
    out_rows, out_width = w_output.shape
    rest_w = pieces[2].reshape(row_count, -1, out_width)
    output_w = rest_w[:, :out_rows].transpose(1, 0, 2).reshape(out_rows, dim)
    expand_w = rest_w[:, out_rows:].reshape(-1, out_width)
    gains = pieces[3].reshape(row_count, -1)
    gain_one = gains[:, :wide].reshape(-1).astype(F32)
    gain_two = gains[:, wide : 2 * wide].reshape(-1).astype(F32)
    latent_g = gains[:, 2 * wide :].reshape(-1).astype(F32)

    (gate_s, up_s, down_s) = after((expert_gate, expert_up, expert_down), (first_w,))
    gate_m, up_m, down_m = mate_swap(gate_s), mate_swap(up_s), mate_swap(down_s)
    gate_s, up_s, down_s = own_slot(gate_s), own_slot(up_s), own_slot(down_s)

    head_count = query_w.shape[1] // (NOPE + ROPE)
    softmax_scale = (NOPE + ROPE) ** (-0.5)
    block_rows = min(512, group_rows)
    row_number = token_ids
    residual = full_x.astype(F32)
    scale_one = lax.rsqrt(jnp.mean(residual * residual, axis=-1, keepdims=True) + EPSILON)
    normed_one = (residual * scale_one * gain_one).astype(BF16)
    (cotangent_s,) = after((cotangent,), (normed_one,))
    query_raw = dot(normed_one, query_w)
    query_raw = query_raw.reshape(group_rows, head_count, NOPE + ROPE)
    query_heads = jnp.concatenate(
        [query_raw[..., :NOPE], rotate(query_raw[..., NOPE:], position, 1.0)], axis=-1
    ).astype(BF16)
    latent = dot(normed_one, latent_w)
    latent_front = latent[:, :LAT]
    scale_lat = lax.rsqrt(jnp.mean(latent_front * latent_front, axis=-1, keepdims=True) + EPSILON)
    unit_lat = latent_front * scale_lat
    compressed = (unit_lat * latent_g).astype(BF16)
    rope_key = rotate(latent[:, LAT:], position, 1.0).astype(BF16)
    expanded = dot(compressed, expand_w).astype(BF16)
    expanded = expanded.reshape(group_rows, head_count, NOPE + VDIM)
    key_heads = jnp.concatenate(
        [
            expanded[..., :NOPE],
            jnp.broadcast_to(rope_key[:, None, :], (group_rows, head_count, ROPE)),
        ],
        axis=-1,
    )
    value_heads = expanded[..., NOPE:]
    dealt_dy = exchange(cotangent_s, out_list, in_slots, (expanded,)) + more[:, slice_width:]

    def block_scores(first_row, last_row):
        raw_scores = (
            jnp.einsum(
                "qhd,khd->hqk",
                query_heads[first_row:last_row],
                key_heads[:last_row],
                preferred_element_type=F32,
            )
            * softmax_scale
        )
        allowed = (document[first_row:last_row, None] == document[None, :last_row]) & (
            row_number[first_row:last_row, None] >= row_number[None, :last_row]
        )
        return jnp.where(allowed[None], raw_scores, -1e30)

    mixed_blocks = []
    lse_blocks = []
    for first_row in range(0, group_rows, block_rows):
        last_row = first_row + block_rows
        scores = block_scores(first_row, last_row)
        row_top = jnp.max(scores, axis=-1, keepdims=True)
        exp_scores = jnp.exp(scores - row_top)
        row_total = jnp.sum(exp_scores, axis=-1, keepdims=True)
        probs_low = (exp_scores / row_total).astype(BF16)
        lse_blocks.append(row_top[..., 0] + jnp.log(row_total[..., 0]))
        mixed_blocks.append(
            jnp.einsum(
                "hqk,khd->qhd",
                probs_low,
                value_heads[:last_row],
                preferred_element_type=F32,
            )
        )
    mixed = (
        jnp.concatenate(mixed_blocks, axis=0).reshape(group_rows, head_count * VDIM).astype(BF16)
    )
    mate_dy = mate(dealt_dy)
    (gate_m,) = after((gate_m,), (mixed,))
    gate_w = half_gather(in_order(gate_s, gate_m), 1).reshape(dim, -1)
    attn_part = cube_scatter(dot(mixed, output_w).astype(BF16))
    mate_dy, up_m = after((mate_dy, up_m), (attn_part,))
    up_w = half_gather(in_order(up_s, up_m), 1).reshape(dim, -1)
    both_dy = cube_gather(jnp.stack([dealt_dy, mate_dy]), 2)
    full_dy = both_dy[0]
    x_part = my_part(full_x).astype(F32)
    hidden_part = x_part + attn_part
    scale_two = lax.rsqrt(jnp.mean(hidden_part * hidden_part, axis=-1, keepdims=True) + EPSILON)
    unit_two = hidden_part * scale_two
    normed_part = (unit_two * gain_two).astype(BF16)
    (down_m,) = after((down_m,), (normed_part,))
    down_w = half_gather(in_order(down_s, down_m), 1)
    down_w = down_w.transpose(2, 0, 1, 3).reshape(down_s.shape[0], dim)
    both_normed = cube_gather(jnp.stack([normed_part, mate(normed_part)]), 1)
    normed_two = both_normed[0]
    shared_g_s, shared_d_s = after(
        (jnp.concatenate([shared_gate, shared_up], axis=1), shared_down), (both_normed,)
    )
    shared_gu_w = row_gather(shared_g_s, 0)
    shared_d_w = row_gather(shared_d_s, 1)

    place_late, rank_late, here_late, source_late, my_rank_late = after(
        (place_in, rank_here, from_here, my_source, my_rank), (normed_part,)
    )
    hit = (place_late[:, :, None] == token_ids[None, None, :]) & here_late[:, :, None]
    rank_of = jnp.sum(jnp.where(hit, rank_late[:, :, None], 0), axis=(0, 1))
    groups = jnp.arange(row_count, dtype=jnp.int32)
    group_of = jnp.sum(jnp.where(hit, groups[:, None, None], 0), axis=(0, 1))

    def maps_back(step):
        places = step * room + jnp.arange(room, dtype=jnp.int32)
        hit = (my_rank_late[None, None, :] == places[None, :, None]) & (
            source_late[None, None, :] == groups[:, None, None]
        )
        listed = jnp.sum(jnp.where(hit, token_ids[None, None, :] + 1, 0), axis=2).reshape(-1) - 1
        slot = rank_of - step * room
        inside = (slot >= 0) & (slot < room)
        return listed, jnp.where(inside, group_of * room + slot, -1)

    back_list, back_slots = maps_back(0)
    gate_w, back_list, back_slots = after((gate_w, back_list, back_slots), ())

    def forward(gate_out, up_out):
        act, slope = silu_parts(gate_out)
        return (act * up_out).astype(BF16), act, up_out * slope

    def backward(grad_hidden, act, up_slope):
        return (grad_hidden * up_slope).astype(BF16), (grad_hidden * act).astype(BF16)

    def picked(values):
        return lax.dot_general(
            both_picks, values, (((2,), (1,)), ((0,), (0,))), preferred_element_type=F32
        )

    both_picks = jnp.stack([pick, mate_pick])
    weights = jnp.concatenate([weight, mate_weight])[:, None]
    rows = picked(both_normed).astype(BF16).reshape(2 * capacity, dim)
    grad_result = (weights * picked(both_dy).reshape(2 * capacity, dim)).astype(BF16)
    hidden, act, up_slope = forward(dot(rows, gate_w), dot(rows, up_w))
    grad_gate, grad_up = backward(dot_nt(grad_result, down_w), act, up_slope)

    def row_grads(gate_part, up_part):
        return (dot_nt(gate_part, gate_w) + dot_nt(up_part, up_w)).astype(BF16)

    mate_rows = row_grads(grad_gate[capacity:], grad_up[capacity:])
    mate_grad = dot_tn(mate_pick, mate_rows).astype(BF16)
    mate_grad_part = mate(cube_scatter(mate_grad).astype(BF16))
    own_gate, own_up, normed_s, dy_s = after(
        (grad_gate[:capacity], grad_up[:capacity], normed_two, full_dy), (mate_grad,)
    )
    own_rows = row_grads(own_gate, own_up)
    shared_width = shared_gate.shape[1]
    shared_out = dot(normed_s, shared_gu_w)
    shared_hidden, shared_act, shared_us = forward(
        shared_out[:, :shared_width], shared_out[:, shared_width:]
    )
    grad_shared_gu = jnp.concatenate(
        backward(dot_nt(dy_s, shared_d_w), shared_act, shared_us), axis=1
    )
    grad_two = dot_nt(grad_shared_gu, shared_gu_w)
    grad_two = (grad_two + dot_tn(pick, own_rows)).astype(BF16)
    grad_two_part = cube_scatter(grad_two)

    def row_sum(value, axis):
        return row_scatter(value.astype(BF16), axis)

    def half_rows(value):
        return half_sum(value.astype(BF16).reshape(2, row_count // 2, -1, value.shape[1]), 1)

    late_rows, late_result, late_hidden = after((rows, grad_result, hidden), (grad_two,))
    sum_down = half_rows(dot_tn(late_result, late_hidden))
    sum_gate = half_rows(dot_tn(late_rows, grad_gate))
    sum_up = half_rows(dot_tn(late_rows, grad_up))
    late = after((normed_two, grad_shared_gu, shared_hidden, full_dy), (grad_two,))
    grad_sgu = row_sum(dot_tn(late[0], late[1]), 0)
    grad_sd = row_sum(dot_tn(late[2], late[3]), 1)

    (mate_grad_part,) = after((mate_grad_part,), (grad_two_part,))
    grad_two_part = grad_two_part + mate_grad_part.astype(F32)
    dy_part = my_part(full_dy).astype(F32)
    hidden_back, gain_two_grad = norm_back(grad_two_part, unit_two, scale_two, gain_two)
    grad_hidden_part = dy_part + hidden_back
    grad_attn = cube_gather(grad_hidden_part.astype(BF16), 0)

    hidden_late, shared_late = after((hidden, shared_hidden), (grad_hidden_part,))
    result_rows = (weights * dot(hidden_late, down_w)).astype(BF16)
    mate_terms = dot_tn(mate_pick, result_rows[capacity:])
    moe_terms = dot(shared_late, shared_d_w) + dot_tn(pick, result_rows[:capacity])
    (both_terms,) = after((jnp.stack([moe_terms.astype(BF16), mate_terms.astype(BF16)]),), (grad_attn,))
    both_terms = cube_scatter(both_terms, 1)
    moe_part, mate_terms = both_terms[0], mate(both_terms[1].astype(BF16))
    sum_down, sum_gate = after((sum_down, sum_gate), (grad_attn,))
    grad_down = in_order(own_slot(sum_down), mate_swap(sum_down)).transpose(0, 2, 1)
    grad_gate = in_order(own_slot(sum_gate), mate_swap(sum_gate))

    grad_output_w = row_sum(dot_tn(mixed, grad_attn), 1)
    grad_mixed = dot_nt(grad_attn, output_w).astype(BF16)
    grad_mixed = grad_mixed.reshape(group_rows, head_count, VDIM)
    grad_query_blocks = []
    grad_keys = jnp.zeros((group_rows, head_count, NOPE + ROPE), F32)
    grad_values = jnp.zeros((group_rows, head_count, VDIM), F32)
    for block_number, first_row in enumerate(range(0, group_rows, block_rows)):
        last_row = first_row + block_rows
        scores = block_scores(first_row, last_row)
        probs_f = jnp.exp(scores - lse_blocks[block_number][..., None])
        probs_low = probs_f.astype(BF16)
        grad_block = grad_mixed[first_row:last_row]
        grad_probs = jnp.einsum(
            "qhd,khd->hqk", grad_block, value_heads[:last_row], preferred_element_type=F32
        )
        row_inner = jnp.sum(probs_f * grad_probs, axis=-1, keepdims=True)
        grad_scores = (probs_f * (grad_probs - row_inner)).astype(BF16)
        grad_values = grad_values.at[:last_row].add(
            jnp.einsum("hqk,qhd->khd", probs_low, grad_block, preferred_element_type=F32)
        )
        grad_query_blocks.append(
            softmax_scale
            * jnp.einsum(
                "hqk,khd->qhd", grad_scores, key_heads[:last_row], preferred_element_type=F32
            )
        )
        grad_keys = grad_keys.at[:last_row].add(
            softmax_scale
            * jnp.einsum(
                "hqk,qhd->khd",
                grad_scores,
                query_heads[first_row:last_row],
                preferred_element_type=F32,
            )
        )
    grad_query = jnp.concatenate(grad_query_blocks, axis=0)
    grad_query_raw = (
        jnp.concatenate(
            [grad_query[..., :NOPE], rotate(grad_query[..., NOPE:], position, -1.0)], axis=-1
        )
        .astype(BF16)
        .reshape(group_rows, head_count * (NOPE + ROPE))
    )
    grad_one = dot_nt(grad_query_raw, query_w).astype(BF16)

    mate_terms, moe_part = after((mate_terms, moe_part), (grad_one,))
    result_part = (hidden_part + (moe_part + mate_terms.astype(F32))).astype(BF16)
    result_slice = lax.all_to_all(result_part, "col", split_axis=1, concat_axis=0, tiled=True)

    grad_one = cube_scatter(grad_one)
    (sum_up,) = after((sum_up,), (grad_one,))
    grad_up = in_order(own_slot(sum_up), mate_swap(sum_up))
    grad_expanded = jnp.concatenate([grad_keys[..., :NOPE], grad_values], axis=-1).astype(BF16)
    grad_expanded = grad_expanded.reshape(group_rows, head_count * (NOPE + VDIM))
    grad_compressed = dot_nt(grad_expanded, expand_w)
    grad_rope_key = rotate(jnp.sum(grad_keys[..., NOPE:], axis=1), position, -1.0)
    grad_latent_part = cube_scatter(
        jnp.concatenate([grad_compressed, grad_rope_key], axis=1).astype(BF16)
    )
    grad_front, latent_gain_grad = norm_back(
        grad_latent_part[:, :LAT], my_part(unit_lat), my_part(scale_lat), latent_g
    )
    grad_latent_part = jnp.concatenate([grad_front, grad_latent_part[:, LAT:]], axis=1).astype(BF16)
    latent_term = dot_nt(grad_latent_part, latent_w)
    grad_one = grad_one + latent_term
    scale_one_part = my_part(scale_one)
    input_back, gain_one_grad = norm_back(
        grad_one, x_part * scale_one_part, scale_one_part, gain_one
    )
    grad_input = (grad_hidden_part + input_back).astype(BF16)
    grad_slice = lax.all_to_all(grad_input, "col", split_axis=1, concat_axis=0, tiled=True)
    result = exchange(result_slice, back_list, back_slots, (grad_input,))
    tokens_grad = exchange(grad_slice, back_list, back_slots)

    def more_back(carry):
        step, total = carry
        back_more, slots_more = maps_back(step)
        dealt = jnp.concatenate([result_slice, grad_slice], axis=1)
        return step + 1, total + exchange(dealt, back_more, slots_more)

    more = lax.while_loop(
        lambda carry: carry[0] < rounds,
        more_back,
        (jnp.int32(1), jnp.concatenate([result, tokens_grad], axis=1)),
    )[1]
    result, tokens_grad = more[:, :slice_width], more[:, slice_width:]

    grad_expand_w = row_sum(dot_tn(compressed, grad_expanded), 0)
    grad_query_w = row_sum(dot_tn(normed_one, grad_query_raw), 0)
    grad_latent = cube_gather(grad_latent_part, 0)
    my_columns = lax.dynamic_index_in_dim(
        normed_one.reshape(group_rows, row_count, col_count, lat_rows), col_index, 2, False
    ).reshape(group_rows, row_count * lat_rows)
    grad_latent_w = cube_gather(row_sum(dot_tn(my_columns, grad_latent), 0), 0)
    gain_grads = small_sum(jnp.concatenate([gain_one_grad, gain_two_grad, latent_gain_grad]))
    width_two = gain_one_grad.shape[0]
    width_lat = latent_gain_grad.shape[0]

    def my_rows(value):
        width = value.shape[0] // row_count
        return lax.dynamic_slice_in_dim(value, row_index * width, width, 0)

    return (
        result,
        tokens_grad,
        my_rows(gain_grads[:width_two]),
        grad_query_w.astype(F32),
        grad_latent_w.astype(F32),
        my_rows(gain_grads[2 * width_two : 2 * width_two + width_lat]),
        grad_expand_w.astype(F32),
        grad_output_w.astype(F32),
        my_rows(gain_grads[width_two : 2 * width_two]),
        grad_sgu[:, : shared_gate.shape[1]].astype(F32),
        grad_sgu[:, shared_gate.shape[1] :].astype(F32),
        grad_sd.astype(F32),
        grad_gate.astype(F32),
        grad_up.astype(F32),
        grad_down.astype(F32),
    )


def solution(mesh):
    return jax.shard_map(
        body,
        mesh=mesh,
        in_specs=(
            P("row", "col"),
            P("row", "col"),
            P(),
            P("row", None),
            P("row", None),
            P("row", None),
            P("row"),
            P("row", "col"),
            P("row", None),
            P("row"),
            P("row", "col"),
            P("col", "row"),
            P("row"),
            P("row", "col"),
            P("row", "col"),
            P("col", "row"),
            P("col", "row", None),
            P("col", "row", None),
            P("col", None, "row"),
        ),
        out_specs=(
            P("row", "col"),
            P("row", "col"),
            P("row"),
            P("row", "col"),
            P("row", None),
            P("row"),
            P("row", "col"),
            P("col", "row"),
            P("row"),
            P("row", "col"),
            P("row", "col"),
            P("col", "row"),
            P("col", "row", None),
            P("col", "row", None),
            P("col", None, "row"),
        ),
        check_vma=False,
    )
```

```python
import jax
import jax.numpy as jnp
from jax import lax
from jax.experimental.layout import Layout, with_layout_constraint
from jax.sharding import PartitionSpec as P

NOPE = 128
ROPE = 64
VDIM = 128
LAT = 512
TOPK = 6

EPSILON = 1e-06
F32 = jnp.float32
BF16 = jnp.bfloat16


def rotate(value, position, orient):
    half_width = value.shape[-1] // 2
    frequency = 10000.0 ** (-jnp.arange(half_width, dtype=F32) / half_width)
    angles = position.astype(F32)[:, None] * frequency[None, :]
    shape_out = (value.shape[0],) + (1,) * (value.ndim - 2) + (half_width,)
    cosine = jnp.cos(angles).reshape(shape_out)
    sine_part = jnp.sin(angles).reshape(shape_out)
    first_half = value[..., :half_width]
    second = value[..., half_width:]
    return jnp.concatenate(
        [
            first_half * cosine - orient * second * sine_part,
            second * cosine + orient * first_half * sine_part,
        ],
        axis=-1,
    )


def documents(lengths_row, row_count):
    doc_ends = jnp.cumsum(lengths_row)
    starts = doc_ends - lengths_row
    row_number = jnp.arange(row_count, dtype=jnp.int32)
    document = jnp.sum((row_number[:, None] >= doc_ends[None, :]).astype(jnp.int32), axis=1)
    onehot = document[:, None] == jnp.arange(lengths_row.shape[0], dtype=jnp.int32)[None, :]
    position = row_number - jnp.sum(jnp.where(onehot, starts[None, :], 0), axis=1)
    return (document, position)


def silu_parts(value):
    sigmoid_value = jax.nn.sigmoid(value)
    activation = value * sigmoid_value
    activ_slope = sigmoid_value * (1.0 + value * (1.0 - sigmoid_value))
    return (activation, activ_slope)


def norm_back(grad_normed, unit_rows, row_scale, gain_vector):
    scaled = grad_normed * gain_vector
    row_inner = jnp.mean(scaled * unit_rows, axis=-1, keepdims=True)
    return (row_scale * (scaled - unit_rows * row_inner), jnp.sum(grad_normed * unit_rows, axis=0))


def dot(left, right):
    return jnp.dot(left, right, preferred_element_type=F32)


def dot_nt(left, right):
    return lax.dot_general(left, right, (((1,), (1,)), ((), ())), preferred_element_type=F32)


def dot_tn(left, right):
    return lax.dot_general(left, right, (((0,), (0,)), ((), ())), preferred_element_type=F32)


def row_major(value):
    return with_layout_constraint(value, Layout(tuple(range(value.ndim))))


def mate(value):
    count = lax.axis_size("row")
    return lax.ppermute(value, "row", [(j, j ^ (count // 2)) for j in range(count)])


def mates():
    half = lax.axis_size("row") // 2
    return [[j, j + half] for j in range(half)]


def halves():
    half = lax.axis_size("row") // 2
    return [list(range(half)), list(range(half, 2 * half))]


def mate_swap(value):
    host = lax.axis_index("row") // (lax.axis_size("row") // 2)
    slot = jnp.arange(2, dtype=jnp.int32).reshape((2,) + (1,) * (value.ndim - 1))
    masked = jnp.where(slot == host, jnp.zeros((), value.dtype), value)
    return lax.psum_scatter(masked, "row", scatter_dimension=0, axis_index_groups=mates())


def in_order(own, other):
    first = lax.axis_index("row") // (lax.axis_size("row") // 2) == 0
    return jnp.stack([jnp.where(first, own, other), jnp.where(first, other, own)])


def own_slot(value):
    host = lax.axis_index("row") // (lax.axis_size("row") // 2)
    return lax.dynamic_index_in_dim(value, host, 0, False)


def half_gather(value, axis):
    return lax.all_gather(value, "row", axis=axis, axis_index_groups=halves())


def half_sum(value, axis):
    return lax.psum_scatter(value, "row", scatter_dimension=axis, axis_index_groups=halves())


def swap(value, bit):
    return lax.ppermute(value, "col", [(j, j ^ bit) for j in range(lax.axis_size("col"))])


def chip_bits():
    return [1 << b for b in range(1, (lax.axis_size("col") - 1).bit_length())]


def chip_swap(value, step):
    bits = chip_bits()
    other = bits[::-1]
    return lax.ppermute(
        value,
        "col",
        [(j, j ^ (other if j % 2 else bits)[step]) for j in range(lax.axis_size("col"))],
    )


def block_at(device, place):
    bits = chip_bits()
    even = sum(bit for n, bit in enumerate(bits) if place >> n & 1)
    odd = sum(bit for n, bit in enumerate(bits[::-1]) if place >> n & 1)
    return jnp.bitwise_xor(device, jnp.where(device % 2 == 0, even, odd))


def cube_gather(block, axis):
    count = lax.axis_size("col")
    index = lax.axis_index("col")
    width = block.shape[axis]
    shape = list(block.shape)
    shape[axis] = width * count
    out = jnp.zeros(shape, block.dtype)
    held = row_major(block)[None]
    sibling = jnp.bitwise_xor(index, 1)
    done = 0
    for step in range(len(chip_bits()) + 1):
        theirs = swap(held[done:], 1)
        for place in range(done, held.shape[0]):
            for item, owner in ((held[place], index), (theirs[place - done], sibling)):
                out = lax.dynamic_update_slice_in_dim(
                    out, item, block_at(owner, place) * width, axis
                )
        done = held.shape[0]
        if step < len(chip_bits()):
            held = jnp.concatenate([held, chip_swap(held, step)], axis=0)
    return out


def scatter_stages(value, axis=0):
    count = lax.axis_size("col")
    index = lax.axis_index("col")
    rows = value.shape[axis] // count
    value = row_major(value)

    def blocks(device):
        return jnp.stack(
            [
                lax.dynamic_slice_in_dim(value, block_at(device, place) * rows, rows, axis)
                for place in range(count // 2)
            ]
        )

    got = swap(blocks(jnp.bitwise_xor(index, 1)), 1)
    held = blocks(index).astype(F32) + got.astype(F32)
    for step in range(len(chip_bits()) - 1, -1, -1):
        held = held.astype(BF16)
        yield held
        half = held.shape[0] // 2
        got = chip_swap(held[half:], step)
        held = held[:half].astype(F32) + got.astype(F32)
    yield held[0]


def cube_scatter(value, axis=0):
    return list(scatter_stages(value, axis))[-1]


def row_gather(shard, axis):
    return lax.all_gather(shard, "row", axis=axis, tiled=True)


def after(values, earlier):
    out = lax.optimization_barrier(tuple(values) + tuple(earlier))
    return out[: len(values)]


def row_scatter(value, axis):
    return lax.psum_scatter(value, "row", scatter_dimension=axis, tiled=True)


def small_sum(value):
    for bit in [1] + chip_bits():
        value = value + swap(value, bit)
    count = lax.axis_size("row")
    total = value
    for k in range(1, count):
        total = total + lax.ppermute(value, "row", [(j, (j + k) % count) for j in range(count)])
    return total


def onehot(index, width):
    return (index[:, None] == jnp.arange(width, dtype=jnp.int32)[None, :]).astype(BF16)


def exchange(value, sent_of, slot_of, hold=()):
    count = lax.axis_size("row")
    sent = row_major(dot(onehot(sent_of, value.shape[0]), value).astype(BF16))
    sent = sent.reshape(count, -1, value.shape[1])
    got = lax.all_to_all(sent, "row", split_axis=0, concat_axis=0, tiled=True)
    (got,) = after((got.reshape(-1, value.shape[1]),), hold)
    return row_major(dot(onehot(slot_of, got.shape[0]), got).astype(BF16))


def body(
    tokens,
    cotangent,
    dealing,
    doc_lengths,
    routes,
    gate_weights,
    attn_gain,
    w_query,
    w_latent,
    latent_gain,
    w_expand,
    w_output,
    ffn_gain,
    shared_gate,
    shared_up,
    shared_down,
    expert_gate,
    expert_up,
    expert_down,
):
    group_rows = routes.shape[0]
    row_count = lax.axis_size("row")
    col_count = lax.axis_size("col")
    row_index = lax.axis_index("row")
    col_index = lax.axis_index("col")
    part_rows = group_rows // col_count
    local_count = expert_gate.shape[0]
    capacity = 4 * group_rows * TOPK // (3 * local_count * col_count)

    def my_part(value):
        return lax.dynamic_slice_in_dim(value, col_index * part_rows, part_rows, 0)

    token_ids = jnp.arange(group_rows, dtype=jnp.int32)
    room = max(16, 5 * group_rows // (16 * row_count) * 4)
    lists = dealing.reshape(row_count, group_rows)
    source = lists // group_rows
    place_in = lists - source * group_rows
    from_here = source == row_index
    rank_here = jnp.where(from_here, jnp.cumsum(from_here.astype(jnp.int32), axis=1) - 1, -1)
    my_source = lax.dynamic_index_in_dim(source, row_index, 0, False)
    by_source = my_source[None, :] == jnp.arange(row_count, dtype=jnp.int32)[:, None]
    count_in = jnp.cumsum(by_source.astype(jnp.int32), axis=1)
    my_rank = jnp.sum(jnp.where(by_source, count_in, 0), axis=0) - 1
    all_counts = jnp.sum(
        (source[:, None, :] == jnp.arange(row_count, dtype=jnp.int32)[None, :, None]).astype(
            jnp.int32
        ),
        axis=2,
    )
    rounds = (jnp.max(all_counts) + room - 1) // room

    def maps_out(step):
        places = step * room + jnp.arange(room, dtype=jnp.int32)
        hit = rank_here[:, None, :] == places[None, :, None]
        listed = jnp.sum(jnp.where(hit, place_in[:, None, :] + 1, 0), axis=2).reshape(-1) - 1
        slot = my_rank - step * room
        inside = (slot >= 0) & (slot < room)
        return listed, jnp.where(inside, my_source * room + slot, -1)

    out_list, in_slots = maps_out(0)

    def more_dealt(carry):
        step, total = carry
        out_more, in_more = maps_out(step)
        given = jnp.concatenate([tokens, cotangent], axis=1)
        return step + 1, total + exchange(given, out_more, in_more)

    host = row_index // (row_count // 2)
    expert = col_index * local_count + host

    def chosen(group_routes, group_gates):
        named = group_routes == expert
        named_any = jnp.any(named, axis=1)
        running = jnp.cumsum(named_any.astype(jnp.int32))
        place = jnp.where(named_any, running - 1, -1)
        pick = place[None, :] == jnp.arange(capacity, dtype=jnp.int32)[:, None]
        token_weight = jnp.sum(jnp.where(named, group_gates, 0.0), axis=1)
        return pick.astype(BF16), jnp.sum(jnp.where(pick, token_weight[None, :], 0.0), axis=1)

    document, position = documents(doc_lengths[0], group_rows)

    rows_in, dim = w_query.shape[0], w_query.shape[0] * row_count
    wide = attn_gain.shape[0]
    slice_width = tokens.shape[1]
    more = lax.while_loop(
        lambda carry: carry[0] < rounds,
        more_dealt,
        (jnp.int32(1), jnp.zeros((group_rows, 2 * slice_width), BF16)),
    )[1]
    dealt_x = exchange(tokens, out_list, in_slots) + more[:, :slice_width]
    dealt_x, mate_routes, mate_gates = after((dealt_x, mate(routes), mate(gate_weights)), ())
    routes_late, gates_late = after((routes, gate_weights), (dealt_x,))
    pick, weight = chosen(routes_late, gates_late)
    mate_pick, mate_weight = chosen(mate_routes, mate_gates)
    full_x = cube_gather(dealt_x, 1)

    query_width = w_query.shape[1]
    lat_rows = rows_in // col_count
    w_latent_s = lax.dynamic_slice_in_dim(w_latent, col_index * lat_rows, lat_rows, 0)
    parts = [
        w_query,
        w_latent_s.reshape(-1, query_width),
        jnp.concatenate([w_output, w_expand], axis=0).reshape(-1, query_width),
        jnp.concatenate([attn_gain, ffn_gain, latent_gain]).reshape(-1, query_width),
    ]
    first_s = jnp.concatenate(parts, axis=0)
    first_s = jnp.pad(first_s, ((0, -first_s.shape[0] % 16), (0, 0)))
    (first_s,) = after((first_s,), (dealt_x,))
    (first_w,) = after((row_gather(first_s[None], 0),), (full_x,))
    pieces, start = [], 0
    for part in parts:
        pieces.append(first_w[:, start : start + part.shape[0]])
        start += part.shape[0]
    query_w = pieces[0].reshape(dim, query_width)
    latent_w = cube_gather(pieces[1].reshape(row_count * lat_rows, w_latent.shape[1]), 0)
    latent_w = latent_w.reshape(col_count, row_count, lat_rows, -1).transpose(1, 0, 2, 3)
    latent_w = latent_w.reshape(dim, w_latent.shape[1])
    out_rows, out_width = w_output.shape
    rest_w = pieces[2].reshape(row_count, -1, out_width)
    output_w = rest_w[:, :out_rows].transpose(1, 0, 2).reshape(out_rows, dim)
    expand_w = rest_w[:, out_rows:].reshape(-1, out_width)
    gains = pieces[3].reshape(row_count, -1)
    gain_one = gains[:, :wide].reshape(-1).astype(F32)
    gain_two = gains[:, wide : 2 * wide].reshape(-1).astype(F32)
    latent_g = gains[:, 2 * wide :].reshape(-1).astype(F32)

    (gate_s, up_s, down_s) = after((expert_gate, expert_up, expert_down), (first_w,))
    gate_m, up_m, down_m = mate_swap(gate_s), mate_swap(up_s), mate_swap(down_s)
    gate_s, up_s, down_s = own_slot(gate_s), own_slot(up_s), own_slot(down_s)

    head_count = query_w.shape[1] // (NOPE + ROPE)
    softmax_scale = (NOPE + ROPE) ** (-0.5)
    block_rows = min(512, group_rows)
    row_number = token_ids
    residual = full_x.astype(F32)
    scale_one = lax.rsqrt(jnp.mean(residual * residual, axis=-1, keepdims=True) + EPSILON)
    normed_one = (residual * scale_one * gain_one).astype(BF16)
    query_raw = dot(normed_one, query_w)
    query_raw = query_raw.reshape(group_rows, head_count, NOPE + ROPE)
    query_heads = jnp.concatenate(
        [query_raw[..., :NOPE], rotate(query_raw[..., NOPE:], position, 1.0)], axis=-1
    ).astype(BF16)
    latent = dot(normed_one, latent_w)
    latent_front = latent[:, :LAT]
    scale_lat = lax.rsqrt(jnp.mean(latent_front * latent_front, axis=-1, keepdims=True) + EPSILON)
    unit_lat = latent_front * scale_lat
    compressed = (unit_lat * latent_g).astype(BF16)
    rope_key = rotate(latent[:, LAT:], position, 1.0).astype(BF16)
    expanded = dot(compressed, expand_w).astype(BF16)
    expanded = expanded.reshape(group_rows, head_count, NOPE + VDIM)
    key_heads = jnp.concatenate(
        [
            expanded[..., :NOPE],
            jnp.broadcast_to(rope_key[:, None, :], (group_rows, head_count, ROPE)),
        ],
        axis=-1,
    )
    value_heads = expanded[..., NOPE:]

    def block_scores(first_row, last_row):
        raw_scores = (
            jnp.einsum(
                "qhd,khd->hqk",
                query_heads[first_row:last_row],
                key_heads[:last_row],
                preferred_element_type=F32,
            )
            * softmax_scale
        )
        allowed = (document[first_row:last_row, None] == document[None, :last_row]) & (
            row_number[first_row:last_row, None] >= row_number[None, :last_row]
        )
        return jnp.where(allowed[None], raw_scores, -1e30)

    mixed_blocks = []
    lse_blocks = []
    for first_row in range(0, group_rows, block_rows):
        last_row = first_row + block_rows
        scores = block_scores(first_row, last_row)
        row_top = jnp.max(scores, axis=-1, keepdims=True)
        exp_scores = jnp.exp(scores - row_top)
        row_total = jnp.sum(exp_scores, axis=-1, keepdims=True)
        probs_low = (exp_scores / row_total).astype(BF16)
        lse_blocks.append(row_top[..., 0] + jnp.log(row_total[..., 0]))
        mixed_blocks.append(
            jnp.einsum(
                "hqk,khd->qhd",
                probs_low,
                value_heads[:last_row],
                preferred_element_type=F32,
            )
        )
    mixed = (
        jnp.concatenate(mixed_blocks, axis=0).reshape(group_rows, head_count * VDIM).astype(BF16)
    )
    (gate_m,) = after((gate_m,), (mixed,))
    gate_w = half_gather(in_order(gate_s, gate_m), 1).reshape(dim, -1)
    attn_terms = dot(mixed, output_w).astype(BF16)
    (cotangent_s,) = after((cotangent,), (attn_terms,))
    attn_part = cube_scatter(attn_terms)
    x_part = my_part(full_x).astype(F32)
    hidden_part = x_part + attn_part
    scale_two = lax.rsqrt(jnp.mean(hidden_part * hidden_part, axis=-1, keepdims=True) + EPSILON)
    unit_two = hidden_part * scale_two
    normed_part = (unit_two * gain_two).astype(BF16)
    mate_normed, up_m = after((mate(normed_part), up_m), (normed_part,))
    up_w = half_gather(in_order(up_s, up_m), 1).reshape(dim, -1)
    (down_m,) = after((down_m,), (mate_normed,))
    down_w = half_gather(in_order(down_s, down_m), 1)
    down_w = down_w.transpose(2, 0, 1, 3).reshape(down_s.shape[0], dim)
    both_normed = cube_gather(jnp.stack([normed_part, mate_normed]), 1)
    normed_two = both_normed[0]
    dealt_dy = exchange(cotangent_s, out_list, in_slots, (mate_normed,)) + more[:, slice_width:]
    (mate_dy,) = after((mate(dealt_dy),), (both_normed,))
    both_dy = cube_gather(jnp.stack([dealt_dy, mate_dy]), 2)
    full_dy = both_dy[0]
    shared_g_s, shared_d_s = after(
        (jnp.concatenate([shared_gate, shared_up], axis=1), shared_down), (mate_normed,)
    )
    shared_gu_w = row_gather(shared_g_s, 0)
    shared_d_w = row_gather(shared_d_s, 1)

    place_late, rank_late, here_late, source_late, my_rank_late = after(
        (place_in, rank_here, from_here, my_source, my_rank), (both_normed,)
    )
    hit = (place_late[:, :, None] == token_ids[None, None, :]) & here_late[:, :, None]
    rank_of = jnp.sum(jnp.where(hit, rank_late[:, :, None], 0), axis=(0, 1))
    groups = jnp.arange(row_count, dtype=jnp.int32)
    group_of = jnp.sum(jnp.where(hit, groups[:, None, None], 0), axis=(0, 1))

    def maps_back(step):
        places = step * room + jnp.arange(room, dtype=jnp.int32)
        hit = (my_rank_late[None, None, :] == places[None, :, None]) & (
            source_late[None, None, :] == groups[:, None, None]
        )
        listed = jnp.sum(jnp.where(hit, token_ids[None, None, :] + 1, 0), axis=2).reshape(-1) - 1
        slot = rank_of - step * room
        inside = (slot >= 0) & (slot < room)
        return listed, jnp.where(inside, group_of * room + slot, -1)

    back_list, back_slots = maps_back(0)
    gate_w, back_list, back_slots = after((gate_w, back_list, back_slots), ())

    def forward(gate_out, up_out):
        act, slope = silu_parts(gate_out)
        return (act * up_out).astype(BF16), act, up_out * slope

    def backward(grad_hidden, act, up_slope):
        return (grad_hidden * up_slope).astype(BF16), (grad_hidden * act).astype(BF16)

    def picked(values):
        return lax.dot_general(
            both_picks, values, (((2,), (1,)), ((0,), (0,))), preferred_element_type=F32
        )

    both_picks = jnp.stack([pick, mate_pick])
    weights = jnp.concatenate([weight, mate_weight])[:, None]
    rows = picked(both_normed).astype(BF16).reshape(2 * capacity, dim)
    grad_result = (weights * picked(both_dy).reshape(2 * capacity, dim)).astype(BF16)
    hidden, act, up_slope = forward(dot(rows, gate_w), dot(rows, up_w))
    grad_gate, grad_up = backward(dot_nt(grad_result, down_w), act, up_slope)

    def row_grads(gate_part, up_part):
        return (dot_nt(gate_part, gate_w) + dot_nt(up_part, up_w)).astype(BF16)

    def row_sum(value, axis):
        return row_scatter(value.astype(BF16), axis)

    def half_rows(value):
        return half_sum(value.reshape(2, row_count // 2, -1, value.shape[1]), 1)

    expert_grads = [
        dot_tn(grad_result, hidden).astype(BF16),
        dot_tn(rows, grad_gate).astype(BF16),
        dot_tn(rows, grad_up).astype(BF16),
    ]
    sum_down, sum_gate, sum_up = [half_rows(value) for value in expert_grads]
    gate_late, up_late = after((grad_gate, grad_up), expert_grads)
    mate_rows = row_grads(gate_late[capacity:], up_late[capacity:])
    mate_grad = dot_tn(mate_pick, mate_rows).astype(BF16)
    stages = scatter_stages(mate_grad)
    own_gate, own_up = after((gate_late[:capacity], up_late[:capacity]), (mate_grad,))
    own_rows = row_grads(own_gate, own_up)
    normed_s, dy_s = after((normed_two, full_dy), (own_rows, next(stages)))
    shared_width = shared_gate.shape[1]
    shared_out = dot(normed_s, shared_gu_w)
    shared_hidden, shared_act, shared_us = forward(
        shared_out[:, :shared_width], shared_out[:, shared_width:]
    )
    stage = next(stages)
    shared_grad_hidden, stage = after((dot_nt(dy_s, shared_d_w), stage), ())
    grad_shared_gu = jnp.concatenate(
        backward(shared_grad_hidden, shared_act, shared_us), axis=1
    )
    *_, mate_sum = stages
    grad_two = dot_nt(grad_shared_gu, shared_gu_w)
    grad_two = (grad_two + dot_tn(pick, own_rows)).astype(BF16)
    grad_two, mate_sum, sum_down = after((grad_two, mate_sum, sum_down), ())
    mate_grad_part = mate(mate_sum.astype(BF16))
    grad_two_part = cube_scatter(grad_two)
    swap_down = mate_swap(sum_down)
    (sum_gate,) = after((sum_gate,), (grad_two_part,))
    swap_gate = mate_swap(sum_gate)
    late = after((normed_two, grad_shared_gu, shared_hidden, full_dy), (grad_two,))
    grad_sgu = row_sum(dot_tn(late[0], late[1]), 0)
    grad_sd = row_sum(dot_tn(late[2], late[3]), 1)

    (mate_grad_part,) = after((mate_grad_part,), (grad_two_part,))
    grad_two_part = grad_two_part + mate_grad_part.astype(F32)
    dy_part = my_part(full_dy).astype(F32)
    hidden_back, gain_two_grad = norm_back(grad_two_part, unit_two, scale_two, gain_two)
    grad_hidden_part = dy_part + hidden_back
    grad_attn = cube_gather(grad_hidden_part.astype(BF16), 0)

    hidden_late, shared_late = after((hidden, shared_hidden), (grad_hidden_part,))
    result_rows = (weights * dot(hidden_late, down_w)).astype(BF16)
    mate_terms = dot_tn(mate_pick, result_rows[capacity:])
    moe_terms = dot(shared_late, shared_d_w) + dot_tn(pick, result_rows[:capacity])
    both_terms = jnp.stack([moe_terms.astype(BF16), mate_terms.astype(BF16)])
    grad_attn, both_terms, sum_up = after((grad_attn, both_terms, sum_up), ())
    swap_up = mate_swap(sum_up)
    term_stages = scatter_stages(both_terms, 1)

    grad_output_w = row_sum(dot_tn(mixed, grad_attn), 1)
    grad_mixed = dot_nt(grad_attn, output_w).astype(BF16)
    grad_mixed = grad_mixed.reshape(group_rows, head_count, VDIM)
    grad_query_blocks = []
    grad_keys = jnp.zeros((group_rows, head_count, NOPE + ROPE), F32)
    grad_values = jnp.zeros((group_rows, head_count, VDIM), F32)
    for block_number, first_row in enumerate(range(0, group_rows, block_rows)):
        last_row = first_row + block_rows
        scores = block_scores(first_row, last_row)
        probs_f = jnp.exp(scores - lse_blocks[block_number][..., None])
        probs_low = probs_f.astype(BF16)
        grad_block = grad_mixed[first_row:last_row]
        grad_probs = jnp.einsum(
            "qhd,khd->hqk", grad_block, value_heads[:last_row], preferred_element_type=F32
        )
        row_inner = jnp.sum(probs_f * grad_probs, axis=-1, keepdims=True)
        grad_scores = (probs_f * (grad_probs - row_inner)).astype(BF16)
        grad_values = grad_values.at[:last_row].add(
            jnp.einsum("hqk,qhd->khd", probs_low, grad_block, preferred_element_type=F32)
        )
        grad_query_blocks.append(
            softmax_scale
            * jnp.einsum(
                "hqk,khd->qhd", grad_scores, key_heads[:last_row], preferred_element_type=F32
            )
        )
        grad_keys = grad_keys.at[:last_row].add(
            softmax_scale
            * jnp.einsum(
                "hqk,qhd->khd",
                grad_scores,
                query_heads[first_row:last_row],
                preferred_element_type=F32,
            )
        )
    grad_query = jnp.concatenate(grad_query_blocks, axis=0)
    grad_query_raw = (
        jnp.concatenate(
            [grad_query[..., :NOPE], rotate(grad_query[..., NOPE:], position, -1.0)], axis=-1
        )
        .astype(BF16)
        .reshape(group_rows, head_count * (NOPE + ROPE))
    )
    grad_query_raw, _ = after((grad_query_raw, next(term_stages)), ())
    grad_one = dot_nt(grad_query_raw, query_w).astype(BF16)
    *_, both_terms = term_stages
    moe_part, mate_terms = both_terms[0], mate(both_terms[1].astype(BF16))

    grad_one_part = cube_scatter(grad_one)
    mate_terms, moe_part = after((mate_terms, moe_part), (grad_one_part,))
    result_part = (hidden_part + (moe_part + mate_terms.astype(F32))).astype(BF16)
    result_slice = lax.all_to_all(result_part, "col", split_axis=1, concat_axis=0, tiled=True)

    grad_expanded = jnp.concatenate([grad_keys[..., :NOPE], grad_values], axis=-1).astype(BF16)
    grad_expanded = grad_expanded.reshape(group_rows, head_count * (NOPE + VDIM))
    grad_compressed = dot_nt(grad_expanded, expand_w)
    grad_rope_key = rotate(jnp.sum(grad_keys[..., NOPE:], axis=1), position, -1.0)
    grad_latent_part = cube_scatter(
        jnp.concatenate([grad_compressed, grad_rope_key], axis=1).astype(BF16)
    )
    grad_front, latent_gain_grad = norm_back(
        grad_latent_part[:, :LAT], my_part(unit_lat), my_part(scale_lat), latent_g
    )
    grad_latent_part = jnp.concatenate([grad_front, grad_latent_part[:, LAT:]], axis=1).astype(BF16)
    latent_term = dot_nt(grad_latent_part, latent_w)
    grad_one = grad_one_part + latent_term
    scale_one_part = my_part(scale_one)
    input_back, gain_one_grad = norm_back(
        grad_one, x_part * scale_one_part, scale_one_part, gain_one
    )
    grad_input = (grad_hidden_part + input_back).astype(BF16)
    grad_slice = lax.all_to_all(grad_input, "col", split_axis=1, concat_axis=0, tiled=True)
    result = exchange(result_slice, back_list, back_slots)
    tokens_grad = exchange(grad_slice, back_list, back_slots)

    def more_back(carry):
        step, total = carry
        back_more, slots_more = maps_back(step)
        dealt = jnp.concatenate([result_slice, grad_slice], axis=1)
        return step + 1, total + exchange(dealt, back_more, slots_more)

    more = lax.while_loop(
        lambda carry: carry[0] < rounds,
        more_back,
        (jnp.int32(1), jnp.concatenate([result, tokens_grad], axis=1)),
    )[1]
    result, tokens_grad = more[:, :slice_width], more[:, slice_width:]

    grad_expand_w = row_sum(dot_tn(compressed, grad_expanded), 0)
    grad_query_w = row_sum(dot_tn(normed_one, grad_query_raw), 0)
    grad_latent = cube_gather(grad_latent_part, 0)
    my_columns = lax.dynamic_index_in_dim(
        normed_one.reshape(group_rows, row_count, col_count, lat_rows), col_index, 2, False
    ).reshape(group_rows, row_count * lat_rows)
    (grad_latent_w,) = after((row_sum(dot_tn(my_columns, grad_latent), 0),), (grad_one_part,))
    grad_latent_w = cube_gather(grad_latent_w, 0)
    sums = after(
        (swap_down, swap_gate, swap_up, grad_sgu, grad_sd, grad_query_w, grad_expand_w, grad_output_w),
        (grad_slice,),
    )
    swap_down, swap_gate, swap_up, grad_sgu, grad_sd, grad_query_w, grad_expand_w, grad_output_w = sums
    grad_down = in_order(own_slot(sum_down), swap_down).transpose(0, 2, 1)
    grad_gate = in_order(own_slot(sum_gate), swap_gate)
    grad_up = in_order(own_slot(sum_up), swap_up)
    gain_grads = small_sum(jnp.concatenate([gain_one_grad, gain_two_grad, latent_gain_grad]))
    width_two = gain_one_grad.shape[0]
    width_lat = latent_gain_grad.shape[0]

    def my_rows(value):
        width = value.shape[0] // row_count
        return lax.dynamic_slice_in_dim(value, row_index * width, width, 0)

    return (
        result,
        tokens_grad,
        my_rows(gain_grads[:width_two]),
        grad_query_w.astype(F32),
        grad_latent_w.astype(F32),
        my_rows(gain_grads[2 * width_two : 2 * width_two + width_lat]),
        grad_expand_w.astype(F32),
        grad_output_w.astype(F32),
        my_rows(gain_grads[width_two : 2 * width_two]),
        grad_sgu[:, : shared_gate.shape[1]].astype(F32),
        grad_sgu[:, shared_gate.shape[1] :].astype(F32),
        grad_sd.astype(F32),
        grad_gate.astype(F32),
        grad_up.astype(F32),
        grad_down.astype(F32),
    )


def solution(mesh):
    return jax.shard_map(
        body,
        mesh=mesh,
        in_specs=(
            P("row", "col"),
            P("row", "col"),
            P(),
            P("row", None),
            P("row", None),
            P("row", None),
            P("row"),
            P("row", "col"),
            P("row", None),
            P("row"),
            P("row", "col"),
            P("col", "row"),
            P("row"),
            P("row", "col"),
            P("row", "col"),
            P("col", "row"),
            P("col", "row", None),
            P("col", "row", None),
            P("col", None, "row"),
        ),
        out_specs=(
            P("row", "col"),
            P("row", "col"),
            P("row"),
            P("row", "col"),
            P("row", None),
            P("row"),
            P("row", "col"),
            P("col", "row"),
            P("row"),
            P("row", "col"),
            P("row", "col"),
            P("col", "row"),
            P("col", "row", None),
            P("col", "row", None),
            P("col", None, "row"),
        ),
        check_vma=False,
    )
```

```python
import jax
import jax.numpy as jnp
from jax import lax
from jax.experimental.layout import Layout, with_layout_constraint
from jax.sharding import PartitionSpec as P

NOPE = 128
ROPE = 64
VDIM = 128
LAT = 512
TOPK = 6

EPSILON = 1e-06
F32 = jnp.float32
BF16 = jnp.bfloat16


def rotate(value, position, orient):
    half_width = value.shape[-1] // 2
    frequency = 10000.0 ** (-jnp.arange(half_width, dtype=F32) / half_width)
    angles = position.astype(F32)[:, None] * frequency[None, :]
    shape_out = (value.shape[0],) + (1,) * (value.ndim - 2) + (half_width,)
    cosine = jnp.cos(angles).reshape(shape_out)
    sine_part = jnp.sin(angles).reshape(shape_out)
    first_half = value[..., :half_width]
    second = value[..., half_width:]
    return jnp.concatenate(
        [
            first_half * cosine - orient * second * sine_part,
            second * cosine + orient * first_half * sine_part,
        ],
        axis=-1,
    )


def documents(lengths_row, row_count):
    doc_ends = jnp.cumsum(lengths_row)
    starts = doc_ends - lengths_row
    row_number = jnp.arange(row_count, dtype=jnp.int32)
    document = jnp.sum((row_number[:, None] >= doc_ends[None, :]).astype(jnp.int32), axis=1)
    onehot = document[:, None] == jnp.arange(lengths_row.shape[0], dtype=jnp.int32)[None, :]
    position = row_number - jnp.sum(jnp.where(onehot, starts[None, :], 0), axis=1)
    return (document, position)


def silu_parts(value):
    sigmoid_value = jax.nn.sigmoid(value)
    activation = value * sigmoid_value
    activ_slope = sigmoid_value * (1.0 + value * (1.0 - sigmoid_value))
    return (activation, activ_slope)


def norm_back(grad_normed, unit_rows, row_scale, gain_vector):
    scaled = grad_normed * gain_vector
    row_inner = jnp.mean(scaled * unit_rows, axis=-1, keepdims=True)
    return (row_scale * (scaled - unit_rows * row_inner), jnp.sum(grad_normed * unit_rows, axis=0))


def dot(left, right):
    return jnp.dot(left, right, preferred_element_type=F32)


def dot_nt(left, right):
    return lax.dot_general(left, right, (((1,), (1,)), ((), ())), preferred_element_type=F32)


def dot_tn(left, right):
    return lax.dot_general(left, right, (((0,), (0,)), ((), ())), preferred_element_type=F32)


def row_major(value):
    return with_layout_constraint(value, Layout(tuple(range(value.ndim))))


def row_swap(value, bit):
    return lax.ppermute(value, "row", [(j, j ^ bit) for j in range(lax.axis_size("row"))])


def mate(value):
    return row_swap(value, lax.axis_size("row") // 2)


def half_bits():
    return [1 << b for b in range((lax.axis_size("row") // 2).bit_length() - 1)]


def half_pieces(first, item):
    items = {first: item}
    for bit in half_bits():
        items.update({key ^ bit: row_swap(items[key], bit) for key in list(items)})
    return items


def placed(pieces, start, width):
    index = lax.axis_index("row")
    rows = pieces[0].shape[0]
    out = jnp.zeros((rows * lax.axis_size("row"), width), pieces[0].dtype)
    for key, piece in pieces.items():
        out = lax.dynamic_update_slice_in_dim(
            out, piece[:, start : start + width], jnp.bitwise_xor(index, key) * rows, 0
        )
    return out


def expert_scatter(values, holds):
    count = lax.axis_size("row")
    index = lax.axis_index("row")
    rows = values[0].shape[0] // count
    sums = []
    for first, hold in zip((count // 2, 0), holds):
        items = {
            key: jnp.concatenate(
                [
                    lax.dynamic_slice_in_dim(
                        value, jnp.bitwise_xor(index, key ^ first) * rows, rows, 0
                    )
                    for value in values
                ],
                axis=1,
            )
            for key in range(count // 2)
        }
        for bit in half_bits()[::-1]:
            keys = [key for key in items if key < bit]
            new = after([row_swap(items[key ^ bit], bit) for key in keys], hold)
            items = {
                key: (items[key].astype(F32) + piece.astype(F32)).astype(BF16)
                for key, piece in zip(keys, new)
            }
        sums.append(items[0])
    return sums[1], sums[0]


def swap(value, bit):
    return lax.ppermute(value, "col", [(j, j ^ bit) for j in range(lax.axis_size("col"))])


def chip_bits():
    return [1 << b for b in range(1, (lax.axis_size("col") - 1).bit_length())]


def chip_swap(value, step):
    bits = chip_bits()
    other = bits[::-1]
    return lax.ppermute(
        value,
        "col",
        [(j, j ^ (other if j % 2 else bits)[step]) for j in range(lax.axis_size("col"))],
    )


def block_at(device, place):
    bits = chip_bits()
    even = sum(bit for n, bit in enumerate(bits) if place >> n & 1)
    odd = sum(bit for n, bit in enumerate(bits[::-1]) if place >> n & 1)
    return jnp.bitwise_xor(device, jnp.where(device % 2 == 0, even, odd))


def cube_gather(block, axis):
    count = lax.axis_size("col")
    index = lax.axis_index("col")
    width = block.shape[axis]
    shape = list(block.shape)
    shape[axis] = width * count
    out = jnp.zeros(shape, block.dtype)
    held = row_major(block)[None]
    sibling = jnp.bitwise_xor(index, 1)
    done = 0
    for step in range(len(chip_bits()) + 1):
        theirs = swap(held[done:], 1)
        for place in range(done, held.shape[0]):
            for item, owner in ((held[place], index), (theirs[place - done], sibling)):
                out = lax.dynamic_update_slice_in_dim(
                    out, item, block_at(owner, place) * width, axis
                )
        done = held.shape[0]
        if step < len(chip_bits()):
            held = jnp.concatenate([held, chip_swap(held, step)], axis=0)
    return out


def cube_scatter(value, axis=0):
    count = lax.axis_size("col")
    index = lax.axis_index("col")
    rows = value.shape[axis] // count
    value = row_major(value)

    def blocks(device):
        return jnp.stack(
            [
                lax.dynamic_slice_in_dim(value, block_at(device, place) * rows, rows, axis)
                for place in range(count // 2)
            ]
        )

    got = swap(blocks(jnp.bitwise_xor(index, 1)), 1)
    held = blocks(index).astype(F32) + got.astype(F32)
    for step in range(len(chip_bits()) - 1, -1, -1):
        held = held.astype(BF16)
        half = held.shape[0] // 2
        got = chip_swap(held[half:], step)
        held = held[:half].astype(F32) + got.astype(F32)
    return held[0]


def row_gather(shard, axis):
    return lax.all_gather(shard, "row", axis=axis, tiled=True)


def after(values, earlier):
    out = lax.optimization_barrier(tuple(values) + tuple(earlier))
    return out[: len(values)]


def row_scatter(value, axis):
    return lax.psum_scatter(value, "row", scatter_dimension=axis, tiled=True)


def small_sum(value):
    for bit in [1] + chip_bits():
        value = value + swap(value, bit)
    count = lax.axis_size("row")
    total = value
    for k in range(1, count):
        total = total + lax.ppermute(value, "row", [(j, (j + k) % count) for j in range(count)])
    return total


def onehot(index, width):
    return (index[:, None] == jnp.arange(width, dtype=jnp.int32)[None, :]).astype(BF16)


def exchange(value, sent_of, slot_of):
    count = lax.axis_size("row")
    sent = row_major(dot(onehot(sent_of, value.shape[0]), value).astype(BF16))
    sent = sent.reshape(count, -1, value.shape[1])
    got = lax.all_to_all(sent, "row", split_axis=0, concat_axis=0, tiled=True)
    got = got.reshape(-1, value.shape[1])
    return row_major(dot(onehot(slot_of, got.shape[0]), got).astype(BF16))


def body(
    tokens,
    cotangent,
    dealing,
    doc_lengths,
    routes,
    gate_weights,
    attn_gain,
    w_query,
    w_latent,
    latent_gain,
    w_expand,
    w_output,
    ffn_gain,
    shared_gate,
    shared_up,
    shared_down,
    expert_gate,
    expert_up,
    expert_down,
):
    group_rows = routes.shape[0]
    row_count = lax.axis_size("row")
    col_count = lax.axis_size("col")
    row_index = lax.axis_index("row")
    col_index = lax.axis_index("col")
    part_rows = group_rows // col_count
    local_count = expert_gate.shape[0]
    capacity = 4 * group_rows * TOPK // (3 * local_count * col_count)

    def my_part(value):
        return lax.dynamic_slice_in_dim(value, col_index * part_rows, part_rows, 0)

    token_ids = jnp.arange(group_rows, dtype=jnp.int32)
    room = max(16, 5 * group_rows // (16 * row_count) * 4)
    lists = dealing.reshape(row_count, group_rows)
    source = lists // group_rows
    place_in = lists - source * group_rows
    from_here = source == row_index
    rank_here = jnp.where(from_here, jnp.cumsum(from_here.astype(jnp.int32), axis=1) - 1, -1)
    my_source = lax.dynamic_index_in_dim(source, row_index, 0, False)
    by_source = my_source[None, :] == jnp.arange(row_count, dtype=jnp.int32)[:, None]
    count_in = jnp.cumsum(by_source.astype(jnp.int32), axis=1)
    my_rank = jnp.sum(jnp.where(by_source, count_in, 0), axis=0) - 1
    all_counts = jnp.sum(
        (source[:, None, :] == jnp.arange(row_count, dtype=jnp.int32)[None, :, None]).astype(
            jnp.int32
        ),
        axis=2,
    )
    rounds = (jnp.max(all_counts) + room - 1) // room

    def maps_out(step):
        places = step * room + jnp.arange(room, dtype=jnp.int32)
        hit = rank_here[:, None, :] == places[None, :, None]
        listed = jnp.sum(jnp.where(hit, place_in[:, None, :] + 1, 0), axis=2).reshape(-1) - 1
        slot = my_rank - step * room
        inside = (slot >= 0) & (slot < room)
        return listed, jnp.where(inside, my_source * room + slot, -1)

    out_list, in_slots = maps_out(0)

    def more_dealt(carry):
        step, total = carry
        out_more, in_more = maps_out(step)
        given = jnp.concatenate([tokens, cotangent], axis=1)
        return step + 1, total + exchange(given, out_more, in_more)

    host = row_index // (row_count // 2)
    expert = col_index * local_count + host

    def chosen(group_routes, group_gates):
        named = group_routes == expert
        named_any = jnp.any(named, axis=1)
        running = jnp.cumsum(named_any.astype(jnp.int32))
        place = jnp.where(named_any, running - 1, -1)
        pick = place[None, :] == jnp.arange(capacity, dtype=jnp.int32)[:, None]
        token_weight = jnp.sum(jnp.where(named, group_gates, 0.0), axis=1)
        return pick.astype(BF16), jnp.sum(jnp.where(pick, token_weight[None, :], 0.0), axis=1)

    document, position = documents(doc_lengths[0], group_rows)

    rows_in, dim = w_query.shape[0], w_query.shape[0] * row_count
    wide = attn_gain.shape[0]
    slice_width = tokens.shape[1]
    more = lax.while_loop(
        lambda carry: carry[0] < rounds,
        more_dealt,
        (jnp.int32(1), jnp.zeros((group_rows, 2 * slice_width), BF16)),
    )[1]
    dealt_x = exchange(tokens, out_list, in_slots) + more[:, :slice_width]
    dealt_x, mate_routes, mate_gates = after((dealt_x, mate(routes), mate(gate_weights)), ())
    routes_late, gates_late = after((routes, gate_weights), (dealt_x,))
    pick, weight = chosen(routes_late, gates_late)
    mate_pick, mate_weight = chosen(mate_routes, mate_gates)
    full_x = cube_gather(dealt_x, 1)

    query_width = w_query.shape[1]
    lat_rows = rows_in // col_count
    w_latent_s = lax.dynamic_slice_in_dim(w_latent, col_index * lat_rows, lat_rows, 0)
    parts = [
        w_query,
        w_latent_s.reshape(-1, query_width),
        jnp.concatenate([w_output, w_expand], axis=0).reshape(-1, query_width),
        jnp.concatenate([attn_gain, ffn_gain, latent_gain]).reshape(-1, query_width),
    ]
    first_s = jnp.concatenate(parts, axis=0)
    first_s = jnp.pad(first_s, ((0, -first_s.shape[0] % 16), (0, 0)))
    (first_s,) = after((first_s,), (dealt_x,))
    first_w = row_gather(first_s[None], 0)
    pieces, start = [], 0
    for part in parts:
        pieces.append(first_w[:, start : start + part.shape[0]])
        start += part.shape[0]
    query_w = pieces[0].reshape(dim, query_width)
    latent_w = cube_gather(pieces[1].reshape(row_count * lat_rows, w_latent.shape[1]), 0)
    latent_w = latent_w.reshape(col_count, row_count, lat_rows, -1).transpose(1, 0, 2, 3)
    latent_w = latent_w.reshape(dim, w_latent.shape[1])
    out_rows, out_width = w_output.shape
    rest_w = pieces[2].reshape(row_count, -1, out_width)
    output_w = rest_w[:, :out_rows].transpose(1, 0, 2).reshape(out_rows, dim)
    expand_w = rest_w[:, out_rows:].reshape(-1, out_width)
    gains = pieces[3].reshape(row_count, -1)
    gain_one = gains[:, :wide].reshape(-1).astype(F32)
    gain_two = gains[:, wide : 2 * wide].reshape(-1).astype(F32)
    latent_g = gains[:, 2 * wide :].reshape(-1).astype(F32)

    (cotangent_s,) = after((cotangent,), (dealt_x,))
    dealt_dy = exchange(cotangent_s, out_list, in_slots) + more[:, slice_width:]

    def expert_part(number):
        parts = [lax.dynamic_index_in_dim(v, number, 0, False) for v in (expert_gate, expert_up)]
        down = lax.dynamic_index_in_dim(expert_down, number, 0, False)
        return jnp.concatenate(parts + [down.T], axis=1)

    kept, given = after((expert_part(host), expert_part(1 - host)), (first_w,))
    width_ff = expert_gate.shape[2]
    kept_pieces = half_pieces(0, kept)
    mate_gu, mate_down = mate(given[:, : 2 * width_ff]), mate(given[:, 2 * width_ff :])
    shared_gu_s, shared_d_s = after(
        (jnp.concatenate([shared_gate, shared_up], axis=1), shared_down), (first_w,)
    )
    shared_gu_w = row_gather(shared_gu_s, 0)
    shared_d_w = row_gather(shared_d_s, 1)

    head_count = query_w.shape[1] // (NOPE + ROPE)
    softmax_scale = (NOPE + ROPE) ** (-0.5)
    block_rows = min(512, group_rows)
    row_number = token_ids
    residual = full_x.astype(F32)
    scale_one = lax.rsqrt(jnp.mean(residual * residual, axis=-1, keepdims=True) + EPSILON)
    normed_one = (residual * scale_one * gain_one).astype(BF16)
    query_raw = dot(normed_one, query_w)
    query_raw = query_raw.reshape(group_rows, head_count, NOPE + ROPE)
    query_heads = jnp.concatenate(
        [query_raw[..., :NOPE], rotate(query_raw[..., NOPE:], position, 1.0)], axis=-1
    ).astype(BF16)
    keys = sorted(kept_pieces)
    query_heads, *pieces = after([query_heads] + [kept_pieces[key] for key in keys], ())
    kept_pieces = dict(zip(keys, pieces))
    latent = dot(normed_one, latent_w)
    latent_front = latent[:, :LAT]
    scale_lat = lax.rsqrt(jnp.mean(latent_front * latent_front, axis=-1, keepdims=True) + EPSILON)
    unit_lat = latent_front * scale_lat
    compressed = (unit_lat * latent_g).astype(BF16)
    rope_key = rotate(latent[:, LAT:], position, 1.0).astype(BF16)
    expanded = dot(compressed, expand_w).astype(BF16)
    expanded = expanded.reshape(group_rows, head_count, NOPE + VDIM)
    key_heads = jnp.concatenate(
        [
            expanded[..., :NOPE],
            jnp.broadcast_to(rope_key[:, None, :], (group_rows, head_count, ROPE)),
        ],
        axis=-1,
    )
    value_heads = expanded[..., NOPE:]

    def block_scores(first_row, last_row):
        raw_scores = (
            jnp.einsum(
                "qhd,khd->hqk",
                query_heads[first_row:last_row],
                key_heads[:last_row],
                preferred_element_type=F32,
            )
            * softmax_scale
        )
        allowed = (document[first_row:last_row, None] == document[None, :last_row]) & (
            row_number[first_row:last_row, None] >= row_number[None, :last_row]
        )
        return jnp.where(allowed[None], raw_scores, -1e30)

    mixed_blocks = []
    lse_blocks = []
    for first_row in range(0, group_rows, block_rows):
        last_row = first_row + block_rows
        scores = block_scores(first_row, last_row)
        row_top = jnp.max(scores, axis=-1, keepdims=True)
        exp_scores = jnp.exp(scores - row_top)
        row_total = jnp.sum(exp_scores, axis=-1, keepdims=True)
        probs_low = (exp_scores / row_total).astype(BF16)
        lse_blocks.append(row_top[..., 0] + jnp.log(row_total[..., 0]))
        mixed_blocks.append(
            jnp.einsum(
                "hqk,khd->qhd",
                probs_low,
                value_heads[:last_row],
                preferred_element_type=F32,
            )
        )
    mixed = (
        jnp.concatenate(mixed_blocks, axis=0).reshape(group_rows, head_count * VDIM).astype(BF16)
    )
    attn_terms, mate_down = after((dot(mixed, output_w).astype(BF16), mate_down), ())
    attn_part = cube_scatter(attn_terms)
    dy_pair = after((dealt_dy, mate(dealt_dy)), (attn_part,))
    both_dy = cube_gather(jnp.concatenate(dy_pair, axis=0), 1)
    full_dy, mate_dy = both_dy[:group_rows], both_dy[group_rows:]
    mate_down, mate_gu = after((mate_down, mate_gu), (attn_part,))
    down_pieces = half_pieces(row_count // 2, mate_down)
    gu_pieces = half_pieces(row_count // 2, mate_gu)
    kept_down = {key: piece[:, 2 * width_ff :] for key, piece in kept_pieces.items()}
    gate_up_w = placed({**kept_pieces, **gu_pieces}, 0, 2 * width_ff)
    down_t = placed({**kept_down, **down_pieces}, 0, width_ff)
    x_part = my_part(full_x).astype(F32)
    hidden_part = x_part + attn_part
    scale_two = lax.rsqrt(jnp.mean(hidden_part * hidden_part, axis=-1, keepdims=True) + EPSILON)
    unit_two = hidden_part * scale_two
    normed_part = (unit_two * gain_two).astype(BF16)
    mate_part = mate(normed_part)
    normed_two = cube_gather(normed_part, 0)
    (mate_part,) = after((mate_part,), (normed_two,))
    mate_two = cube_gather(mate_part, 0)

    place_late, rank_late, here_late, source_late, my_rank_late = after(
        (place_in, rank_here, from_here, my_source, my_rank), (normed_part,)
    )
    hit = (place_late[:, :, None] == token_ids[None, None, :]) & here_late[:, :, None]
    rank_of = jnp.sum(jnp.where(hit, rank_late[:, :, None], 0), axis=(0, 1))
    groups = jnp.arange(row_count, dtype=jnp.int32)
    group_of = jnp.sum(jnp.where(hit, groups[:, None, None], 0), axis=(0, 1))

    def maps_back(step):
        places = step * room + jnp.arange(room, dtype=jnp.int32)
        hit = (my_rank_late[None, None, :] == places[None, :, None]) & (
            source_late[None, None, :] == groups[:, None, None]
        )
        listed = jnp.sum(jnp.where(hit, token_ids[None, None, :] + 1, 0), axis=2).reshape(-1) - 1
        slot = rank_of - step * room
        inside = (slot >= 0) & (slot < room)
        return listed, jnp.where(inside, group_of * room + slot, -1)

    back_list, back_slots = maps_back(0)
    gate_up_w, back_list, back_slots = after((gate_up_w, back_list, back_slots), ())

    def forward(rows, gate_up_w):
        width = gate_up_w.shape[1] // 2
        gate_up = dot(rows, gate_up_w)
        gate_out, up_out = gate_up[:, :width], gate_up[:, width:]
        act, slope = silu_parts(gate_out)
        hidden = (act * up_out).astype(BF16)
        return hidden, act, up_out * slope

    def backward(grad_hidden, act, up_slope):
        return jnp.concatenate(
            [(grad_hidden * up_slope).astype(BF16), (grad_hidden * act).astype(BF16)], axis=1
        )

    def row_sum(value, axis):
        return row_scatter(value.astype(BF16), axis)

    shared_hidden, shared_act, shared_us = forward(normed_two, shared_gu_w)
    grad_shared_gu = backward(dot_nt(full_dy, shared_d_w), shared_act, shared_us)
    grad_two = dot_nt(grad_shared_gu, shared_gu_w)
    moe_terms = dot(shared_hidden, shared_d_w)
    grad_sgu = row_sum(dot_tn(normed_two, grad_shared_gu), 0)
    grad_sd = row_sum(dot_tn(shared_hidden, full_dy), 1)

    rows = jnp.concatenate(
        [dot(pick, normed_two).astype(BF16), dot(mate_pick, mate_two).astype(BF16)], axis=0
    )
    grad_result = jnp.concatenate(
        [
            (weight[:, None] * dot(pick, full_dy)).astype(BF16),
            (mate_weight[:, None] * dot(mate_pick, mate_dy)).astype(BF16),
        ],
        axis=0,
    )
    hidden, act, up_slope = forward(rows, gate_up_w)
    grad_gate_up = backward(dot(grad_result, down_t), act, up_slope)
    mate_rows = dot_nt(grad_gate_up[capacity:], gate_up_w).astype(BF16)
    mate_grad = dot_tn(mate_pick, mate_rows).astype(BF16)
    (own_gate_up,) = after((grad_gate_up[:capacity],), (mate_grad,))
    own_rows = dot_nt(own_gate_up, gate_up_w).astype(BF16)
    grad_two = (grad_two + dot_tn(pick, own_rows)).astype(BF16)
    mate_grad = mate(cube_scatter(mate_grad).astype(BF16))
    grad_gu = dot_tn(rows, grad_gate_up).astype(BF16)
    grad_down = dot_tn(grad_result, hidden).astype(BF16)

    grad_two_part = cube_scatter(grad_two) + mate_grad.astype(F32)
    dy_part = my_part(full_dy).astype(F32)
    hidden_back, gain_two_grad = norm_back(grad_two_part, unit_two, scale_two, gain_two)
    grad_hidden_part = dy_part + hidden_back
    grad_attn = cube_gather(grad_hidden_part.astype(BF16), 0)

    (hidden_late,) = after((hidden,), (grad_hidden_part,))
    weights = jnp.concatenate([weight, mate_weight])
    result_rows = (weights[:, None] * dot_nt(hidden_late, down_t)).astype(BF16)
    mate_terms = dot_tn(mate_pick, result_rows[capacity:]).astype(BF16)
    moe_terms = (moe_terms + dot_tn(pick, result_rows[:capacity])).astype(BF16)
    (both_terms,) = after((jnp.stack([moe_terms, mate_terms]),), (grad_attn,))
    both_terms = cube_scatter(both_terms, 1)
    moe_part, mate_terms = both_terms[0], mate(both_terms[1].astype(BF16))

    grad_mixed = dot_nt(grad_attn, output_w).astype(BF16)
    grad_mixed = grad_mixed.reshape(group_rows, head_count, VDIM)
    grad_query_blocks = []
    grad_keys = jnp.zeros((group_rows, head_count, NOPE + ROPE), F32)
    grad_values = jnp.zeros((group_rows, head_count, VDIM), F32)
    for block_number, first_row in enumerate(range(0, group_rows, block_rows)):
        last_row = first_row + block_rows
        scores = block_scores(first_row, last_row)
        probs_f = jnp.exp(scores - lse_blocks[block_number][..., None])
        probs_low = probs_f.astype(BF16)
        grad_block = grad_mixed[first_row:last_row]
        grad_probs = jnp.einsum(
            "qhd,khd->hqk", grad_block, value_heads[:last_row], preferred_element_type=F32
        )
        row_inner = jnp.sum(probs_f * grad_probs, axis=-1, keepdims=True)
        grad_scores = (probs_f * (grad_probs - row_inner)).astype(BF16)
        grad_values = grad_values.at[:last_row].add(
            jnp.einsum("hqk,qhd->khd", probs_low, grad_block, preferred_element_type=F32)
        )
        grad_query_blocks.append(
            softmax_scale
            * jnp.einsum(
                "hqk,khd->qhd", grad_scores, key_heads[:last_row], preferred_element_type=F32
            )
        )
        grad_keys = grad_keys.at[:last_row].add(
            softmax_scale
            * jnp.einsum(
                "hqk,qhd->khd",
                grad_scores,
                query_heads[first_row:last_row],
                preferred_element_type=F32,
            )
        )
    grad_query = jnp.concatenate(grad_query_blocks, axis=0)
    grad_query_raw = (
        jnp.concatenate(
            [grad_query[..., :NOPE], rotate(grad_query[..., NOPE:], position, -1.0)], axis=-1
        )
        .astype(BF16)
        .reshape(group_rows, head_count * (NOPE + ROPE))
    )
    own_sum, mate_sum = expert_scatter([grad_gu, grad_down], ((grad_attn,), (grad_attn,)))
    grad_query_raw, mate_sum, grad_sgu, grad_sd = after(
        (grad_query_raw, mate_sum, grad_sgu, grad_sd), ()
    )
    other_gu, other_down = mate(mate_sum[:, : 2 * width_ff]), mate(mate_sum[:, 2 * width_ff :])
    grad_one = dot_nt(grad_query_raw, query_w).astype(BF16)
    grad_one_part, other_down = after((cube_scatter(grad_one), other_down), ())

    mate_terms, moe_part = after((mate_terms, moe_part), (grad_one,))
    result_part = (hidden_part + (moe_part + mate_terms.astype(F32))).astype(BF16)
    result_slice = lax.all_to_all(result_part, "col", split_axis=1, concat_axis=0, tiled=True)
    result = exchange(result_slice, back_list, back_slots)

    grad_expanded = jnp.concatenate([grad_keys[..., :NOPE], grad_values], axis=-1).astype(BF16)
    grad_expanded = grad_expanded.reshape(group_rows, head_count * (NOPE + VDIM))
    grad_compressed = dot_nt(grad_expanded, expand_w)
    grad_rope_key = rotate(jnp.sum(grad_keys[..., NOPE:], axis=1), position, -1.0)
    grad_latent_part = cube_scatter(
        jnp.concatenate([grad_compressed, grad_rope_key], axis=1).astype(BF16)
    )
    grad_front, latent_gain_grad = norm_back(
        grad_latent_part[:, :LAT], my_part(unit_lat), my_part(scale_lat), latent_g
    )
    grad_latent_part = jnp.concatenate([grad_front, grad_latent_part[:, LAT:]], axis=1).astype(BF16)
    latent_term = dot_nt(grad_latent_part, latent_w)
    grad_one = grad_one_part + latent_term
    scale_one_part = my_part(scale_one)
    input_back, gain_one_grad = norm_back(
        grad_one, x_part * scale_one_part, scale_one_part, gain_one
    )
    grad_input = (grad_hidden_part + input_back).astype(BF16)
    grad_slice = lax.all_to_all(grad_input, "col", split_axis=1, concat_axis=0, tiled=True)
    tokens_grad = exchange(grad_slice, back_list, back_slots)

    def more_back(carry):
        step, total = carry
        back_more, slots_more = maps_back(step)
        dealt = jnp.concatenate([result_slice, grad_slice], axis=1)
        return step + 1, total + exchange(dealt, back_more, slots_more)

    more = lax.while_loop(
        lambda carry: carry[0] < rounds,
        more_back,
        (jnp.int32(1), jnp.concatenate([result, tokens_grad], axis=1)),
    )[1]
    result, tokens_grad = more[:, :slice_width], more[:, slice_width:]

    late = after((normed_one, compressed, mixed), (grad_one,))
    grad_expand_w = row_sum(dot_tn(late[1], grad_expanded), 0)
    grad_query_w = row_sum(dot_tn(late[0], grad_query_raw), 0)
    grad_output_w = row_sum(dot_tn(late[2], grad_attn), 1)
    grad_latent = cube_gather(grad_latent_part, 0)
    my_columns = lax.dynamic_index_in_dim(
        late[0].reshape(group_rows, row_count, col_count, lat_rows), col_index, 2, False
    ).reshape(group_rows, row_count * lat_rows)
    (grad_latent_w,) = after((row_sum(dot_tn(my_columns, grad_latent), 0),), (grad_one_part,))
    grad_latent_w = cube_gather(grad_latent_w, 0)
    sums = after(
        (own_sum, other_gu, other_down, grad_sgu, grad_sd, grad_query_w, grad_expand_w, grad_output_w),
        (grad_slice,),
    )
    own_sum, other_gu, other_down, grad_sgu, grad_sd, grad_query_w, grad_expand_w, grad_output_w = sums
    gain_grads = small_sum(jnp.concatenate([gain_one_grad, gain_two_grad, latent_gain_grad]))
    def in_order(own, other):
        return jnp.stack([jnp.where(host == 0, own, other), jnp.where(host == 0, other, own)])

    expert_gu = in_order(own_sum[:, : 2 * width_ff], other_gu).astype(F32)
    expert_d = in_order(own_sum[:, 2 * width_ff :].T, other_down.T).astype(F32)
    width_two = gain_one_grad.shape[0]
    width_lat = latent_gain_grad.shape[0]

    def my_rows(value):
        width = value.shape[0] // row_count
        return lax.dynamic_slice_in_dim(value, row_index * width, width, 0)

    return (
        result,
        tokens_grad,
        my_rows(gain_grads[:width_two]),
        grad_query_w.astype(F32),
        grad_latent_w.astype(F32),
        my_rows(gain_grads[2 * width_two : 2 * width_two + width_lat]),
        grad_expand_w.astype(F32),
        grad_output_w.astype(F32),
        my_rows(gain_grads[width_two : 2 * width_two]),
        grad_sgu[:, : shared_gate.shape[1]].astype(F32),
        grad_sgu[:, shared_gate.shape[1] :].astype(F32),
        grad_sd.astype(F32),
        expert_gu[:, :, :width_ff],
        expert_gu[:, :, width_ff:],
        expert_d,
    )


def solution(mesh):
    return jax.shard_map(
        body,
        mesh=mesh,
        in_specs=(
            P("row", "col"),
            P("row", "col"),
            P(),
            P("row", None),
            P("row", None),
            P("row", None),
            P("row"),
            P("row", "col"),
            P("row", None),
            P("row"),
            P("row", "col"),
            P("col", "row"),
            P("row"),
            P("row", "col"),
            P("row", "col"),
            P("col", "row"),
            P("col", "row", None),
            P("col", "row", None),
            P("col", None, "row"),
        ),
        out_specs=(
            P("row", "col"),
            P("row", "col"),
            P("row"),
            P("row", "col"),
            P("row", None),
            P("row"),
            P("row", "col"),
            P("col", "row"),
            P("row"),
            P("row", "col"),
            P("row", "col"),
            P("col", "row"),
            P("col", "row", None),
            P("col", "row", None),
            P("col", None, "row"),
        ),
        check_vma=False,
    )
```

```python
import jax
import jax.numpy as jnp
from jax import lax
from jax.experimental.layout import Layout, with_layout_constraint
from jax.sharding import PartitionSpec as P

NOPE = 128
ROPE = 64
VDIM = 128
LAT = 512
TOPK = 6

EPSILON = 1e-06
F32 = jnp.float32
BF16 = jnp.bfloat16


def rotate(value, position, orient):
    half_width = value.shape[-1] // 2
    frequency = 10000.0 ** (-jnp.arange(half_width, dtype=F32) / half_width)
    angles = position.astype(F32)[:, None] * frequency[None, :]
    shape_out = (value.shape[0],) + (1,) * (value.ndim - 2) + (half_width,)
    cosine = jnp.cos(angles).reshape(shape_out)
    sine_part = jnp.sin(angles).reshape(shape_out)
    first_half = value[..., :half_width]
    second = value[..., half_width:]
    return jnp.concatenate(
        [
            first_half * cosine - orient * second * sine_part,
            second * cosine + orient * first_half * sine_part,
        ],
        axis=-1,
    )


def documents(lengths_row, row_count):
    doc_ends = jnp.cumsum(lengths_row)
    starts = doc_ends - lengths_row
    row_number = jnp.arange(row_count, dtype=jnp.int32)
    document = jnp.sum((row_number[:, None] >= doc_ends[None, :]).astype(jnp.int32), axis=1)
    onehot = document[:, None] == jnp.arange(lengths_row.shape[0], dtype=jnp.int32)[None, :]
    position = row_number - jnp.sum(jnp.where(onehot, starts[None, :], 0), axis=1)
    return (document, position)


def silu_parts(value):
    sigmoid_value = jax.nn.sigmoid(value)
    activation = value * sigmoid_value
    activ_slope = sigmoid_value * (1.0 + value * (1.0 - sigmoid_value))
    return (activation, activ_slope)


def norm_back(grad_normed, unit_rows, row_scale, gain_vector):
    scaled = grad_normed * gain_vector
    row_inner = jnp.mean(scaled * unit_rows, axis=-1, keepdims=True)
    return (row_scale * (scaled - unit_rows * row_inner), jnp.sum(grad_normed * unit_rows, axis=0))


def dot(left, right):
    return jnp.dot(left, right, preferred_element_type=F32)


def dot_nt(left, right):
    return lax.dot_general(left, right, (((1,), (1,)), ((), ())), preferred_element_type=F32)


def dot_tn(left, right):
    return lax.dot_general(left, right, (((0,), (0,)), ((), ())), preferred_element_type=F32)


def row_major(value):
    return with_layout_constraint(value, Layout(tuple(range(value.ndim))))


def row_swap(value, bit):
    return lax.ppermute(value, "row", [(j, j ^ bit) for j in range(lax.axis_size("row"))])


def mate(value):
    return row_swap(value, lax.axis_size("row") // 2)


def half_bits():
    return [1 << b for b in range((lax.axis_size("row") // 2).bit_length() - 1)]


def expert_gather(kept, given, axis):
    count = lax.axis_size("row")
    index = lax.axis_index("row")
    width = kept.shape[axis]
    shape = list(kept.shape)
    shape[axis] = width * count
    out = jnp.zeros(shape, kept.dtype)
    for first, item in ((0, kept), (count // 2, mate(given))):
        items = {first: item}
        for bit in half_bits():
            items.update({key ^ bit: row_swap(items[key], bit) for key in list(items)})
        for key, piece in items.items():
            out = lax.dynamic_update_slice_in_dim(
                out, piece, jnp.bitwise_xor(index, key) * width, axis
            )
    return out


def expert_scatter(value, axis):
    count = lax.axis_size("row")
    index = lax.axis_index("row")
    width = value.shape[axis] // count
    sums = []
    for first in (count // 2, 0):
        items = {
            key: lax.dynamic_slice_in_dim(
                value, jnp.bitwise_xor(index, key ^ first) * width, width, axis
            )
            for key in range(count // 2)
        }
        for bit in half_bits()[::-1]:
            items = {
                key: (
                    items[key].astype(F32) + row_swap(items[key ^ bit], bit).astype(F32)
                ).astype(BF16)
                for key in items
                if key < bit
            }
        sums.append(items[0])
    return sums[1], sums[0]


def swap(value, bit):
    return lax.ppermute(value, "col", [(j, j ^ bit) for j in range(lax.axis_size("col"))])


def chip_bits():
    return [1 << b for b in range(1, (lax.axis_size("col") - 1).bit_length())]


def chip_swap(value, step):
    bits = chip_bits()
    other = bits[::-1]
    return lax.ppermute(
        value,
        "col",
        [(j, j ^ (other if j % 2 else bits)[step]) for j in range(lax.axis_size("col"))],
    )


def block_at(device, place):
    bits = chip_bits()
    even = sum(bit for n, bit in enumerate(bits) if place >> n & 1)
    odd = sum(bit for n, bit in enumerate(bits[::-1]) if place >> n & 1)
    return jnp.bitwise_xor(device, jnp.where(device % 2 == 0, even, odd))


def cube_gather(block, axis):
    count = lax.axis_size("col")
    index = lax.axis_index("col")
    width = block.shape[axis]
    shape = list(block.shape)
    shape[axis] = width * count
    out = jnp.zeros(shape, block.dtype)
    held = row_major(block)[None]
    sibling = jnp.bitwise_xor(index, 1)
    done = 0
    for step in range(len(chip_bits()) + 1):
        theirs = swap(held[done:], 1)
        for place in range(done, held.shape[0]):
            for item, owner in ((held[place], index), (theirs[place - done], sibling)):
                out = lax.dynamic_update_slice_in_dim(
                    out, item, block_at(owner, place) * width, axis
                )
        done = held.shape[0]
        if step < len(chip_bits()):
            held = jnp.concatenate([held, chip_swap(held, step)], axis=0)
    return out


def cube_scatter(value):
    count = lax.axis_size("col")
    index = lax.axis_index("col")
    rows = value.shape[0] // count
    value = row_major(value)

    def blocks(device):
        return jnp.stack(
            [
                lax.dynamic_slice_in_dim(value, block_at(device, place) * rows, rows, 0)
                for place in range(count // 2)
            ]
        )

    got = swap(blocks(jnp.bitwise_xor(index, 1)), 1)
    held = blocks(index).astype(F32) + got.astype(F32)
    for step in range(len(chip_bits()) - 1, -1, -1):
        held = held.astype(BF16)
        half = held.shape[0] // 2
        got = chip_swap(held[half:], step)
        held = held[:half].astype(F32) + got.astype(F32)
    return held[0]


def row_gather(shard, axis):
    return lax.all_gather(shard, "row", axis=axis, tiled=True)


def after(values, earlier):
    out = lax.optimization_barrier(tuple(values) + tuple(earlier))
    return out[: len(values)]


def row_scatter(value, axis):
    return lax.psum_scatter(value, "row", scatter_dimension=axis, tiled=True)


def small_sum(value):
    for bit in [1] + chip_bits():
        value = value + swap(value, bit)
    count = lax.axis_size("row")
    total = value
    for k in range(1, count):
        total = total + lax.ppermute(value, "row", [(j, (j + k) % count) for j in range(count)])
    return total


def onehot(index, width):
    return (index[:, None] == jnp.arange(width, dtype=jnp.int32)[None, :]).astype(BF16)


def exchange(value, sent_of, slot_of):
    count = lax.axis_size("row")
    sent = row_major(dot(onehot(sent_of, value.shape[0]), value).astype(BF16))
    sent = sent.reshape(count, -1, value.shape[1])
    got = lax.all_to_all(sent, "row", split_axis=0, concat_axis=0, tiled=True)
    got = got.reshape(-1, value.shape[1])
    return row_major(dot(onehot(slot_of, got.shape[0]), got).astype(BF16))


def body(
    tokens,
    cotangent,
    dealing,
    doc_lengths,
    routes,
    gate_weights,
    attn_gain,
    w_query,
    w_latent,
    latent_gain,
    w_expand,
    w_output,
    ffn_gain,
    shared_gate,
    shared_up,
    shared_down,
    expert_gate,
    expert_up,
    expert_down,
):
    group_rows = routes.shape[0]
    row_count = lax.axis_size("row")
    col_count = lax.axis_size("col")
    row_index = lax.axis_index("row")
    col_index = lax.axis_index("col")
    part_rows = group_rows // col_count
    local_count = expert_gate.shape[0]
    capacity = 4 * group_rows * TOPK // (3 * local_count * col_count)

    def my_part(value):
        return lax.dynamic_slice_in_dim(value, col_index * part_rows, part_rows, 0)

    token_ids = jnp.arange(group_rows, dtype=jnp.int32)
    room = max(16, 5 * group_rows // (16 * row_count) * 4)
    lists = dealing.reshape(row_count, group_rows)
    source = lists // group_rows
    place_in = lists - source * group_rows
    from_here = source == row_index
    rank_here = jnp.where(from_here, jnp.cumsum(from_here.astype(jnp.int32), axis=1) - 1, -1)
    my_source = lax.dynamic_index_in_dim(source, row_index, 0, False)
    by_source = my_source[None, :] == jnp.arange(row_count, dtype=jnp.int32)[:, None]
    count_in = jnp.cumsum(by_source.astype(jnp.int32), axis=1)
    my_rank = jnp.sum(jnp.where(by_source, count_in, 0), axis=0) - 1
    all_counts = jnp.sum(
        (source[:, None, :] == jnp.arange(row_count, dtype=jnp.int32)[None, :, None]).astype(
            jnp.int32
        ),
        axis=2,
    )
    rounds = (jnp.max(all_counts) + room - 1) // room

    def maps_out(step):
        places = step * room + jnp.arange(room, dtype=jnp.int32)
        hit = rank_here[:, None, :] == places[None, :, None]
        listed = jnp.sum(jnp.where(hit, place_in[:, None, :] + 1, 0), axis=2).reshape(-1) - 1
        slot = my_rank - step * room
        inside = (slot >= 0) & (slot < room)
        return listed, jnp.where(inside, my_source * room + slot, -1)

    out_list, in_slots = maps_out(0)

    def more_dealt(carry):
        step, total = carry
        out_more, in_more = maps_out(step)
        given = jnp.concatenate([tokens, cotangent], axis=1)
        return step + 1, total + exchange(given, out_more, in_more)

    host = row_index // (row_count // 2)
    expert = col_index * local_count + host

    def chosen(group_routes, group_gates):
        named = group_routes == expert
        named_any = jnp.any(named, axis=1)
        running = jnp.cumsum(named_any.astype(jnp.int32))
        place = jnp.where(named_any, running - 1, -1)
        pick = place[None, :] == jnp.arange(capacity, dtype=jnp.int32)[:, None]
        token_weight = jnp.sum(jnp.where(named, group_gates, 0.0), axis=1)
        return pick.astype(BF16), jnp.sum(jnp.where(pick, token_weight[None, :], 0.0), axis=1)

    document, position = documents(doc_lengths[0], group_rows)

    rows_in, dim = w_query.shape[0], w_query.shape[0] * row_count
    wide = attn_gain.shape[0]
    slice_width = tokens.shape[1]
    more = lax.while_loop(
        lambda carry: carry[0] < rounds,
        more_dealt,
        (jnp.int32(1), jnp.zeros((group_rows, 2 * slice_width), BF16)),
    )[1]
    dealt_x = exchange(tokens, out_list, in_slots) + more[:, :slice_width]
    dealt_x, mate_routes, mate_gates = after((dealt_x, mate(routes), mate(gate_weights)), ())
    routes_late, gates_late = after((routes, gate_weights), (dealt_x,))
    pick, weight = chosen(routes_late, gates_late)
    mate_pick, mate_weight = chosen(mate_routes, mate_gates)
    full_x = cube_gather(dealt_x, 1)

    query_width = w_query.shape[1]
    lat_rows = rows_in // col_count
    w_latent_s = lax.dynamic_slice_in_dim(w_latent, col_index * lat_rows, lat_rows, 0)
    lat_wide = w_latent.shape[1]
    first_s = jnp.concatenate(
        [
            w_query,
            w_latent_s.reshape(-1, query_width),
            jnp.concatenate([attn_gain, ffn_gain, latent_gain]).reshape(-1, query_width),
        ],
        axis=0,
    )
    first_s = jnp.pad(first_s, ((0, -first_s.shape[0] % 16), (0, 0)))
    (first_s,) = after((first_s,), (dealt_x,))
    first_w = row_gather(first_s[None], 0)
    query_w = first_w[:, :rows_in].reshape(dim, query_width)
    lat_end = rows_in + lat_rows * lat_wide // query_width
    latent_w = cube_gather(first_w[:, rows_in:lat_end].reshape(row_count * lat_rows, lat_wide), 0)
    latent_w = latent_w.reshape(col_count, row_count, lat_rows, lat_wide).transpose(1, 0, 2, 3)
    latent_w = latent_w.reshape(dim, lat_wide)
    gains = first_w[:, lat_end:].reshape(row_count, -1)
    gain_one = gains[:, :wide].reshape(-1).astype(F32)
    gain_two = gains[:, wide : 2 * wide].reshape(-1).astype(F32)
    latent_g = gains[:, 2 * wide : 2 * wide + latent_gain.shape[0]].reshape(-1).astype(F32)

    (cotangent_s,) = after((cotangent,), (dealt_x,))
    dealt_dy = exchange(cotangent_s, out_list, in_slots) + more[:, slice_width:]
    both_dy = cube_gather(jnp.concatenate([dealt_dy, mate(dealt_dy)], axis=0), 1)
    full_dy, mate_dy = both_dy[:group_rows], both_dy[group_rows:]

    out_rows = w_output.shape[0]
    rest_s = jnp.concatenate([w_output.reshape(-1, w_expand.shape[1]), w_expand])
    (rest_s,) = after((rest_s,), (dealt_x,))
    rest_w = row_gather(rest_s[None], 0)
    out_count = w_output.size // w_expand.shape[1]
    output_w = rest_w[:, :out_count].reshape(row_count, out_rows, -1)
    output_w = output_w.transpose(1, 0, 2).reshape(out_rows, dim)
    expand_w = rest_w[:, out_count:].reshape(-1, w_expand.shape[1])

    (shared_gu_s,) = after((jnp.concatenate([shared_gate, shared_up], axis=1),), (first_w,))
    shared_gu_w = row_gather(shared_gu_s, 0)
    (shared_d_s,) = after((shared_down,), (rest_w,))
    shared_d_w = row_gather(shared_d_s, 1)

    def of_expert(value, number):
        return lax.dynamic_index_in_dim(value, number, 0, False)

    def both_parts(number):
        return jnp.concatenate([of_expert(expert_gate, number), of_expert(expert_up, number)], 1)

    kept, given = after((both_parts(host), both_parts(1 - host)), (dealt_dy,))
    gate_up_w = expert_gather(kept, given, 0)
    kept, given = after((of_expert(expert_down, host), of_expert(expert_down, 1 - host)), (dealt_dy,))
    down_w = expert_gather(kept, given, 1)

    head_count = query_w.shape[1] // (NOPE + ROPE)
    softmax_scale = (NOPE + ROPE) ** (-0.5)
    block_rows = min(512, group_rows)
    row_number = token_ids
    residual = full_x.astype(F32)
    scale_one = lax.rsqrt(jnp.mean(residual * residual, axis=-1, keepdims=True) + EPSILON)
    normed_one = (residual * scale_one * gain_one).astype(BF16)
    query_raw = dot(normed_one, query_w)
    query_raw = query_raw.reshape(group_rows, head_count, NOPE + ROPE)
    query_heads = jnp.concatenate(
        [query_raw[..., :NOPE], rotate(query_raw[..., NOPE:], position, 1.0)], axis=-1
    ).astype(BF16)
    latent = dot(normed_one, latent_w)
    latent_front = latent[:, :LAT]
    scale_lat = lax.rsqrt(jnp.mean(latent_front * latent_front, axis=-1, keepdims=True) + EPSILON)
    unit_lat = latent_front * scale_lat
    compressed = (unit_lat * latent_g).astype(BF16)
    rope_key = rotate(latent[:, LAT:], position, 1.0).astype(BF16)
    expanded = dot(compressed, expand_w).astype(BF16)
    expanded = expanded.reshape(group_rows, head_count, NOPE + VDIM)
    key_heads = jnp.concatenate(
        [
            expanded[..., :NOPE],
            jnp.broadcast_to(rope_key[:, None, :], (group_rows, head_count, ROPE)),
        ],
        axis=-1,
    )
    value_heads = expanded[..., NOPE:]

    def block_scores(first_row, last_row):
        raw_scores = (
            jnp.einsum(
                "qhd,khd->hqk",
                query_heads[first_row:last_row],
                key_heads[:last_row],
                preferred_element_type=F32,
            )
            * softmax_scale
        )
        allowed = (document[first_row:last_row, None] == document[None, :last_row]) & (
            row_number[first_row:last_row, None] >= row_number[None, :last_row]
        )
        return jnp.where(allowed[None], raw_scores, -1e30)

    mixed_blocks = []
    lse_blocks = []
    for first_row in range(0, group_rows, block_rows):
        last_row = first_row + block_rows
        scores = block_scores(first_row, last_row)
        row_top = jnp.max(scores, axis=-1, keepdims=True)
        exp_scores = jnp.exp(scores - row_top)
        row_total = jnp.sum(exp_scores, axis=-1, keepdims=True)
        probs_low = (exp_scores / row_total).astype(BF16)
        lse_blocks.append(row_top[..., 0] + jnp.log(row_total[..., 0]))
        mixed_blocks.append(
            jnp.einsum(
                "hqk,khd->qhd",
                probs_low,
                value_heads[:last_row],
                preferred_element_type=F32,
            )
        )
    mixed = (
        jnp.concatenate(mixed_blocks, axis=0).reshape(group_rows, head_count * VDIM).astype(BF16)
    )
    attn_part = cube_scatter(dot(mixed, output_w).astype(BF16))
    x_part = my_part(full_x).astype(F32)
    hidden_part = x_part + attn_part
    scale_two = lax.rsqrt(jnp.mean(hidden_part * hidden_part, axis=-1, keepdims=True) + EPSILON)
    unit_two = hidden_part * scale_two
    normed_part = (unit_two * gain_two).astype(BF16)
    mate_part = mate(normed_part)
    normed_two = cube_gather(normed_part, 0)
    (mate_part,) = after((mate_part,), (normed_two,))
    mate_two = cube_gather(mate_part, 0)

    place_late, rank_late, here_late, source_late, my_rank_late = after(
        (place_in, rank_here, from_here, my_source, my_rank), (normed_part,)
    )
    hit = (place_late[:, :, None] == token_ids[None, None, :]) & here_late[:, :, None]
    rank_of = jnp.sum(jnp.where(hit, rank_late[:, :, None], 0), axis=(0, 1))
    groups = jnp.arange(row_count, dtype=jnp.int32)
    group_of = jnp.sum(jnp.where(hit, groups[:, None, None], 0), axis=(0, 1))

    def maps_back(step):
        places = step * room + jnp.arange(room, dtype=jnp.int32)
        hit = (my_rank_late[None, None, :] == places[None, :, None]) & (
            source_late[None, None, :] == groups[:, None, None]
        )
        listed = jnp.sum(jnp.where(hit, token_ids[None, None, :] + 1, 0), axis=2).reshape(-1) - 1
        slot = rank_of - step * room
        inside = (slot >= 0) & (slot < room)
        return listed, jnp.where(inside, group_of * room + slot, -1)

    back_list, back_slots = maps_back(0)
    gate_up_w, back_list, back_slots = after((gate_up_w, back_list, back_slots), ())

    def forward(rows, gate_up_w):
        width = gate_up_w.shape[1] // 2
        gate_up = dot(rows, gate_up_w)
        gate_out, up_out = gate_up[:, :width], gate_up[:, width:]
        act, slope = silu_parts(gate_out)
        hidden = (act * up_out).astype(BF16)
        return hidden, act, up_out * slope

    def backward(grad_hidden, act, up_slope):
        return jnp.concatenate(
            [(grad_hidden * up_slope).astype(BF16), (grad_hidden * act).astype(BF16)], axis=1
        )

    ordered = []

    def queued_sum(value, axis):
        ordered.append(row_scatter(value.astype(BF16), axis))
        return ordered[-1]

    shared_hidden, shared_act, shared_us = forward(normed_two, shared_gu_w)
    grad_shared_gu = backward(dot_nt(full_dy, shared_d_w), shared_act, shared_us)
    grad_two = dot_nt(grad_shared_gu, shared_gu_w)
    moe_terms = dot(shared_hidden, shared_d_w)
    grad_sgu = queued_sum(dot_tn(normed_two, grad_shared_gu), 0)
    grad_sd = queued_sum(dot_tn(shared_hidden, full_dy), 1)

    rows = jnp.concatenate(
        [dot(pick, normed_two).astype(BF16), dot(mate_pick, mate_two).astype(BF16)], axis=0
    )
    grad_result = jnp.concatenate(
        [
            (weight[:, None] * dot(pick, full_dy)).astype(BF16),
            (mate_weight[:, None] * dot(mate_pick, mate_dy)).astype(BF16),
        ],
        axis=0,
    )
    hidden, act, up_slope = forward(rows, gate_up_w)
    grad_gate_up = backward(dot_nt(grad_result, down_w), act, up_slope)
    mate_rows = dot_nt(grad_gate_up[capacity:], gate_up_w).astype(BF16)
    mate_grad = dot_tn(mate_pick, mate_rows).astype(BF16)
    (own_gate_up,) = after((grad_gate_up[:capacity],), (mate_grad,))
    own_rows = dot_nt(own_gate_up, gate_up_w).astype(BF16)
    grad_two = (grad_two + dot_tn(pick, own_rows)).astype(BF16)
    mate_grad = mate(cube_scatter(mate_grad).astype(BF16))
    grad_gu = dot_tn(rows, grad_gate_up).astype(BF16)
    grad_down = dot_tn(hidden, grad_result).astype(BF16)

    grad_two_part = cube_scatter(grad_two) + mate_grad.astype(F32)
    dy_part = my_part(full_dy).astype(F32)
    hidden_back, gain_two_grad = norm_back(grad_two_part, unit_two, scale_two, gain_two)
    grad_hidden_part = dy_part + hidden_back
    grad_attn = cube_gather(grad_hidden_part.astype(BF16), 0)

    (hidden_late,) = after((hidden,), (grad_two,))
    weights = jnp.concatenate([weight, mate_weight])
    result_rows = (weights[:, None] * dot(hidden_late, down_w)).astype(BF16)
    mate_terms = dot_tn(mate_pick, result_rows[capacity:]).astype(BF16)
    moe_terms = (moe_terms + dot_tn(pick, result_rows[:capacity])).astype(BF16)
    mate_terms, moe_terms = after((mate_terms, moe_terms), (grad_attn,))
    mate_terms = mate(cube_scatter(mate_terms).astype(BF16))
    moe_part = cube_scatter(moe_terms) + mate_terms.astype(F32)
    result_part = (hidden_part + moe_part).astype(BF16)
    result_slice = lax.all_to_all(result_part, "col", split_axis=1, concat_axis=0, tiled=True)
    result = exchange(result_slice, back_list, back_slots)

    grad_output_w = queued_sum(dot_tn(mixed, grad_attn), 1)
    grad_mixed = dot_nt(grad_attn, output_w).astype(BF16)
    grad_mixed = grad_mixed.reshape(group_rows, head_count, VDIM)
    grad_query_blocks = []
    grad_keys = jnp.zeros((group_rows, head_count, NOPE + ROPE), F32)
    grad_values = jnp.zeros((group_rows, head_count, VDIM), F32)
    for block_number, first_row in enumerate(range(0, group_rows, block_rows)):
        last_row = first_row + block_rows
        scores = block_scores(first_row, last_row)
        probs_f = jnp.exp(scores - lse_blocks[block_number][..., None])
        probs_low = probs_f.astype(BF16)
        grad_block = grad_mixed[first_row:last_row]
        grad_probs = jnp.einsum(
            "qhd,khd->hqk", grad_block, value_heads[:last_row], preferred_element_type=F32
        )
        row_inner = jnp.sum(probs_f * grad_probs, axis=-1, keepdims=True)
        grad_scores = (probs_f * (grad_probs - row_inner)).astype(BF16)
        grad_values = grad_values.at[:last_row].add(
            jnp.einsum("hqk,qhd->khd", probs_low, grad_block, preferred_element_type=F32)
        )
        grad_query_blocks.append(
            softmax_scale
            * jnp.einsum(
                "hqk,khd->qhd", grad_scores, key_heads[:last_row], preferred_element_type=F32
            )
        )
        grad_keys = grad_keys.at[:last_row].add(
            softmax_scale
            * jnp.einsum(
                "hqk,qhd->khd",
                grad_scores,
                query_heads[first_row:last_row],
                preferred_element_type=F32,
            )
        )
    grad_query = jnp.concatenate(grad_query_blocks, axis=0)
    grad_query_raw = (
        jnp.concatenate(
            [grad_query[..., :NOPE], rotate(grad_query[..., NOPE:], position, -1.0)], axis=-1
        )
        .astype(BF16)
        .reshape(group_rows, head_count * (NOPE + ROPE))
    )
    own_gu, mate_gu = expert_scatter(grad_gu, 0)
    own_down, mate_down = expert_scatter(grad_down, 1)
    grad_query_raw, mate_gu = after((grad_query_raw, mate_gu), ())
    grad_one = cube_scatter(dot_nt(grad_query_raw, query_w).astype(BF16))
    grad_expanded = jnp.concatenate([grad_keys[..., :NOPE], grad_values], axis=-1).astype(BF16)
    grad_expanded = grad_expanded.reshape(group_rows, head_count * (NOPE + VDIM))
    grad_compressed = dot_nt(grad_expanded, expand_w)
    grad_rope_key = rotate(jnp.sum(grad_keys[..., NOPE:], axis=1), position, -1.0)
    grad_latent_part = cube_scatter(
        jnp.concatenate([grad_compressed, grad_rope_key], axis=1).astype(BF16)
    )
    grad_front, latent_gain_grad = norm_back(
        grad_latent_part[:, :LAT], my_part(unit_lat), my_part(scale_lat), latent_g
    )
    grad_latent_part = jnp.concatenate([grad_front, grad_latent_part[:, LAT:]], axis=1).astype(BF16)
    latent_term = dot_nt(grad_latent_part, latent_w)
    grad_one = grad_one + latent_term
    scale_one_part = my_part(scale_one)
    input_back, gain_one_grad = norm_back(
        grad_one, x_part * scale_one_part, scale_one_part, gain_one
    )
    grad_input = (grad_hidden_part + input_back).astype(BF16)
    grad_slice = lax.all_to_all(grad_input, "col", split_axis=1, concat_axis=0, tiled=True)
    tokens_grad = exchange(grad_slice, back_list, back_slots)

    def more_back(carry):
        step, total = carry
        back_more, slots_more = maps_back(step)
        dealt = jnp.concatenate([result_slice, grad_slice], axis=1)
        return step + 1, total + exchange(dealt, back_more, slots_more)

    more = lax.while_loop(
        lambda carry: carry[0] < rounds,
        more_back,
        (jnp.int32(1), jnp.concatenate([result, tokens_grad], axis=1)),
    )[1]
    result, tokens_grad = more[:, :slice_width], more[:, slice_width:]

    grad_expand_w = queued_sum(dot_tn(compressed, grad_expanded), 0)
    grad_query_w = queued_sum(dot_tn(normed_one, grad_query_raw), 0)
    grad_latent = cube_gather(grad_latent_part, 0)
    my_columns = lax.dynamic_index_in_dim(
        normed_one.reshape(group_rows, row_count, col_count, lat_rows), col_index, 2, False
    ).reshape(group_rows, row_count * lat_rows)
    grad_latent_w = cube_gather(queued_sum(dot_tn(my_columns, grad_latent), 0), 0)
    gain_grads = small_sum(jnp.concatenate([gain_one_grad, gain_two_grad, latent_gain_grad]))
    width_ff = expert_gate.shape[2]
    other_gu, other_down = mate(mate_gu), mate(mate_down)

    def in_order(own, other):
        return jnp.stack([jnp.where(host == 0, own, other), jnp.where(host == 0, other, own)])

    width_two = gain_one_grad.shape[0]
    width_lat = latent_gain_grad.shape[0]

    def my_rows(value):
        width = value.shape[0] // row_count
        return lax.dynamic_slice_in_dim(value, row_index * width, width, 0)

    return (
        result,
        tokens_grad,
        my_rows(gain_grads[:width_two]),
        grad_query_w.astype(F32),
        grad_latent_w.astype(F32),
        my_rows(gain_grads[2 * width_two : 2 * width_two + width_lat]),
        grad_expand_w.astype(F32),
        grad_output_w.astype(F32),
        my_rows(gain_grads[width_two : 2 * width_two]),
        grad_sgu[:, : shared_gate.shape[1]].astype(F32),
        grad_sgu[:, shared_gate.shape[1] :].astype(F32),
        grad_sd.astype(F32),
        in_order(own_gu[:, :width_ff], other_gu[:, :width_ff]).astype(F32),
        in_order(own_gu[:, width_ff:], other_gu[:, width_ff:]).astype(F32),
        in_order(own_down, other_down).astype(F32),
    )


def solution(mesh):
    return jax.shard_map(
        body,
        mesh=mesh,
        in_specs=(
            P("row", "col"),
            P("row", "col"),
            P(),
            P("row", None),
            P("row", None),
            P("row", None),
            P("row"),
            P("row", "col"),
            P("row", None),
            P("row"),
            P("row", "col"),
            P("col", "row"),
            P("row"),
            P("row", "col"),
            P("row", "col"),
            P("col", "row"),
            P("col", "row", None),
            P("col", "row", None),
            P("col", None, "row"),
        ),
        out_specs=(
            P("row", "col"),
            P("row", "col"),
            P("row"),
            P("row", "col"),
            P("row", None),
            P("row"),
            P("row", "col"),
            P("col", "row"),
            P("row"),
            P("row", "col"),
            P("row", "col"),
            P("col", "row"),
            P("col", "row", None),
            P("col", "row", None),
            P("col", None, "row"),
        ),
        check_vma=False,
    )
```

```python
import jax
import jax.numpy as jnp
from jax import lax
from jax.experimental.layout import Layout, with_layout_constraint
from jax.sharding import PartitionSpec as P

NOPE = 128
ROPE = 64
VDIM = 128
LAT = 512
TOPK = 6

EPSILON = 1e-06
F32 = jnp.float32
BF16 = jnp.bfloat16


def rotate(value, position, orient):
    half_width = value.shape[-1] // 2
    frequency = 10000.0 ** (-jnp.arange(half_width, dtype=F32) / half_width)
    angles = position.astype(F32)[:, None] * frequency[None, :]
    shape_out = (value.shape[0],) + (1,) * (value.ndim - 2) + (half_width,)
    cosine = jnp.cos(angles).reshape(shape_out)
    sine_part = jnp.sin(angles).reshape(shape_out)
    first_half = value[..., :half_width]
    second = value[..., half_width:]
    return jnp.concatenate(
        [
            first_half * cosine - orient * second * sine_part,
            second * cosine + orient * first_half * sine_part,
        ],
        axis=-1,
    )


def documents(lengths_row, row_count):
    doc_ends = jnp.cumsum(lengths_row)
    starts = doc_ends - lengths_row
    row_number = jnp.arange(row_count, dtype=jnp.int32)
    document = jnp.sum((row_number[:, None] >= doc_ends[None, :]).astype(jnp.int32), axis=1)
    onehot = document[:, None] == jnp.arange(lengths_row.shape[0], dtype=jnp.int32)[None, :]
    position = row_number - jnp.sum(jnp.where(onehot, starts[None, :], 0), axis=1)
    return (document, position)


def silu_parts(value):
    sigmoid_value = jax.nn.sigmoid(value)
    activation = value * sigmoid_value
    activ_slope = sigmoid_value * (1.0 + value * (1.0 - sigmoid_value))
    return (activation, activ_slope)


def norm_back(grad_normed, unit_rows, row_scale, gain_vector):
    scaled = grad_normed * gain_vector
    row_inner = jnp.mean(scaled * unit_rows, axis=-1, keepdims=True)
    return (row_scale * (scaled - unit_rows * row_inner), jnp.sum(grad_normed * unit_rows, axis=0))


def dot(left, right):
    return jnp.dot(left, right, preferred_element_type=F32)


def dot_nt(left, right):
    return lax.dot_general(left, right, (((1,), (1,)), ((), ())), preferred_element_type=F32)


def dot_tn(left, right):
    return lax.dot_general(left, right, (((0,), (0,)), ((), ())), preferred_element_type=F32)


def row_major(value):
    return with_layout_constraint(value, Layout(tuple(range(value.ndim))))


def row_swap(value, bit):
    return lax.ppermute(value, "row", [(j, j ^ bit) for j in range(lax.axis_size("row"))])


def mate(value):
    return row_swap(value, lax.axis_size("row") // 2)


def half_bits():
    return [1 << b for b in range((lax.axis_size("row") // 2).bit_length() - 1)]


def expert_gather(kept, given, axis):
    count = lax.axis_size("row")
    index = lax.axis_index("row")
    width = kept.shape[axis]
    shape = list(kept.shape)
    shape[axis] = width * count
    out = jnp.zeros(shape, kept.dtype)
    for first, item in ((0, kept), (count // 2, mate(given))):
        items = {first: item}
        for bit in half_bits():
            items.update({key ^ bit: row_swap(items[key], bit) for key in list(items)})
        for key, piece in items.items():
            out = lax.dynamic_update_slice_in_dim(
                out, piece, jnp.bitwise_xor(index, key) * width, axis
            )
    return out


def expert_scatter(value, axis):
    count = lax.axis_size("row")
    index = lax.axis_index("row")
    width = value.shape[axis] // count
    sums = []
    for first in (count // 2, 0):
        items = {
            key: lax.dynamic_slice_in_dim(
                value, jnp.bitwise_xor(index, key ^ first) * width, width, axis
            )
            for key in range(count // 2)
        }
        for bit in half_bits()[::-1]:
            items = {
                key: (
                    items[key].astype(F32) + row_swap(items[key ^ bit], bit).astype(F32)
                ).astype(BF16)
                for key in items
                if key < bit
            }
        sums.append(items[0])
    return sums[1], sums[0]


def swap(value, bit):
    return lax.ppermute(value, "col", [(j, j ^ bit) for j in range(lax.axis_size("col"))])


def chip_bits():
    return [1 << b for b in range(1, (lax.axis_size("col") - 1).bit_length())]


def chip_swap(value, step):
    bits = chip_bits()
    other = bits[::-1]
    return lax.ppermute(
        value,
        "col",
        [(j, j ^ (other if j % 2 else bits)[step]) for j in range(lax.axis_size("col"))],
    )


def block_at(device, place):
    bits = chip_bits()
    even = sum(bit for n, bit in enumerate(bits) if place >> n & 1)
    odd = sum(bit for n, bit in enumerate(bits[::-1]) if place >> n & 1)
    return jnp.bitwise_xor(device, jnp.where(device % 2 == 0, even, odd))


def cube_gather(block, axis):
    count = lax.axis_size("col")
    index = lax.axis_index("col")
    width = block.shape[axis]
    shape = list(block.shape)
    shape[axis] = width * count
    out = jnp.zeros(shape, block.dtype)
    held = row_major(block)[None]
    sibling = jnp.bitwise_xor(index, 1)
    done = 0
    for step in range(len(chip_bits()) + 1):
        theirs = swap(held[done:], 1)
        for place in range(done, held.shape[0]):
            for item, owner in ((held[place], index), (theirs[place - done], sibling)):
                out = lax.dynamic_update_slice_in_dim(
                    out, item, block_at(owner, place) * width, axis
                )
        done = held.shape[0]
        if step < len(chip_bits()):
            held = jnp.concatenate([held, chip_swap(held, step)], axis=0)
    return out


def cube_scatter(value, axis=0):
    count = lax.axis_size("col")
    index = lax.axis_index("col")
    rows = value.shape[axis] // count
    value = row_major(value)

    def blocks(device):
        return jnp.stack(
            [
                lax.dynamic_slice_in_dim(value, block_at(device, place) * rows, rows, axis)
                for place in range(count // 2)
            ]
        )

    got = swap(blocks(jnp.bitwise_xor(index, 1)), 1)
    held = blocks(index).astype(F32) + got.astype(F32)
    for step in range(len(chip_bits()) - 1, -1, -1):
        held = held.astype(BF16)
        half = held.shape[0] // 2
        got = chip_swap(held[half:], step)
        held = held[:half].astype(F32) + got.astype(F32)
    return held[0]


def row_gather(shard, axis):
    return lax.all_gather(shard, "row", axis=axis, tiled=True)


def after(values, earlier):
    out = lax.optimization_barrier(tuple(values) + tuple(earlier))
    return out[: len(values)]


def row_scatter(value, axis):
    return lax.psum_scatter(value, "row", scatter_dimension=axis, tiled=True)


def small_sum(value):
    for bit in [1] + chip_bits():
        value = value + swap(value, bit)
    count = lax.axis_size("row")
    total = value
    for k in range(1, count):
        total = total + lax.ppermute(value, "row", [(j, (j + k) % count) for j in range(count)])
    return total


def onehot(index, width):
    return (index[:, None] == jnp.arange(width, dtype=jnp.int32)[None, :]).astype(BF16)


def exchange(value, sent_of, slot_of):
    count = lax.axis_size("row")
    sent = row_major(dot(onehot(sent_of, value.shape[0]), value).astype(BF16))
    sent = sent.reshape(count, -1, value.shape[1])
    got = lax.all_to_all(sent, "row", split_axis=0, concat_axis=0, tiled=True)
    got = got.reshape(-1, value.shape[1])
    return row_major(dot(onehot(slot_of, got.shape[0]), got).astype(BF16))


def body(
    tokens,
    cotangent,
    dealing,
    doc_lengths,
    routes,
    gate_weights,
    attn_gain,
    w_query,
    w_latent,
    latent_gain,
    w_expand,
    w_output,
    ffn_gain,
    shared_gate,
    shared_up,
    shared_down,
    expert_gate,
    expert_up,
    expert_down,
):
    group_rows = routes.shape[0]
    row_count = lax.axis_size("row")
    col_count = lax.axis_size("col")
    row_index = lax.axis_index("row")
    col_index = lax.axis_index("col")
    part_rows = group_rows // col_count
    local_count = expert_gate.shape[0]
    capacity = 4 * group_rows * TOPK // (3 * local_count * col_count)

    def my_part(value):
        return lax.dynamic_slice_in_dim(value, col_index * part_rows, part_rows, 0)

    token_ids = jnp.arange(group_rows, dtype=jnp.int32)
    room = max(16, 5 * group_rows // (16 * row_count) * 4)
    lists = dealing.reshape(row_count, group_rows)
    source = lists // group_rows
    place_in = lists - source * group_rows
    from_here = source == row_index
    rank_here = jnp.where(from_here, jnp.cumsum(from_here.astype(jnp.int32), axis=1) - 1, -1)
    my_source = lax.dynamic_index_in_dim(source, row_index, 0, False)
    by_source = my_source[None, :] == jnp.arange(row_count, dtype=jnp.int32)[:, None]
    count_in = jnp.cumsum(by_source.astype(jnp.int32), axis=1)
    my_rank = jnp.sum(jnp.where(by_source, count_in, 0), axis=0) - 1
    all_counts = jnp.sum(
        (source[:, None, :] == jnp.arange(row_count, dtype=jnp.int32)[None, :, None]).astype(
            jnp.int32
        ),
        axis=2,
    )
    rounds = (jnp.max(all_counts) + room - 1) // room

    def maps_out(step):
        places = step * room + jnp.arange(room, dtype=jnp.int32)
        hit = rank_here[:, None, :] == places[None, :, None]
        listed = jnp.sum(jnp.where(hit, place_in[:, None, :] + 1, 0), axis=2).reshape(-1) - 1
        slot = my_rank - step * room
        inside = (slot >= 0) & (slot < room)
        return listed, jnp.where(inside, my_source * room + slot, -1)

    out_list, in_slots = maps_out(0)

    def more_dealt(carry):
        step, total = carry
        out_more, in_more = maps_out(step)
        given = jnp.concatenate([tokens, cotangent], axis=1)
        return step + 1, total + exchange(given, out_more, in_more)

    host = row_index // (row_count // 2)
    expert = col_index * local_count + host

    def chosen(group_routes, group_gates):
        named = group_routes == expert
        named_any = jnp.any(named, axis=1)
        running = jnp.cumsum(named_any.astype(jnp.int32))
        place = jnp.where(named_any, running - 1, -1)
        pick = place[None, :] == jnp.arange(capacity, dtype=jnp.int32)[:, None]
        token_weight = jnp.sum(jnp.where(named, group_gates, 0.0), axis=1)
        return pick.astype(BF16), jnp.sum(jnp.where(pick, token_weight[None, :], 0.0), axis=1)

    document, position = documents(doc_lengths[0], group_rows)

    rows_in, dim = w_query.shape[0], w_query.shape[0] * row_count
    wide = attn_gain.shape[0]
    slice_width = tokens.shape[1]
    more = lax.while_loop(
        lambda carry: carry[0] < rounds,
        more_dealt,
        (jnp.int32(1), jnp.zeros((group_rows, 2 * slice_width), BF16)),
    )[1]
    dealt_x = exchange(tokens, out_list, in_slots) + more[:, :slice_width]
    dealt_x, mate_routes, mate_gates = after((dealt_x, mate(routes), mate(gate_weights)), ())
    routes_late, gates_late = after((routes, gate_weights), (dealt_x,))
    pick, weight = chosen(routes_late, gates_late)
    mate_pick, mate_weight = chosen(mate_routes, mate_gates)
    full_x = cube_gather(dealt_x, 1)

    query_width = w_query.shape[1]
    lat_rows = rows_in // col_count
    w_latent_s = lax.dynamic_slice_in_dim(w_latent, col_index * lat_rows, lat_rows, 0)
    lat_wide = w_latent.shape[1]
    first_s = jnp.concatenate(
        [
            w_query,
            w_latent_s.reshape(-1, query_width),
            jnp.concatenate([attn_gain, ffn_gain, latent_gain]).reshape(-1, query_width),
        ],
        axis=0,
    )
    first_s = jnp.pad(first_s, ((0, -first_s.shape[0] % 16), (0, 0)))
    (first_s,) = after((first_s,), (dealt_x,))
    first_w = row_gather(first_s[None], 0)
    query_w = first_w[:, :rows_in].reshape(dim, query_width)
    lat_end = rows_in + lat_rows * lat_wide // query_width
    latent_w = cube_gather(first_w[:, rows_in:lat_end].reshape(row_count * lat_rows, lat_wide), 0)
    latent_w = latent_w.reshape(col_count, row_count, lat_rows, lat_wide).transpose(1, 0, 2, 3)
    latent_w = latent_w.reshape(dim, lat_wide)
    gains = first_w[:, lat_end:].reshape(row_count, -1)
    gain_one = gains[:, :wide].reshape(-1).astype(F32)
    gain_two = gains[:, wide : 2 * wide].reshape(-1).astype(F32)
    latent_g = gains[:, 2 * wide : 2 * wide + latent_gain.shape[0]].reshape(-1).astype(F32)

    (cotangent_s,) = after((cotangent,), (dealt_x,))
    dealt_dy = exchange(cotangent_s, out_list, in_slots) + more[:, slice_width:]
    both_dy = cube_gather(jnp.concatenate([dealt_dy, mate(dealt_dy)], axis=0), 1)
    full_dy, mate_dy = both_dy[:group_rows], both_dy[group_rows:]

    out_rows = w_output.shape[0]
    rest_s = jnp.concatenate([w_output.reshape(-1, w_expand.shape[1]), w_expand])
    (rest_s,) = after((rest_s,), (dealt_x,))
    rest_w = row_gather(rest_s[None], 0)
    out_count = w_output.size // w_expand.shape[1]
    output_w = rest_w[:, :out_count].reshape(row_count, out_rows, -1)
    output_w = output_w.transpose(1, 0, 2).reshape(out_rows, dim)
    expand_w = rest_w[:, out_count:].reshape(-1, w_expand.shape[1])

    (shared_gu_s,) = after((jnp.concatenate([shared_gate, shared_up], axis=1),), (first_w,))
    shared_gu_w = row_gather(shared_gu_s, 0)
    (shared_d_s,) = after((shared_down,), (rest_w,))
    shared_d_w = row_gather(shared_d_s, 1)

    def of_expert(value, number):
        return lax.dynamic_index_in_dim(value, number, 0, False)

    def both_parts(number):
        return jnp.concatenate([of_expert(expert_gate, number), of_expert(expert_up, number)], 1)

    kept, given = after((both_parts(host), both_parts(1 - host)), (dealt_dy,))
    gate_up_w = expert_gather(kept, given, 0)
    kept, given = after((of_expert(expert_down, host), of_expert(expert_down, 1 - host)), (dealt_dy,))
    down_w = expert_gather(kept, given, 1)

    head_count = query_w.shape[1] // (NOPE + ROPE)
    softmax_scale = (NOPE + ROPE) ** (-0.5)
    block_rows = min(512, group_rows)
    row_number = token_ids
    residual = full_x.astype(F32)
    scale_one = lax.rsqrt(jnp.mean(residual * residual, axis=-1, keepdims=True) + EPSILON)
    normed_one = (residual * scale_one * gain_one).astype(BF16)
    query_raw = dot(normed_one, query_w)
    query_raw = query_raw.reshape(group_rows, head_count, NOPE + ROPE)
    query_heads = jnp.concatenate(
        [query_raw[..., :NOPE], rotate(query_raw[..., NOPE:], position, 1.0)], axis=-1
    ).astype(BF16)
    latent = dot(normed_one, latent_w)
    latent_front = latent[:, :LAT]
    scale_lat = lax.rsqrt(jnp.mean(latent_front * latent_front, axis=-1, keepdims=True) + EPSILON)
    unit_lat = latent_front * scale_lat
    compressed = (unit_lat * latent_g).astype(BF16)
    rope_key = rotate(latent[:, LAT:], position, 1.0).astype(BF16)
    expanded = dot(compressed, expand_w).astype(BF16)
    expanded = expanded.reshape(group_rows, head_count, NOPE + VDIM)
    key_heads = jnp.concatenate(
        [
            expanded[..., :NOPE],
            jnp.broadcast_to(rope_key[:, None, :], (group_rows, head_count, ROPE)),
        ],
        axis=-1,
    )
    value_heads = expanded[..., NOPE:]

    def block_scores(first_row, last_row):
        raw_scores = (
            jnp.einsum(
                "qhd,khd->hqk",
                query_heads[first_row:last_row],
                key_heads[:last_row],
                preferred_element_type=F32,
            )
            * softmax_scale
        )
        allowed = (document[first_row:last_row, None] == document[None, :last_row]) & (
            row_number[first_row:last_row, None] >= row_number[None, :last_row]
        )
        return jnp.where(allowed[None], raw_scores, -1e30)

    mixed_blocks = []
    lse_blocks = []
    for first_row in range(0, group_rows, block_rows):
        last_row = first_row + block_rows
        scores = block_scores(first_row, last_row)
        row_top = jnp.max(scores, axis=-1, keepdims=True)
        exp_scores = jnp.exp(scores - row_top)
        row_total = jnp.sum(exp_scores, axis=-1, keepdims=True)
        probs_low = (exp_scores / row_total).astype(BF16)
        lse_blocks.append(row_top[..., 0] + jnp.log(row_total[..., 0]))
        mixed_blocks.append(
            jnp.einsum(
                "hqk,khd->qhd",
                probs_low,
                value_heads[:last_row],
                preferred_element_type=F32,
            )
        )
    mixed = (
        jnp.concatenate(mixed_blocks, axis=0).reshape(group_rows, head_count * VDIM).astype(BF16)
    )
    attn_part = cube_scatter(dot(mixed, output_w).astype(BF16))
    x_part = my_part(full_x).astype(F32)
    hidden_part = x_part + attn_part
    scale_two = lax.rsqrt(jnp.mean(hidden_part * hidden_part, axis=-1, keepdims=True) + EPSILON)
    unit_two = hidden_part * scale_two
    normed_part = (unit_two * gain_two).astype(BF16)
    mate_part = mate(normed_part)
    normed_two = cube_gather(normed_part, 0)
    (mate_part,) = after((mate_part,), (normed_two,))
    mate_two = cube_gather(mate_part, 0)

    place_late, rank_late, here_late, source_late, my_rank_late = after(
        (place_in, rank_here, from_here, my_source, my_rank), (normed_part,)
    )
    hit = (place_late[:, :, None] == token_ids[None, None, :]) & here_late[:, :, None]
    rank_of = jnp.sum(jnp.where(hit, rank_late[:, :, None], 0), axis=(0, 1))
    groups = jnp.arange(row_count, dtype=jnp.int32)
    group_of = jnp.sum(jnp.where(hit, groups[:, None, None], 0), axis=(0, 1))

    def maps_back(step):
        places = step * room + jnp.arange(room, dtype=jnp.int32)
        hit = (my_rank_late[None, None, :] == places[None, :, None]) & (
            source_late[None, None, :] == groups[:, None, None]
        )
        listed = jnp.sum(jnp.where(hit, token_ids[None, None, :] + 1, 0), axis=2).reshape(-1) - 1
        slot = rank_of - step * room
        inside = (slot >= 0) & (slot < room)
        return listed, jnp.where(inside, group_of * room + slot, -1)

    back_list, back_slots = maps_back(0)
    gate_up_w, back_list, back_slots = after((gate_up_w, back_list, back_slots), ())

    def forward(rows, gate_up_w):
        width = gate_up_w.shape[1] // 2
        gate_up = dot(rows, gate_up_w)
        gate_out, up_out = gate_up[:, :width], gate_up[:, width:]
        act, slope = silu_parts(gate_out)
        hidden = (act * up_out).astype(BF16)
        return hidden, act, up_out * slope

    def backward(grad_hidden, act, up_slope):
        return jnp.concatenate(
            [(grad_hidden * up_slope).astype(BF16), (grad_hidden * act).astype(BF16)], axis=1
        )

    ordered = []

    def queued_sum(value, axis):
        ordered.append(row_scatter(value.astype(BF16), axis))
        return ordered[-1]

    shared_hidden, shared_act, shared_us = forward(normed_two, shared_gu_w)
    grad_shared_gu = backward(dot_nt(full_dy, shared_d_w), shared_act, shared_us)
    grad_two = dot_nt(grad_shared_gu, shared_gu_w)
    moe_terms = dot(shared_hidden, shared_d_w)
    grad_sgu = queued_sum(dot_tn(normed_two, grad_shared_gu), 0)
    grad_sd = queued_sum(dot_tn(shared_hidden, full_dy), 1)

    rows = jnp.concatenate(
        [dot(pick, normed_two).astype(BF16), dot(mate_pick, mate_two).astype(BF16)], axis=0
    )
    grad_result = jnp.concatenate(
        [
            (weight[:, None] * dot(pick, full_dy)).astype(BF16),
            (mate_weight[:, None] * dot(mate_pick, mate_dy)).astype(BF16),
        ],
        axis=0,
    )
    hidden, act, up_slope = forward(rows, gate_up_w)
    grad_gate_up = backward(dot_nt(grad_result, down_w), act, up_slope)
    mate_rows = dot_nt(grad_gate_up[capacity:], gate_up_w).astype(BF16)
    mate_grad = dot_tn(mate_pick, mate_rows).astype(BF16)
    (own_gate_up,) = after((grad_gate_up[:capacity],), (mate_grad,))
    own_rows = dot_nt(own_gate_up, gate_up_w).astype(BF16)
    grad_two = (grad_two + dot_tn(pick, own_rows)).astype(BF16)
    mate_grad = mate(cube_scatter(mate_grad).astype(BF16))
    grad_gu = dot_tn(rows, grad_gate_up).astype(BF16)
    grad_down = dot_tn(hidden, grad_result).astype(BF16)

    grad_two_part = cube_scatter(grad_two) + mate_grad.astype(F32)
    dy_part = my_part(full_dy).astype(F32)
    hidden_back, gain_two_grad = norm_back(grad_two_part, unit_two, scale_two, gain_two)
    grad_hidden_part = dy_part + hidden_back
    grad_attn = cube_gather(grad_hidden_part.astype(BF16), 0)

    (hidden_late,) = after((hidden,), (grad_two,))
    weights = jnp.concatenate([weight, mate_weight])
    result_rows = (weights[:, None] * dot(hidden_late, down_w)).astype(BF16)
    mate_terms = dot_tn(mate_pick, result_rows[capacity:]).astype(BF16)
    moe_terms = (moe_terms + dot_tn(pick, result_rows[:capacity])).astype(BF16)
    mate_terms, moe_terms = after((mate_terms, moe_terms), (grad_attn,))
    both_terms = cube_scatter(jnp.stack([moe_terms, mate_terms]), 1)
    moe_part = both_terms[0] + mate(both_terms[1].astype(BF16)).astype(F32)
    result_part = (hidden_part + moe_part).astype(BF16)
    result_slice = lax.all_to_all(result_part, "col", split_axis=1, concat_axis=0, tiled=True)
    result = exchange(result_slice, back_list, back_slots)

    grad_output_w = queued_sum(dot_tn(mixed, grad_attn), 1)
    grad_mixed = dot_nt(grad_attn, output_w).astype(BF16)
    grad_mixed = grad_mixed.reshape(group_rows, head_count, VDIM)
    grad_query_blocks = []
    grad_keys = jnp.zeros((group_rows, head_count, NOPE + ROPE), F32)
    grad_values = jnp.zeros((group_rows, head_count, VDIM), F32)
    for block_number, first_row in enumerate(range(0, group_rows, block_rows)):
        last_row = first_row + block_rows
        scores = block_scores(first_row, last_row)
        probs_f = jnp.exp(scores - lse_blocks[block_number][..., None])
        probs_low = probs_f.astype(BF16)
        grad_block = grad_mixed[first_row:last_row]
        grad_probs = jnp.einsum(
            "qhd,khd->hqk", grad_block, value_heads[:last_row], preferred_element_type=F32
        )
        row_inner = jnp.sum(probs_f * grad_probs, axis=-1, keepdims=True)
        grad_scores = (probs_f * (grad_probs - row_inner)).astype(BF16)
        grad_values = grad_values.at[:last_row].add(
            jnp.einsum("hqk,qhd->khd", probs_low, grad_block, preferred_element_type=F32)
        )
        grad_query_blocks.append(
            softmax_scale
            * jnp.einsum(
                "hqk,khd->qhd", grad_scores, key_heads[:last_row], preferred_element_type=F32
            )
        )
        grad_keys = grad_keys.at[:last_row].add(
            softmax_scale
            * jnp.einsum(
                "hqk,qhd->khd",
                grad_scores,
                query_heads[first_row:last_row],
                preferred_element_type=F32,
            )
        )
    grad_query = jnp.concatenate(grad_query_blocks, axis=0)
    grad_query_raw = (
        jnp.concatenate(
            [grad_query[..., :NOPE], rotate(grad_query[..., NOPE:], position, -1.0)], axis=-1
        )
        .astype(BF16)
        .reshape(group_rows, head_count * (NOPE + ROPE))
    )
    own_gu, mate_gu = expert_scatter(grad_gu, 0)
    own_down, mate_down = expert_scatter(grad_down, 1)
    grad_one = cube_scatter(dot_nt(grad_query_raw, query_w).astype(BF16))
    grad_expanded = jnp.concatenate([grad_keys[..., :NOPE], grad_values], axis=-1).astype(BF16)
    grad_expanded = grad_expanded.reshape(group_rows, head_count * (NOPE + VDIM))
    grad_compressed = dot_nt(grad_expanded, expand_w)
    grad_rope_key = rotate(jnp.sum(grad_keys[..., NOPE:], axis=1), position, -1.0)
    grad_latent_part = cube_scatter(
        jnp.concatenate([grad_compressed, grad_rope_key], axis=1).astype(BF16)
    )
    grad_front, latent_gain_grad = norm_back(
        grad_latent_part[:, :LAT], my_part(unit_lat), my_part(scale_lat), latent_g
    )
    grad_latent_part = jnp.concatenate([grad_front, grad_latent_part[:, LAT:]], axis=1).astype(BF16)
    latent_term = dot_nt(grad_latent_part, latent_w)
    grad_one = grad_one + latent_term
    scale_one_part = my_part(scale_one)
    input_back, gain_one_grad = norm_back(
        grad_one, x_part * scale_one_part, scale_one_part, gain_one
    )
    grad_input = (grad_hidden_part + input_back).astype(BF16)
    grad_slice = lax.all_to_all(grad_input, "col", split_axis=1, concat_axis=0, tiled=True)
    tokens_grad = exchange(grad_slice, back_list, back_slots)

    def more_back(carry):
        step, total = carry
        back_more, slots_more = maps_back(step)
        dealt = jnp.concatenate([result_slice, grad_slice], axis=1)
        return step + 1, total + exchange(dealt, back_more, slots_more)

    more = lax.while_loop(
        lambda carry: carry[0] < rounds,
        more_back,
        (jnp.int32(1), jnp.concatenate([result, tokens_grad], axis=1)),
    )[1]
    result, tokens_grad = more[:, :slice_width], more[:, slice_width:]

    grad_expand_w = queued_sum(dot_tn(compressed, grad_expanded), 0)
    grad_query_w = queued_sum(dot_tn(normed_one, grad_query_raw), 0)
    grad_latent = cube_gather(grad_latent_part, 0)
    my_columns = lax.dynamic_index_in_dim(
        normed_one.reshape(group_rows, row_count, col_count, lat_rows), col_index, 2, False
    ).reshape(group_rows, row_count * lat_rows)
    grad_latent_w = cube_gather(queued_sum(dot_tn(my_columns, grad_latent), 0), 0)
    gain_grads = small_sum(jnp.concatenate([gain_one_grad, gain_two_grad, latent_gain_grad]))
    width_ff = expert_gate.shape[2]
    other_gu, other_down = mate(mate_gu), mate(mate_down)

    def in_order(own, other):
        return jnp.stack([jnp.where(host == 0, own, other), jnp.where(host == 0, other, own)])

    width_two = gain_one_grad.shape[0]
    width_lat = latent_gain_grad.shape[0]

    def my_rows(value):
        width = value.shape[0] // row_count
        return lax.dynamic_slice_in_dim(value, row_index * width, width, 0)

    return (
        result,
        tokens_grad,
        my_rows(gain_grads[:width_two]),
        grad_query_w.astype(F32),
        grad_latent_w.astype(F32),
        my_rows(gain_grads[2 * width_two : 2 * width_two + width_lat]),
        grad_expand_w.astype(F32),
        grad_output_w.astype(F32),
        my_rows(gain_grads[width_two : 2 * width_two]),
        grad_sgu[:, : shared_gate.shape[1]].astype(F32),
        grad_sgu[:, shared_gate.shape[1] :].astype(F32),
        grad_sd.astype(F32),
        in_order(own_gu[:, :width_ff], other_gu[:, :width_ff]).astype(F32),
        in_order(own_gu[:, width_ff:], other_gu[:, width_ff:]).astype(F32),
        in_order(own_down, other_down).astype(F32),
    )


def solution(mesh):
    return jax.shard_map(
        body,
        mesh=mesh,
        in_specs=(
            P("row", "col"),
            P("row", "col"),
            P(),
            P("row", None),
            P("row", None),
            P("row", None),
            P("row"),
            P("row", "col"),
            P("row", None),
            P("row"),
            P("row", "col"),
            P("col", "row"),
            P("row"),
            P("row", "col"),
            P("row", "col"),
            P("col", "row"),
            P("col", "row", None),
            P("col", "row", None),
            P("col", None, "row"),
        ),
        out_specs=(
            P("row", "col"),
            P("row", "col"),
            P("row"),
            P("row", "col"),
            P("row", None),
            P("row"),
            P("row", "col"),
            P("col", "row"),
            P("row"),
            P("row", "col"),
            P("row", "col"),
            P("col", "row"),
            P("col", "row", None),
            P("col", "row", None),
            P("col", None, "row"),
        ),
        check_vma=False,
    )
```

```python
import jax
import jax.numpy as jnp
from jax import lax
from jax.experimental.layout import Layout, with_layout_constraint
from jax.sharding import PartitionSpec as P

NOPE = 128
ROPE = 64
VDIM = 128
LAT = 512
TOPK = 6

EPSILON = 1e-06
F32 = jnp.float32
BF16 = jnp.bfloat16


def rotate(value, position, orient):
    half_width = value.shape[-1] // 2
    frequency = 10000.0 ** (-jnp.arange(half_width, dtype=F32) / half_width)
    angles = position.astype(F32)[:, None] * frequency[None, :]
    shape_out = (value.shape[0],) + (1,) * (value.ndim - 2) + (half_width,)
    cosine = jnp.cos(angles).reshape(shape_out)
    sine_part = jnp.sin(angles).reshape(shape_out)
    first_half = value[..., :half_width]
    second = value[..., half_width:]
    return jnp.concatenate(
        [
            first_half * cosine - orient * second * sine_part,
            second * cosine + orient * first_half * sine_part,
        ],
        axis=-1,
    )


def documents(lengths_row, row_count):
    doc_ends = jnp.cumsum(lengths_row)
    starts = doc_ends - lengths_row
    row_number = jnp.arange(row_count, dtype=jnp.int32)
    document = jnp.sum((row_number[:, None] >= doc_ends[None, :]).astype(jnp.int32), axis=1)
    onehot = document[:, None] == jnp.arange(lengths_row.shape[0], dtype=jnp.int32)[None, :]
    position = row_number - jnp.sum(jnp.where(onehot, starts[None, :], 0), axis=1)
    return (document, position)


def silu_parts(value):
    sigmoid_value = jax.nn.sigmoid(value)
    activation = value * sigmoid_value
    activ_slope = sigmoid_value * (1.0 + value * (1.0 - sigmoid_value))
    return (activation, activ_slope)


def norm_back(grad_normed, unit_rows, row_scale, gain_vector):
    scaled = grad_normed * gain_vector
    row_inner = jnp.mean(scaled * unit_rows, axis=-1, keepdims=True)
    return (row_scale * (scaled - unit_rows * row_inner), jnp.sum(grad_normed * unit_rows, axis=0))


def dot(left, right):
    return jnp.dot(left, right, preferred_element_type=F32)


def dot_nt(left, right):
    return lax.dot_general(left, right, (((1,), (1,)), ((), ())), preferred_element_type=F32)


def dot_tn(left, right):
    return lax.dot_general(left, right, (((0,), (0,)), ((), ())), preferred_element_type=F32)


def row_major(value):
    return with_layout_constraint(value, Layout(tuple(range(value.ndim))))


def row_swap(value, bit):
    return lax.ppermute(value, "row", [(j, j ^ bit) for j in range(lax.axis_size("row"))])


def mate(value):
    return row_swap(value, lax.axis_size("row") // 2)


def half_bits():
    return [1 << b for b in range((lax.axis_size("row") // 2).bit_length() - 1)]


def expert_gather(kept, given, axis):
    count = lax.axis_size("row")
    index = lax.axis_index("row")
    width = kept.shape[axis]
    shape = list(kept.shape)
    shape[axis] = width * count
    out = jnp.zeros(shape, kept.dtype)
    for first, item in ((0, kept), (count // 2, mate(given))):
        items = {first: item}
        for bit in half_bits():
            items.update({key ^ bit: row_swap(items[key], bit) for key in list(items)})
        for key, piece in items.items():
            out = lax.dynamic_update_slice_in_dim(
                out, piece, jnp.bitwise_xor(index, key) * width, axis
            )
    return out


def expert_scatter(value, axis):
    count = lax.axis_size("row")
    index = lax.axis_index("row")
    width = value.shape[axis] // count
    sums = []
    for first in (count // 2, 0):
        items = {
            key: lax.dynamic_slice_in_dim(
                value, jnp.bitwise_xor(index, key ^ first) * width, width, axis
            )
            for key in range(count // 2)
        }
        for bit in half_bits()[::-1]:
            items = {
                key: (
                    items[key].astype(F32) + row_swap(items[key ^ bit], bit).astype(F32)
                ).astype(BF16)
                for key in items
                if key < bit
            }
        sums.append(items[0])
    return sums[1], sums[0]


def swap(value, bit):
    return lax.ppermute(value, "col", [(j, j ^ bit) for j in range(lax.axis_size("col"))])


def chip_bits():
    return [1 << b for b in range(1, (lax.axis_size("col") - 1).bit_length())]


def chip_swap(value, step):
    bits = chip_bits()
    other = bits[::-1]
    return lax.ppermute(
        value,
        "col",
        [(j, j ^ (other if j % 2 else bits)[step]) for j in range(lax.axis_size("col"))],
    )


def block_at(device, place):
    bits = chip_bits()
    even = sum(bit for n, bit in enumerate(bits) if place >> n & 1)
    odd = sum(bit for n, bit in enumerate(bits[::-1]) if place >> n & 1)
    return jnp.bitwise_xor(device, jnp.where(device % 2 == 0, even, odd))


def cube_gather(block, axis):
    count = lax.axis_size("col")
    index = lax.axis_index("col")
    width = block.shape[axis]
    shape = list(block.shape)
    shape[axis] = width * count
    out = jnp.zeros(shape, block.dtype)
    held = row_major(block)[None]
    sibling = jnp.bitwise_xor(index, 1)
    done = 0
    for step in range(len(chip_bits()) + 1):
        theirs = swap(held[done:], 1)
        for place in range(done, held.shape[0]):
            for item, owner in ((held[place], index), (theirs[place - done], sibling)):
                out = lax.dynamic_update_slice_in_dim(
                    out, item, block_at(owner, place) * width, axis
                )
        done = held.shape[0]
        if step < len(chip_bits()):
            held = jnp.concatenate([held, chip_swap(held, step)], axis=0)
    return out


def cube_scatter(value, axis=0):
    count = lax.axis_size("col")
    index = lax.axis_index("col")
    rows = value.shape[axis] // count
    value = row_major(value)

    def blocks(device):
        return jnp.stack(
            [
                lax.dynamic_slice_in_dim(value, block_at(device, place) * rows, rows, axis)
                for place in range(count // 2)
            ]
        )

    got = swap(blocks(jnp.bitwise_xor(index, 1)), 1)
    held = blocks(index).astype(F32) + got.astype(F32)
    for step in range(len(chip_bits()) - 1, -1, -1):
        held = held.astype(BF16)
        half = held.shape[0] // 2
        got = chip_swap(held[half:], step)
        held = held[:half].astype(F32) + got.astype(F32)
    return held[0]


def row_gather(shard, axis):
    return lax.all_gather(shard, "row", axis=axis, tiled=True)


def after(values, earlier):
    out = lax.optimization_barrier(tuple(values) + tuple(earlier))
    return out[: len(values)]


def row_scatter(value, axis):
    return lax.psum_scatter(value, "row", scatter_dimension=axis, tiled=True)


def small_sum(value):
    for bit in [1] + chip_bits():
        value = value + swap(value, bit)
    count = lax.axis_size("row")
    total = value
    for k in range(1, count):
        total = total + lax.ppermute(value, "row", [(j, (j + k) % count) for j in range(count)])
    return total


def onehot(index, width):
    return (index[:, None] == jnp.arange(width, dtype=jnp.int32)[None, :]).astype(BF16)


def exchange(value, sent_of, slot_of):
    count = lax.axis_size("row")
    sent = row_major(dot(onehot(sent_of, value.shape[0]), value).astype(BF16))
    sent = sent.reshape(count, -1, value.shape[1])
    got = lax.all_to_all(sent, "row", split_axis=0, concat_axis=0, tiled=True)
    got = got.reshape(-1, value.shape[1])
    return row_major(dot(onehot(slot_of, got.shape[0]), got).astype(BF16))


def body(
    tokens,
    cotangent,
    dealing,
    doc_lengths,
    routes,
    gate_weights,
    attn_gain,
    w_query,
    w_latent,
    latent_gain,
    w_expand,
    w_output,
    ffn_gain,
    shared_gate,
    shared_up,
    shared_down,
    expert_gate,
    expert_up,
    expert_down,
):
    group_rows = routes.shape[0]
    row_count = lax.axis_size("row")
    col_count = lax.axis_size("col")
    row_index = lax.axis_index("row")
    col_index = lax.axis_index("col")
    part_rows = group_rows // col_count
    local_count = expert_gate.shape[0]
    capacity = 4 * group_rows * TOPK // (3 * local_count * col_count)

    def my_part(value):
        return lax.dynamic_slice_in_dim(value, col_index * part_rows, part_rows, 0)

    token_ids = jnp.arange(group_rows, dtype=jnp.int32)
    room = max(16, 5 * group_rows // (16 * row_count) * 4)
    lists = dealing.reshape(row_count, group_rows)
    source = lists // group_rows
    place_in = lists - source * group_rows
    from_here = source == row_index
    rank_here = jnp.where(from_here, jnp.cumsum(from_here.astype(jnp.int32), axis=1) - 1, -1)
    my_source = lax.dynamic_index_in_dim(source, row_index, 0, False)
    by_source = my_source[None, :] == jnp.arange(row_count, dtype=jnp.int32)[:, None]
    count_in = jnp.cumsum(by_source.astype(jnp.int32), axis=1)
    my_rank = jnp.sum(jnp.where(by_source, count_in, 0), axis=0) - 1
    all_counts = jnp.sum(
        (source[:, None, :] == jnp.arange(row_count, dtype=jnp.int32)[None, :, None]).astype(
            jnp.int32
        ),
        axis=2,
    )
    rounds = (jnp.max(all_counts) + room - 1) // room

    def maps_out(step):
        places = step * room + jnp.arange(room, dtype=jnp.int32)
        hit = rank_here[:, None, :] == places[None, :, None]
        listed = jnp.sum(jnp.where(hit, place_in[:, None, :] + 1, 0), axis=2).reshape(-1) - 1
        slot = my_rank - step * room
        inside = (slot >= 0) & (slot < room)
        return listed, jnp.where(inside, my_source * room + slot, -1)

    out_list, in_slots = maps_out(0)

    def more_dealt(carry):
        step, total = carry
        out_more, in_more = maps_out(step)
        given = jnp.concatenate([tokens, cotangent], axis=1)
        return step + 1, total + exchange(given, out_more, in_more)

    host = row_index // (row_count // 2)
    expert = col_index * local_count + host

    def chosen(group_routes, group_gates):
        named = group_routes == expert
        named_any = jnp.any(named, axis=1)
        running = jnp.cumsum(named_any.astype(jnp.int32))
        place = jnp.where(named_any, running - 1, -1)
        pick = place[None, :] == jnp.arange(capacity, dtype=jnp.int32)[:, None]
        token_weight = jnp.sum(jnp.where(named, group_gates, 0.0), axis=1)
        return pick.astype(BF16), jnp.sum(jnp.where(pick, token_weight[None, :], 0.0), axis=1)

    document, position = documents(doc_lengths[0], group_rows)

    rows_in, dim = w_query.shape[0], w_query.shape[0] * row_count
    wide = attn_gain.shape[0]
    slice_width = tokens.shape[1]
    more = lax.while_loop(
        lambda carry: carry[0] < rounds,
        more_dealt,
        (jnp.int32(1), jnp.zeros((group_rows, 2 * slice_width), BF16)),
    )[1]
    dealt_x = exchange(tokens, out_list, in_slots) + more[:, :slice_width]
    dealt_x, mate_routes, mate_gates = after((dealt_x, mate(routes), mate(gate_weights)), ())
    routes_late, gates_late = after((routes, gate_weights), (dealt_x,))
    pick, weight = chosen(routes_late, gates_late)
    mate_pick, mate_weight = chosen(mate_routes, mate_gates)
    full_x = cube_gather(dealt_x, 1)

    query_width = w_query.shape[1]
    lat_rows = rows_in // col_count
    w_latent_s = lax.dynamic_slice_in_dim(w_latent, col_index * lat_rows, lat_rows, 0)
    lat_wide = w_latent.shape[1]
    first_s = jnp.concatenate(
        [
            w_query,
            w_latent_s.reshape(-1, query_width),
            jnp.concatenate([attn_gain, ffn_gain, latent_gain]).reshape(-1, query_width),
        ],
        axis=0,
    )
    first_s = jnp.pad(first_s, ((0, -first_s.shape[0] % 16), (0, 0)))
    (first_s,) = after((first_s,), (dealt_x,))
    first_w = row_gather(first_s[None], 0)
    query_w = first_w[:, :rows_in].reshape(dim, query_width)
    lat_end = rows_in + lat_rows * lat_wide // query_width
    latent_w = cube_gather(first_w[:, rows_in:lat_end].reshape(row_count * lat_rows, lat_wide), 0)
    latent_w = latent_w.reshape(col_count, row_count, lat_rows, lat_wide).transpose(1, 0, 2, 3)
    latent_w = latent_w.reshape(dim, lat_wide)
    gains = first_w[:, lat_end:].reshape(row_count, -1)
    gain_one = gains[:, :wide].reshape(-1).astype(F32)
    gain_two = gains[:, wide : 2 * wide].reshape(-1).astype(F32)
    latent_g = gains[:, 2 * wide : 2 * wide + latent_gain.shape[0]].reshape(-1).astype(F32)

    (cotangent_s,) = after((cotangent,), (dealt_x,))
    dealt_dy = exchange(cotangent_s, out_list, in_slots) + more[:, slice_width:]
    both_dy = cube_gather(jnp.concatenate([dealt_dy, mate(dealt_dy)], axis=0), 1)
    full_dy, mate_dy = both_dy[:group_rows], both_dy[group_rows:]

    out_rows = w_output.shape[0]
    rest_s = jnp.concatenate([w_output.reshape(-1, w_expand.shape[1]), w_expand])
    (rest_s,) = after((rest_s,), (dealt_x,))
    rest_w = row_gather(rest_s[None], 0)
    out_count = w_output.size // w_expand.shape[1]
    output_w = rest_w[:, :out_count].reshape(row_count, out_rows, -1)
    output_w = output_w.transpose(1, 0, 2).reshape(out_rows, dim)
    expand_w = rest_w[:, out_count:].reshape(-1, w_expand.shape[1])

    (shared_gu_s,) = after((jnp.concatenate([shared_gate, shared_up], axis=1),), (first_w,))
    shared_gu_w = row_gather(shared_gu_s, 0)
    (shared_d_s,) = after((shared_down,), (rest_w,))
    shared_d_w = row_gather(shared_d_s, 1)

    def of_expert(value, number):
        return lax.dynamic_index_in_dim(value, number, 0, False)

    def both_parts(number):
        return jnp.concatenate([of_expert(expert_gate, number), of_expert(expert_up, number)], 1)

    kept, given = after((both_parts(host), both_parts(1 - host)), (dealt_dy,))
    gate_up_w = expert_gather(kept, given, 0)
    kept, given = after((of_expert(expert_down, host), of_expert(expert_down, 1 - host)), (dealt_dy,))
    down_w = expert_gather(kept, given, 1)

    head_count = query_w.shape[1] // (NOPE + ROPE)
    softmax_scale = (NOPE + ROPE) ** (-0.5)
    block_rows = min(512, group_rows)
    row_number = token_ids
    residual = full_x.astype(F32)
    scale_one = lax.rsqrt(jnp.mean(residual * residual, axis=-1, keepdims=True) + EPSILON)
    normed_one = (residual * scale_one * gain_one).astype(BF16)
    query_raw = dot(normed_one, query_w)
    query_raw = query_raw.reshape(group_rows, head_count, NOPE + ROPE)
    query_heads = jnp.concatenate(
        [query_raw[..., :NOPE], rotate(query_raw[..., NOPE:], position, 1.0)], axis=-1
    ).astype(BF16)
    latent = dot(normed_one, latent_w)
    latent_front = latent[:, :LAT]
    scale_lat = lax.rsqrt(jnp.mean(latent_front * latent_front, axis=-1, keepdims=True) + EPSILON)
    unit_lat = latent_front * scale_lat
    compressed = (unit_lat * latent_g).astype(BF16)
    rope_key = rotate(latent[:, LAT:], position, 1.0).astype(BF16)
    expanded = dot(compressed, expand_w).astype(BF16)
    expanded = expanded.reshape(group_rows, head_count, NOPE + VDIM)
    key_heads = jnp.concatenate(
        [
            expanded[..., :NOPE],
            jnp.broadcast_to(rope_key[:, None, :], (group_rows, head_count, ROPE)),
        ],
        axis=-1,
    )
    value_heads = expanded[..., NOPE:]

    def block_scores(first_row, last_row):
        raw_scores = (
            jnp.einsum(
                "qhd,khd->hqk",
                query_heads[first_row:last_row],
                key_heads[:last_row],
                preferred_element_type=F32,
            )
            * softmax_scale
        )
        allowed = (document[first_row:last_row, None] == document[None, :last_row]) & (
            row_number[first_row:last_row, None] >= row_number[None, :last_row]
        )
        return jnp.where(allowed[None], raw_scores, -1e30)

    mixed_blocks = []
    lse_blocks = []
    for first_row in range(0, group_rows, block_rows):
        last_row = first_row + block_rows
        scores = block_scores(first_row, last_row)
        row_top = jnp.max(scores, axis=-1, keepdims=True)
        exp_scores = jnp.exp(scores - row_top)
        row_total = jnp.sum(exp_scores, axis=-1, keepdims=True)
        probs_low = (exp_scores / row_total).astype(BF16)
        lse_blocks.append(row_top[..., 0] + jnp.log(row_total[..., 0]))
        mixed_blocks.append(
            jnp.einsum(
                "hqk,khd->qhd",
                probs_low,
                value_heads[:last_row],
                preferred_element_type=F32,
            )
        )
    mixed = (
        jnp.concatenate(mixed_blocks, axis=0).reshape(group_rows, head_count * VDIM).astype(BF16)
    )
    attn_part = cube_scatter(dot(mixed, output_w).astype(BF16))
    x_part = my_part(full_x).astype(F32)
    hidden_part = x_part + attn_part
    scale_two = lax.rsqrt(jnp.mean(hidden_part * hidden_part, axis=-1, keepdims=True) + EPSILON)
    unit_two = hidden_part * scale_two
    normed_part = (unit_two * gain_two).astype(BF16)
    mate_part = mate(normed_part)
    normed_two = cube_gather(normed_part, 0)
    (mate_part,) = after((mate_part,), (normed_two,))
    mate_two = cube_gather(mate_part, 0)

    place_late, rank_late, here_late, source_late, my_rank_late = after(
        (place_in, rank_here, from_here, my_source, my_rank), (normed_part,)
    )
    hit = (place_late[:, :, None] == token_ids[None, None, :]) & here_late[:, :, None]
    rank_of = jnp.sum(jnp.where(hit, rank_late[:, :, None], 0), axis=(0, 1))
    groups = jnp.arange(row_count, dtype=jnp.int32)
    group_of = jnp.sum(jnp.where(hit, groups[:, None, None], 0), axis=(0, 1))

    def maps_back(step):
        places = step * room + jnp.arange(room, dtype=jnp.int32)
        hit = (my_rank_late[None, None, :] == places[None, :, None]) & (
            source_late[None, None, :] == groups[:, None, None]
        )
        listed = jnp.sum(jnp.where(hit, token_ids[None, None, :] + 1, 0), axis=2).reshape(-1) - 1
        slot = rank_of - step * room
        inside = (slot >= 0) & (slot < room)
        return listed, jnp.where(inside, group_of * room + slot, -1)

    back_list, back_slots = maps_back(0)
    gate_up_w, back_list, back_slots = after((gate_up_w, back_list, back_slots), ())

    def forward(rows, gate_up_w):
        width = gate_up_w.shape[1] // 2
        gate_up = dot(rows, gate_up_w)
        gate_out, up_out = gate_up[:, :width], gate_up[:, width:]
        act, slope = silu_parts(gate_out)
        hidden = (act * up_out).astype(BF16)
        return hidden, act, up_out * slope

    def backward(grad_hidden, act, up_slope):
        return jnp.concatenate(
            [(grad_hidden * up_slope).astype(BF16), (grad_hidden * act).astype(BF16)], axis=1
        )

    ordered = []

    def queued_sum(value, axis):
        ordered.append(row_scatter(value.astype(BF16), axis))
        return ordered[-1]

    shared_hidden, shared_act, shared_us = forward(normed_two, shared_gu_w)
    grad_shared_gu = backward(dot_nt(full_dy, shared_d_w), shared_act, shared_us)
    grad_two = dot_nt(grad_shared_gu, shared_gu_w)
    moe_terms = dot(shared_hidden, shared_d_w)
    grad_sgu = queued_sum(dot_tn(normed_two, grad_shared_gu), 0)
    grad_sd = queued_sum(dot_tn(shared_hidden, full_dy), 1)

    rows = jnp.concatenate(
        [dot(pick, normed_two).astype(BF16), dot(mate_pick, mate_two).astype(BF16)], axis=0
    )
    grad_result = jnp.concatenate(
        [
            (weight[:, None] * dot(pick, full_dy)).astype(BF16),
            (mate_weight[:, None] * dot(mate_pick, mate_dy)).astype(BF16),
        ],
        axis=0,
    )
    hidden, act, up_slope = forward(rows, gate_up_w)
    grad_gate_up = backward(dot_nt(grad_result, down_w), act, up_slope)
    mate_rows = dot_nt(grad_gate_up[capacity:], gate_up_w).astype(BF16)
    mate_grad = dot_tn(mate_pick, mate_rows).astype(BF16)
    (own_gate_up,) = after((grad_gate_up[:capacity],), (mate_grad,))
    own_rows = dot_nt(own_gate_up, gate_up_w).astype(BF16)
    grad_two = (grad_two + dot_tn(pick, own_rows)).astype(BF16)
    mate_grad = mate(cube_scatter(mate_grad).astype(BF16))
    grad_gu = dot_tn(rows, grad_gate_up).astype(BF16)
    grad_down = dot_tn(hidden, grad_result).astype(BF16)

    grad_two_part = cube_scatter(grad_two) + mate_grad.astype(F32)
    dy_part = my_part(full_dy).astype(F32)
    hidden_back, gain_two_grad = norm_back(grad_two_part, unit_two, scale_two, gain_two)
    grad_hidden_part = dy_part + hidden_back
    grad_attn = cube_gather(grad_hidden_part.astype(BF16), 0)

    (hidden_late,) = after((hidden,), (grad_two,))
    weights = jnp.concatenate([weight, mate_weight])
    result_rows = (weights[:, None] * dot(hidden_late, down_w)).astype(BF16)
    mate_terms = dot_tn(mate_pick, result_rows[capacity:]).astype(BF16)
    moe_terms = (moe_terms + dot_tn(pick, result_rows[:capacity])).astype(BF16)
    mate_terms, moe_terms = after((mate_terms, moe_terms), (grad_attn,))
    both_terms = cube_scatter(jnp.stack([moe_terms, mate_terms]), 1)
    moe_part = both_terms[0] + mate(both_terms[1].astype(BF16)).astype(F32)
    result_part = (hidden_part + moe_part).astype(BF16)
    result_slice = lax.all_to_all(result_part, "col", split_axis=1, concat_axis=0, tiled=True)

    grad_output_w = queued_sum(dot_tn(mixed, grad_attn), 1)
    grad_mixed = dot_nt(grad_attn, output_w).astype(BF16)
    grad_mixed = grad_mixed.reshape(group_rows, head_count, VDIM)
    grad_query_blocks = []
    grad_keys = jnp.zeros((group_rows, head_count, NOPE + ROPE), F32)
    grad_values = jnp.zeros((group_rows, head_count, VDIM), F32)
    for block_number, first_row in enumerate(range(0, group_rows, block_rows)):
        last_row = first_row + block_rows
        scores = block_scores(first_row, last_row)
        probs_f = jnp.exp(scores - lse_blocks[block_number][..., None])
        probs_low = probs_f.astype(BF16)
        grad_block = grad_mixed[first_row:last_row]
        grad_probs = jnp.einsum(
            "qhd,khd->hqk", grad_block, value_heads[:last_row], preferred_element_type=F32
        )
        row_inner = jnp.sum(probs_f * grad_probs, axis=-1, keepdims=True)
        grad_scores = (probs_f * (grad_probs - row_inner)).astype(BF16)
        grad_values = grad_values.at[:last_row].add(
            jnp.einsum("hqk,qhd->khd", probs_low, grad_block, preferred_element_type=F32)
        )
        grad_query_blocks.append(
            softmax_scale
            * jnp.einsum(
                "hqk,khd->qhd", grad_scores, key_heads[:last_row], preferred_element_type=F32
            )
        )
        grad_keys = grad_keys.at[:last_row].add(
            softmax_scale
            * jnp.einsum(
                "hqk,qhd->khd",
                grad_scores,
                query_heads[first_row:last_row],
                preferred_element_type=F32,
            )
        )
    grad_query = jnp.concatenate(grad_query_blocks, axis=0)
    grad_query_raw = (
        jnp.concatenate(
            [grad_query[..., :NOPE], rotate(grad_query[..., NOPE:], position, -1.0)], axis=-1
        )
        .astype(BF16)
        .reshape(group_rows, head_count * (NOPE + ROPE))
    )
    own_gu, mate_gu = expert_scatter(grad_gu, 0)
    own_down, mate_down = expert_scatter(grad_down, 1)
    grad_one = cube_scatter(dot_nt(grad_query_raw, query_w).astype(BF16))
    grad_expanded = jnp.concatenate([grad_keys[..., :NOPE], grad_values], axis=-1).astype(BF16)
    grad_expanded = grad_expanded.reshape(group_rows, head_count * (NOPE + VDIM))
    grad_compressed = dot_nt(grad_expanded, expand_w)
    grad_rope_key = rotate(jnp.sum(grad_keys[..., NOPE:], axis=1), position, -1.0)
    grad_latent_part = cube_scatter(
        jnp.concatenate([grad_compressed, grad_rope_key], axis=1).astype(BF16)
    )
    grad_front, latent_gain_grad = norm_back(
        grad_latent_part[:, :LAT], my_part(unit_lat), my_part(scale_lat), latent_g
    )
    grad_latent_part = jnp.concatenate([grad_front, grad_latent_part[:, LAT:]], axis=1).astype(BF16)
    latent_term = dot_nt(grad_latent_part, latent_w)
    grad_one = grad_one + latent_term
    scale_one_part = my_part(scale_one)
    input_back, gain_one_grad = norm_back(
        grad_one, x_part * scale_one_part, scale_one_part, gain_one
    )
    grad_input = (grad_hidden_part + input_back).astype(BF16)
    grad_slice = lax.all_to_all(grad_input, "col", split_axis=1, concat_axis=0, tiled=True)
    dealt_back = jnp.concatenate([result_slice, grad_slice], axis=1)
    given_back = exchange(dealt_back, back_list, back_slots)

    def more_back(carry):
        step, total = carry
        back_more, slots_more = maps_back(step)
        return step + 1, total + exchange(dealt_back, back_more, slots_more)

    more = lax.while_loop(
        lambda carry: carry[0] < rounds,
        more_back,
        (jnp.int32(1), given_back),
    )[1]
    result, tokens_grad = more[:, :slice_width], more[:, slice_width:]

    grad_expand_w = queued_sum(dot_tn(compressed, grad_expanded), 0)
    grad_query_w = queued_sum(dot_tn(normed_one, grad_query_raw), 0)
    grad_latent = cube_gather(grad_latent_part, 0)
    my_columns = lax.dynamic_index_in_dim(
        normed_one.reshape(group_rows, row_count, col_count, lat_rows), col_index, 2, False
    ).reshape(group_rows, row_count * lat_rows)
    grad_latent_w = cube_gather(queued_sum(dot_tn(my_columns, grad_latent), 0), 0)
    gain_grads = small_sum(jnp.concatenate([gain_one_grad, gain_two_grad, latent_gain_grad]))
    width_ff = expert_gate.shape[2]
    other_gu, other_down = mate(mate_gu), mate(mate_down)

    def in_order(own, other):
        return jnp.stack([jnp.where(host == 0, own, other), jnp.where(host == 0, other, own)])

    width_two = gain_one_grad.shape[0]
    width_lat = latent_gain_grad.shape[0]

    def my_rows(value):
        width = value.shape[0] // row_count
        return lax.dynamic_slice_in_dim(value, row_index * width, width, 0)

    return (
        result,
        tokens_grad,
        my_rows(gain_grads[:width_two]),
        grad_query_w.astype(F32),
        grad_latent_w.astype(F32),
        my_rows(gain_grads[2 * width_two : 2 * width_two + width_lat]),
        grad_expand_w.astype(F32),
        grad_output_w.astype(F32),
        my_rows(gain_grads[width_two : 2 * width_two]),
        grad_sgu[:, : shared_gate.shape[1]].astype(F32),
        grad_sgu[:, shared_gate.shape[1] :].astype(F32),
        grad_sd.astype(F32),
        in_order(own_gu[:, :width_ff], other_gu[:, :width_ff]).astype(F32),
        in_order(own_gu[:, width_ff:], other_gu[:, width_ff:]).astype(F32),
        in_order(own_down, other_down).astype(F32),
    )


def solution(mesh):
    return jax.shard_map(
        body,
        mesh=mesh,
        in_specs=(
            P("row", "col"),
            P("row", "col"),
            P(),
            P("row", None),
            P("row", None),
            P("row", None),
            P("row"),
            P("row", "col"),
            P("row", None),
            P("row"),
            P("row", "col"),
            P("col", "row"),
            P("row"),
            P("row", "col"),
            P("row", "col"),
            P("col", "row"),
            P("col", "row", None),
            P("col", "row", None),
            P("col", None, "row"),
        ),
        out_specs=(
            P("row", "col"),
            P("row", "col"),
            P("row"),
            P("row", "col"),
            P("row", None),
            P("row"),
            P("row", "col"),
            P("col", "row"),
            P("row"),
            P("row", "col"),
            P("row", "col"),
            P("col", "row"),
            P("col", "row", None),
            P("col", "row", None),
            P("col", None, "row"),
        ),
        check_vma=False,
    )
```
